32 devices in a mesh: dp: 8 (over z, y), tensor: 4 (over x, core).
Axes of the slice: x: 2, y: 2, z: 4, core: 2. Of those that a mesh axis runs over, the one named last changes fastest.
Arguments:
- block_input: bfloat16 [2, 8192, 1024], P(None, ('dp', 'tensor')), may hold values from -6 to 6
- cotangent: bfloat16 [2, 8192, 1024], P(None, ('dp', 'tensor')), may hold values from -6 to 6
- routes: int32 [2, 8192, 8], P(None, 'dp'), may hold values from 0 to 31, all different within a row; in each aligned block of 1024 rows (0 to 1023, 1024 to 2047, ..., all dimensions but the last counted through in order) at most 288 rows name the same one
- gate_weights: float32 [2, 8192, 8], P(None, 'dp'), may hold values from 0.2 to 0.6
- w_query: bfloat16 [1024, 1024], P('dp', 'tensor'), may hold values from -0.1875 to 0.1875
- w_key: bfloat16 [1024, 512], P('dp', 'tensor'), may hold values from -0.1875 to 0.1875
- w_value: bfloat16 [1024, 512], P('dp', 'tensor'), may hold values from -0.1875 to 0.1875
- w_out: bfloat16 [1024, 1024], P('tensor', 'dp'), may hold values from -1.5 to 1.5
- w_gate_up: bfloat16 [32, 1024, 2, 512], P(None, 'dp', None, 'tensor'), may hold values from -0.1875 to 0.1875
- w_down: bfloat16 [32, 512, 1024], P(None, 'tensor', 'dp'), may hold values from -0.25 to 0.25
- norm_attn: float32 [1024], replicated, may hold values from 0.1 to 1.9
- norm_moe: float32 [1024], replicated, may hold values from 0.1 to 1.9
Outputs:
- block_output: bfloat16 [2, 8192, 1024], P(None, ('dp', 'tensor'))
- input_grad: float32 [2, 8192, 1024], P(None, ('dp', 'tensor'))
- grad_query: float32 [1024, 1024], P('dp', 'tensor')
- grad_key: float32 [1024, 512], P('dp', 'tensor')
- grad_value: float32 [1024, 512], P('dp', 'tensor')
- grad_out: float32 [1024, 1024], P('tensor', 'dp')
- grad_gate_up: float32 [32, 1024, 2, 512], P(None, 'dp', None, 'tensor')
- grad_down: float32 [32, 512, 1024], P(None, 'tensor', 'dp')
- grad_norm_attn: float32 [1024], replicated
- grad_norm_moe: float32 [1024], replicated
The draws below stay inside these ranges and needn't reach their ends.
Inputs may be any that keep to these rules, and one draw needn't show every extreme that they name: Each token names 8 different experts. In each group of 1024 rows of one micro-batch, no expert is named by more than 288 routes, a bound that some block reaches.
All inputs are finite; a program needn't handle non-finite values.
Results may differ from the reference program's by a relative error of at most 0.013.
Values may be sent and summed in bfloat16 or wider, within the bound.
No kernel may reach another device: no remote copies, remote signals or barrier semaphores. Data moves between devices by JAX's collectives and lax.ppermute only.
A program may use at most 448 MiB of HBM per device.

```python
import math
import jax
import jax.numpy as jnp
import numpy as np
from jax import lax

D = 1024
H = 16
KV = 8
HD = 64
E = 32
F = 512
TOPK = 8
PROMPT = 512
CONT = 512
NCONT = 1
MB = 2
G = 1024
CAP = 288
ROWS = 8192
N_DP = 8


def spiked(drawn, rng, source, target, blocks, factor):
    owner, partner = [(jnp.arange(drawn.shape[axis_at]) // (drawn.shape[axis_at] // blocks)).reshape([-1 if axis == axis_at else 1 for axis in range(drawn.ndim)]) for axis_at in (source, target)]
    chosen = jax.random.permutation(rng, blocks)[partner]
    strong = (owner == chosen) | (owner == (partner + blocks // 2) % blocks)
    return jnp.where(strong, factor * drawn, drawn)


def level_of(rng, shape, split, smallest, high):
    gain, own = 1.0, jax.random.fold_in(rng, 6)
    for position, parts in split:
        draws = jnp.exp(jax.random.uniform(jax.random.fold_in(own, position), (parts,), jnp.float32, smallest / len(split), high / len(split)))
        gain = gain * jnp.repeat(draws, shape[position] // parts).reshape([-1 if axis == position else 1 for axis in range(len(shape))])
    return gain


def shared_out(own_key, own, number, rows, amount, top, reach, slope):
    sequence = jax.random.permutation(own_key, amount)
    crowded, common = load_shares(amount, rows * top, reach, slope, True), load_shares(amount, rows * top, reach, slope, False)
    places = jnp.arange(amount)

    def named(lengths, turn):
        used = int((lengths > 0).sum())
        fixed = max(1, used // 4)
        shifted = fixed + (places - fixed + turn * (used - fixed)) % max(1, amount - fixed)
        return jnp.zeros((amount,), jnp.int32).at[sequence[jnp.where(places < fixed, places, shifted)]].set(jnp.asarray(lengths, jnp.int32))

    lengths = jnp.where(number % 4 == 0, named(crowded, number // 4), named(common, number - number // 4 - 1))
    mixed = jax.random.permutation(jax.random.fold_in(own, 3), amount)
    donor, taker = mixed[0:amount // 2 * 2:2], mixed[1:amount // 2 * 2:2]
    room = jnp.minimum(lengths[donor] - 1, reach - lengths[taker]) // 2
    room = jnp.where((donor == sequence[0]) | (taker == sequence[0]) | (lengths[taker] == 0), 0, jnp.maximum(room, 0))
    shifted = jax.random.randint(jax.random.fold_in(own, 4), (amount // 2,), 0, 1 << 20) % (room + 1)
    lengths = lengths.at[donor].add(-shifted).at[taker].add(shifted)
    items = jnp.searchsorted(jnp.cumsum(lengths), jnp.arange(rows * top), side="right").astype(jnp.int32)
    listing = items.reshape(top, rows).T
    listing = listing[jax.random.permutation(jax.random.fold_in(own, 1), rows)]
    turn = jax.random.randint(jax.random.fold_in(own, 2), (rows, 1), 0, top)
    return jnp.take_along_axis(listing, (jnp.arange(top)[None, :] + turn) % top, axis=1)


def load_shares(number_of, total, limit, skew, full):
    loads = [(1 << 20) // math.isqrt(standing ** skew) + 1 for standing in range(1, number_of + 1)]
    largest = limit if full else min(limit, max(-(-total // number_of), total * loads[0] // sum(loads)))
    least = 1 if total - largest >= number_of - 1 else 0
    given, surplus = [largest] + [least] * (number_of - 1), total - largest - least * (number_of - 1)
    while surplus > 0:
        movable = [i for i in range(1, number_of) if given[i] < largest] or [i for i in range(1, number_of) if given[i] < limit]
        pool, remaining = sum([loads[i] for i in movable]), surplus
        for i in movable:
            more = min(limit - given[i], max(1, remaining * loads[i] // pool), surplus)
            given[i] = given[i] + more
            surplus = surplus - more
    return np.array(given)


def gaussian(key, extent, spread, limit, cuts=(), kind=jnp.bfloat16):
    level = level_of(key, extent, cuts, -0.22, 0.18) if cuts else 1.0
    array = jax.random.normal(key, extent, jnp.float32) * spread * level
    return jnp.minimum(jnp.maximum(array, -limit), limit).astype(kind)


def noise_with(stream_key, dims, width, limit, split, heavy, kind=jnp.bfloat16):
    result = width * jax.random.normal(stream_key, dims, jnp.float32)
    if split:
        result = result * level_of(stream_key, dims, split, -0.22, 0.18)
    return jnp.clip(spiked(result, jax.random.fold_in(stream_key, 3), *heavy), -limit, limit).astype(kind)


def setup_inputs(seed: int = 0) -> dict:
    streams_of = jax.random.split(jax.random.key(seed), 13)
    block_input = noise_with(streams_of[0], (MB, ROWS, D), 1.0, 6.0, ((1, 32),), (1, 2, 32, 2.75))
    cotangent = noise_with(streams_of[1], (MB, ROWS, D), 1.0, 6.0, ((1, 32),), (1, 2, 32, 2.75))
    routes_keys = jax.random.split(jax.random.fold_in(streams_of[2], 1), MB * ROWS // G)
    routes_turns = jax.random.permutation(jax.random.fold_in(streams_of[2], 3), MB * ROWS // G)
    routes = jax.vmap(lambda own, number: shared_out(jax.random.fold_in(streams_of[2], 2), own, number, G, E, TOPK, CAP, 1))(routes_keys, routes_turns).reshape((MB, ROWS, TOPK))
    gate_weights = jnp.clip(0.2 + 0.400000021 * jax.random.uniform(streams_of[3], (MB, ROWS, TOPK), jnp.float32) ** level_of(streams_of[3], (MB, ROWS, TOPK), ((1, 8),), -0.2, 0.2), 0.2, 0.6)
    w_query = gaussian(streams_of[4], (D, H * HD), D ** -0.5, 0.1875, ((0, 8), (1, 4)))
    w_key = gaussian(streams_of[5], (D, KV * HD), D ** -0.5, 0.1875, ((0, 8), (1, 4)))
    w_value = gaussian(streams_of[6], (D, KV * HD), D ** -0.5, 0.1875, ((0, 8), (1, 4)))
    w_out = gaussian(streams_of[7], (H * HD, D), (H * HD // 64) ** -0.5, 1.5, ((0, 4), (1, 8)))
    w_gate_up = gaussian(streams_of[8], (E, D, 2, F), D ** -0.5, 0.1875, ((1, 8), (3, 4)))
    w_down = gaussian(streams_of[9], (E, F, D), F ** -0.5, 0.25, ((1, 4), (2, 8)))
    norm_attn = jnp.clip(1.0 + 0.18 * jax.random.normal(streams_of[10], (D,), jnp.float32), 0.1, 1.9)
    norm_moe = jnp.clip(1.0 + 0.18 * jax.random.normal(streams_of[11], (D,), jnp.float32), 0.1, 1.9)
    return {"block_input": block_input, "cotangent": cotangent, "routes": routes, "gate_weights": gate_weights, "w_query": w_query, "w_key": w_key, "w_value": w_value, "w_out": w_out, "w_gate_up": w_gate_up, "w_down": w_down, "norm_attn": norm_attn, "norm_moe": norm_moe}


@jax.custom_vjp
def low(v):
    return lax.optimization_barrier(v.astype(jnp.bfloat16)).astype(jnp.float32)

@jax.custom_vjp
def low_back(v):
    return v

def low_keep(v):
    return (low(v), None)

def low_pass(kept, grad):
    return (grad,)

def back_keep(v):
    return (v, None)

def back_low(kept, grad):
    return (low(grad),)
low.defvjp(low_keep, low_pass)
low_back.defvjp(back_keep, back_low)
EPSILON = 1e-06
HIGHEST = lax.Precision.HIGHEST

def matmul_high(left, right):
    return jnp.dot(left, right, precision=HIGHEST)

def slot_tables(route_rows, gate_rows):
    flat_routes = route_rows.reshape(-1).astype(jnp.int32)
    expert_ids = jnp.arange(E, dtype=jnp.int32)
    onehot = (flat_routes[:, None] == expert_ids[None, :]).astype(jnp.int32)
    before = (jnp.cumsum(onehot, axis=0) - onehot).astype(jnp.int32)
    slot_place = lax.optimization_barrier(jnp.sum(before * onehot, axis=1)).astype(jnp.int32)
    slot_index = flat_routes * CAP + slot_place
    token_index = jnp.arange(flat_routes.shape[0], dtype=jnp.int32) // TOPK
    source = jnp.zeros((E * CAP,), jnp.int32).at[slot_index].set(token_index)
    filled = jnp.zeros((E * CAP,), gate_rows.dtype).at[slot_index].set(1.0)
    weight = jnp.zeros((E * CAP,), gate_rows.dtype).at[slot_index].set(gate_rows.reshape(-1))
    return (source, filled, weight)

def attend(query, keys_in, values_in, prefix):
    head_ratio = H // KV
    key_heads = jnp.repeat(keys_in, head_ratio, axis=1)
    value_heads = jnp.repeat(values_in, head_ratio, axis=1)
    scores = jnp.einsum('qhd,khd->hqk', query, key_heads, precision=HIGHEST) * (1.0 / math.sqrt(HD))
    scores = low_back(scores)
    row_pos = jnp.arange(query.shape[0], dtype=jnp.int32)[:, None]
    col_pos = jnp.arange(keys_in.shape[0], dtype=jnp.int32)[None, :]
    allowed = (col_pos < prefix) | (col_pos - prefix <= row_pos)
    scores = jnp.where(allowed[None], scores, -1e+30)
    row_max = lax.optimization_barrier(jnp.max(scores, axis=-1, keepdims=True))
    exponent = jnp.exp(scores - row_max)
    attn_probs = low(exponent / lax.optimization_barrier(jnp.sum(exponent, axis=-1, keepdims=True)))
    return jnp.einsum('hqk,khd->qhd', attn_probs, value_heads, precision=HIGHEST)

def layer_forward(param_set, x_group, source, filled, weight):
    w_query, w_key, w_value, w_out, w_gate_up, w_down, norm_attn, norm_moe = param_set
    scale_attn = lax.rsqrt(lax.optimization_barrier(jnp.mean(x_group * x_group, axis=-1, keepdims=True)) + EPSILON)
    normed_attn = low(x_group * scale_attn * norm_attn)
    query = low(low_back(matmul_high(normed_attn, w_query))).reshape(G, H, HD)
    keys_all = low(low_back(matmul_high(normed_attn, w_key))).reshape(G, KV, HD)
    values_all = low(low_back(matmul_high(normed_attn, w_value))).reshape(G, KV, HD)
    pieces = [attend(query[:PROMPT], keys_all[:PROMPT], values_all[:PROMPT], 0)]
    for cont_index in range(NCONT):
        start_row = PROMPT + cont_index * CONT
        key_set = jnp.concatenate([keys_all[:PROMPT], keys_all[start_row:start_row + CONT]], axis=0)
        value_set = jnp.concatenate([values_all[:PROMPT], values_all[start_row:start_row + CONT]], axis=0)
        pieces.append(attend(query[start_row:start_row + CONT], key_set, value_set, PROMPT))
    head_out = low(low_back(jnp.concatenate(pieces, axis=0))).reshape(G, H * HD)
    branch = low_back(matmul_high(head_out, w_out))
    middle = x_group + branch
    scale_moe = lax.rsqrt(lax.optimization_barrier(jnp.mean(middle * middle, axis=-1, keepdims=True)) + EPSILON)
    normed_moe = low(middle * scale_moe * norm_moe)
    expert_in = (normed_moe[source] * filled[:, None]).reshape(E, CAP, D)
    pair_out = jnp.einsum('ecd,edkf->eckf', expert_in, w_gate_up, precision=HIGHEST)
    gate_pre = low_back(pair_out[:, :, 0])
    up_pre = low_back(pair_out[:, :, 1])
    hidden = low(gate_pre * jax.nn.sigmoid(gate_pre) * up_pre)
    expert_out = low_back(jnp.einsum('ecf,efd->ecd', hidden, w_down, precision=HIGHEST))
    mixed_out = jax.ops.segment_sum(expert_out.reshape(E * CAP, D) * weight[:, None], source, num_segments=G)
    mixed_out = low_back(mixed_out)
    return middle + mixed_out

def reference(block_input, cotangent, routes, gate_weights, w_query, w_key, w_value, w_out, w_gate_up, w_down, norm_attn, norm_moe):
    param_set = tuple((weight_in.astype(jnp.float32) for weight_in in (w_query, w_key, w_value, w_out, w_gate_up, w_down, norm_attn, norm_moe)))
    group_count = MB * N_DP
    x_groups = block_input.astype(jnp.float32).reshape(group_count, G, D)
    cot_groups = cotangent.astype(jnp.float32).reshape(group_count, G, D)
    route_groups = routes.reshape(group_count, G, TOPK)
    gate_groups = gate_weights.astype(jnp.float32).reshape(group_count, G, TOPK)

    def group_step(totals, group_item):
        x_group, cot_group, route_rows, gate_rows = group_item
        source, filled, weight = slot_tables(route_rows, gate_rows)
        out_group, pull_back = jax.vjp(lambda params_in, x_in: layer_forward(params_in, x_in, source, filled, weight), param_set, x_group)
        grad_terms, x_grad = pull_back(cot_group)
        totals = jax.tree.map(lambda left_term, right_term: left_term + right_term, totals, grad_terms)
        return (totals, (out_group, x_grad))
    zero_init = jax.tree.map(jnp.zeros_like, param_set)
    totals, (out_groups, grad_groups) = lax.scan(group_step, zero_init, (x_groups, cot_groups, route_groups, gate_groups))
    block_output = out_groups.reshape(MB, N_DP * G, D).astype(jnp.bfloat16)
    input_grad = grad_groups.reshape(MB, N_DP * G, D)
    return (block_output, input_grad, totals[0], totals[1], totals[2], totals[3], totals[4], totals[5], totals[6], totals[7])
```

```python
import functools
import math

import jax
import jax.numpy as jnp
from jax import lax
from jax.experimental import pallas as pl
from jax.experimental.pallas import tpu as pltpu
from jax.sharding import Mesh
from jax.sharding import PartitionSpec as P

HD = 64
E = 32
PROMPT = 512
CONT = 512
CHUNKS = 4

EPSILON = 1e-06
BF = jnp.bfloat16
FP = jnp.float32


def dot_nn(left, right):
    return lax.dot_general(left, right, (((1,), (0,)), ((), ())), preferred_element_type=FP)


def dot_tn(left, right):
    return lax.dot_general(left, right, (((0,), (0,)), ((), ())), preferred_element_type=FP)


def dot_nt(left, right):
    return lax.dot_general(left, right, (((1,), (1,)), ((), ())), preferred_element_type=FP)


def row_norm(in_rows, gain_vec):
    row_scale = lax.rsqrt(jnp.mean(in_rows * in_rows, axis=-1, keepdims=True) + EPSILON)
    return (in_rows * row_scale * gain_vec, row_scale)


def norm_back(in_rows, row_scale, gain_vec, grad_in):
    weighted = grad_in * gain_vec
    inner = jnp.mean(weighted * in_rows, axis=-1, keepdims=True)
    returned = row_scale * weighted - in_rows * row_scale * row_scale * row_scale * inner
    gain_part = jnp.sum(grad_in * in_rows * row_scale, axis=0)
    return (returned, gain_part)


def swap(value, axis):
    return lax.ppermute(value, axis, [(0, 1), (1, 0)])


def in_order(mine, other, axis, dim):
    first = lax.axis_index(axis) == 0
    return jnp.stack([jnp.where(first, mine, other), jnp.where(first, other, mine)], axis=dim)


def gather_rows(rows):
    pair = in_order(rows, swap(rows, "x"), "x", -3)
    whole = in_order(pair, swap(pair, "c"), "c", -3)
    return whole.reshape(*rows.shape[:-2], 4 * rows.shape[-2], rows.shape[-1])


def scatter_rows(partial):
    rows, width = partial.shape
    parts = partial.reshape(2, 2, rows // 4, width)
    core, chip = lax.axis_index("c"), lax.axis_index("x")
    sent = lax.dynamic_index_in_dim(parts, 1 - core, 1, False).astype(BF)
    kept = lax.dynamic_index_in_dim(parts, core, 1, False).astype(FP)
    half = kept + swap(sent, "c").astype(FP)
    sent = lax.dynamic_index_in_dim(half, 1 - chip, 0, False).astype(BF)
    kept = lax.dynamic_index_in_dim(half, chip, 0, False)
    return kept + swap(sent, "x").astype(FP)


def gather_dp(shard, depth):
    turn_up = [(i, (i + 1) % depth) for i in range(depth)]
    turn_down = [(i, (i - 1) % depth) for i in range(depth)]
    before, after = [], []
    piece = shard
    for _ in range(depth // 2):
        piece = lax.ppermute(piece, "z", turn_up)
        before.append(piece)
    piece = shard
    for _ in range((depth - 1) // 2):
        piece = lax.ppermute(piece, "z", turn_down)
        after.append(piece)
    line = before[::-1] + [shard] + after
    place = lax.axis_index("z")
    start = lax.rem(depth + len(before) - place, depth)
    column = lax.dynamic_slice_in_dim(jnp.stack(line + line), start, depth, 0)
    return in_order(column, swap(column, "y"), "y", 1).reshape(-1, shard.shape[-1])


def scatter_dp(partial, depth):
    blocks = partial.reshape(depth, 2, -1, partial.shape[-1])
    mine = lax.axis_index("y")
    sent = lax.dynamic_index_in_dim(blocks, 1 - mine, 1, False).astype(BF)
    kept = lax.dynamic_index_in_dim(blocks, mine, 1, False)
    column = (kept + swap(sent, "y").astype(FP)).astype(BF)
    return lax.psum_scatter(column, "z", scatter_dimension=0, tiled=False)


def moe_kernel(first, side_ref, x_ref, g_ref, gate_ref, mine_ref, other_ref, *rest):
    if first:
        mixed_ref, back_ref, gmine_ref, gother_ref, w_scr, acc = rest
    else:
        mixed_in, back_in, mixed_ref, back_ref, gmine_ref, gother_ref, w_scr, acc = rest
    step = pl.program_id(0)
    depth, pairs, blk, width = mine_ref.shape
    half = width // 3
    side = side_ref[0]

    def spot(z, y):
        return pl.ds(pl.multiple_of((z * 2 + y) * blk, blk), blk)

    @pl.when(step == 0)
    def _():
        for p in range(pairs):
            for z in range(depth):
                w_scr[p, spot(z, side), :] = mine_ref[z, p]
                w_scr[p, spot(z, 1 - side), :] = other_ref[z, p]
        acc[...] = jnp.zeros_like(acc)

    x = x_ref[...]
    g = g_ref[...]
    hidden_local = half // 2
    mixed = None
    back = None
    for p in range(pairs):
        weights = w_scr.at[p]
        pre = dot_nn(x, weights[:, : 2 * half])
        out_back = dot_nn(g, weights[:, 2 * half :])
        gate = pre[:, :half]
        up = pre[:, half:]
        sig = 0.5 + 0.5 * jnp.tanh(0.5 * gate)
        share = jnp.concatenate(
            [
                jnp.broadcast_to(gate_ref[:, i : i + 1], (x.shape[0], hidden_local))
                for i in (2 * p, 2 * p + 1)
            ],
            axis=1,
        )
        silu = gate * sig
        hidden = (share * (silu * up)).astype(BF)
        hidden_grad = share * out_back
        gate_grad = (hidden_grad * up * sig * (1.0 + gate * (1.0 - sig))).astype(BF)
        up_grad = (hidden_grad * silu).astype(BF)
        pair_grad = jnp.concatenate([gate_grad, up_grad], axis=1)
        mixed_p = dot_nt(hidden, weights[:, 2 * half :])
        back_p = dot_nt(pair_grad, weights[:, : 2 * half])
        mixed = mixed_p if mixed is None else mixed + mixed_p
        back = back_p if back is None else back + back_p
        acc[p, :, : 2 * half] += dot_tn(x, pair_grad)
        acc[p, :, 2 * half :] += dot_tn(g, hidden)
    if first:
        mixed_ref[...] = mixed
        back_ref[...] = back
    else:
        mixed_ref[...] = mixed_in[...] + mixed
        back_ref[...] = back_in[...] + back

    @pl.when(step == pl.num_programs(0) - 1)
    def _():
        for p in range(pairs):
            for z in range(depth):
                gmine_ref[z, p] = acc[p, spot(z, side), :].astype(BF)
                gother_ref[z, p] = acc[p, spot(z, 1 - side), :].astype(BF)


def moe_chunk(side, x, g, gates, mine, other, sums):
    rows, model_width = x.shape
    tile = 256
    pairs, width = mine.shape[1], mine.shape[3]
    once = pl.Buffered(1)
    row = pl.BlockSpec((tile, model_width), lambda i, s: (i, 0))
    gate_spec = pl.BlockSpec((tile, gates.shape[1]), lambda i, s: (i, 0))
    whole = pl.BlockSpec(mine.shape, lambda i, s: (0, 0, 0, 0), pipeline_mode=once)
    first = sums is None
    operands = [side, x, g, gates, mine, other] + ([] if first else list(sums))
    return pl.pallas_call(
        functools.partial(moe_kernel, first),
        grid_spec=pltpu.PrefetchScalarGridSpec(
            num_scalar_prefetch=1,
            grid=(rows // tile,),
            in_specs=[row, row, gate_spec, whole, whole] + ([] if first else [row, row]),
            out_specs=[row, row, whole, whole],
            scratch_shapes=[
                pltpu.VMEM((pairs, model_width, width), BF),
                pltpu.VMEM((pairs, model_width, width), FP),
            ],
        ),
        out_shape=[jax.ShapeDtypeStruct((rows, model_width), FP)] * 2
        + [jax.ShapeDtypeStruct(mine.shape, BF)] * 2,
        input_output_aliases={} if first else {6: 0, 7: 1},
        compiler_params=pltpu.CompilerParams(vmem_limit_bytes=60 << 20),
        cost_estimate=pl.CostEstimate(
            flops=6 * rows * model_width * pairs * width,
            bytes_accessed=48 << 20,
            transcendentals=rows * pairs * width // 3,
        ),
    )(*operands)


def pack_experts(w_gate_up, w_down):
    blk, hidden_local = w_gate_up.shape[1], w_gate_up.shape[3]
    gate_up = w_gate_up.reshape(E // 2, 2, blk, 2, hidden_local).transpose(0, 2, 3, 1, 4)
    down = w_down.reshape(E // 2, 2, hidden_local, blk).transpose(0, 3, 1, 2)
    return jnp.concatenate(
        [gate_up.reshape(E // 2, blk, -1), down.reshape(E // 2, blk, -1)], axis=-1
    )


def unpack_experts(packed):
    pairs, blk, width = packed.shape
    hidden_local = width // 6
    packed = packed.astype(FP)
    gate_up = packed[:, :, : 4 * hidden_local].reshape(pairs, blk, 2, 2, hidden_local)
    down = packed[:, :, 4 * hidden_local :].reshape(pairs, blk, 2, hidden_local)
    return (
        gate_up.transpose(0, 3, 1, 2, 4).reshape(2 * pairs, blk, 2, hidden_local),
        down.transpose(0, 2, 3, 1).reshape(2 * pairs, hidden_local, blk),
    )


def mask_scores(query_blk, key_set, prefix, score_scale):
    scores = (
        jnp.einsum("bgrd,lgd->grbl", query_blk, key_set, preferred_element_type=FP) * score_scale
    )
    row_pos = lax.broadcasted_iota(jnp.int32, scores.shape, 2)
    col_pos = lax.broadcasted_iota(jnp.int32, scores.shape, 3)
    allowed = (col_pos < prefix) | (col_pos - prefix <= row_pos)
    return jnp.where(allowed, scores, -1e30)


def segments(rows):
    return ((0, PROMPT, 0), (PROMPT, rows - PROMPT, PROMPT))


def attention_forward(query, keys_all, values_all, score_scale):
    outputs = []
    saved = []
    for start_row, length, prefix in segments(query.shape[0]):
        key_set, value_set = keys_all[: start_row + length], values_all[: start_row + length]
        query_blk = query[start_row : start_row + length]
        scores = mask_scores(query_blk, key_set, prefix, score_scale)
        row_max = jnp.max(scores, axis=-1, keepdims=True)
        exponent = jnp.exp(scores - row_max)
        row_total = jnp.sum(exponent, axis=-1, keepdims=True)
        attn_probs = (exponent / row_total).astype(BF)
        outputs.append(
            jnp.einsum("grbl,lgd->bgrd", attn_probs, value_set, preferred_element_type=FP)
        )
        saved.append(row_max + jnp.log(row_total))
    return (jnp.concatenate(outputs, axis=0), saved)


def attention_backward(query, keys_all, values_all, head_grad, saved, score_scale):
    query_parts = []
    key_grad = jnp.zeros(keys_all.shape, FP)
    value_grad = jnp.zeros(values_all.shape, FP)
    for (start_row, length, prefix), saved_part in zip(segments(query.shape[0]), saved):
        stop = start_row + length
        key_set, value_set = keys_all[:stop], values_all[:stop]
        query_blk = query[start_row:stop]
        grad_blk = head_grad[start_row:stop]
        scores = mask_scores(query_blk, key_set, prefix, score_scale)
        attn_probs = jnp.exp(scores - saved_part)
        prob_grad = jnp.einsum("bgrd,lgd->grbl", grad_blk, value_set, preferred_element_type=FP)
        inner = jnp.sum(attn_probs * prob_grad, axis=-1, keepdims=True)
        score_grad = (attn_probs * (prob_grad - inner)).astype(BF)
        query_parts.append(
            jnp.einsum("grbl,lgd->bgrd", score_grad, key_set, preferred_element_type=FP)
            * score_scale
        )
        key_part = (
            jnp.einsum("grbl,bgrd->lgd", score_grad, query_blk, preferred_element_type=FP)
            * score_scale
        )
        value_part = jnp.einsum(
            "grbl,bgrd->lgd", attn_probs.astype(BF), grad_blk, preferred_element_type=FP
        )
        key_grad = key_grad.at[:stop].add(key_part)
        value_grad = value_grad.at[:stop].add(value_part)
    return (jnp.concatenate(query_parts, axis=0), key_grad, value_grad)


def on_device(
    block_input,
    cotangent,
    routes,
    gate_weights,
    w_query,
    w_key,
    w_value,
    w_out,
    w_gate_up,
    w_down,
    norm_attn,
    norm_moe,
):
    score_scale = 1.0 / math.sqrt(HD)
    depth = lax.axis_size("z")
    micro_count, rows_local, model_width = block_input.shape
    kv_local = w_key.shape[1] // HD
    q_width, kv_width = w_query.shape[1], w_key.shape[1]
    head_ratio = q_width // kv_width
    proj_width = q_width + 2 * kv_width
    side = lax.axis_index("y").astype(jnp.int32).reshape(1)

    packed_attn = jnp.concatenate([w_query, w_key, w_value, w_out.T], axis=1)
    attn_full = gather_dp(packed_attn, depth)
    w_project, out_t = attn_full[:, :proj_width], attn_full[:, proj_width:]
    packed = pack_experts(w_gate_up, w_down)
    per_chunk = packed.shape[0] // CHUNKS
    chunk_weights = []
    for chunk in range(CHUNKS):
        mine = lax.all_gather(packed[chunk * per_chunk : (chunk + 1) * per_chunk], "z", axis=0)
        chunk_weights.append((mine, swap(mine, "y")))

    in_rows = block_input.astype(FP)
    normed_attn, scale_attn = row_norm(in_rows, norm_attn)
    normed_attn = normed_attn.astype(BF)
    attn_in, projections, saved_all, heads_all = [], [], [], []
    middles = []
    for m in range(micro_count):
        attn_in.append(gather_rows(normed_attn[m]))
        projected = dot_nn(attn_in[m], w_project).astype(BF)
        query = projected[:, :q_width].reshape(-1, kv_local, head_ratio, HD)
        keys_all = projected[:, q_width : q_width + kv_width].reshape(-1, kv_local, HD)
        values_all = projected[:, q_width + kv_width :].reshape(-1, kv_local, HD)
        attn_raw, saved = attention_forward(query, keys_all, values_all, score_scale)
        head_out = attn_raw.astype(BF).reshape(-1, q_width)
        projections.append((query, keys_all, values_all))
        saved_all.append(saved)
        heads_all.append(head_out)
        middles.append(in_rows[m] + scatter_rows(dot_nt(head_out, out_t)))
    middle = jnp.stack(middles)
    normed_moe, scale_moe = row_norm(middle, norm_moe)
    moe_in = jnp.concatenate([gather_rows(normed_moe[m].astype(BF)) for m in range(micro_count)])
    moe_grad = gather_rows(cotangent).reshape(-1, model_width)

    expert_ids = jnp.arange(E, dtype=jnp.int32)
    gates = jnp.sum(
        jnp.where(routes[..., None] == expert_ids, gate_weights[..., None], 0.0), axis=2
    ).reshape(-1, CHUNKS, 2 * per_chunk)
    sums = None
    shards = []
    for chunk in range(CHUNKS):
        mine, other = chunk_weights[chunk]
        *sums, grad_mine, grad_other = moe_chunk(
            side, moe_in, moe_grad, gates[:, chunk], mine, other, sums
        )
        column = (grad_mine.astype(FP) + swap(grad_other, "y").astype(FP)).astype(BF)
        shards.append(lax.psum_scatter(column, "z", scatter_dimension=0, tiled=False))
    mixed, moe_back = (s.reshape(micro_count, -1, model_width) for s in sums)
    shard_pair, shard_down = unpack_experts(jnp.concatenate(shards))

    out_grad = cotangent.astype(FP)
    outputs, input_grads = [], []
    gain_attn_total = jnp.zeros(norm_attn.shape, FP)
    gain_moe_total = jnp.zeros(norm_moe.shape, FP)
    attn_grad_total = None
    for m in range(micro_count):
        moe_in_grad = scatter_rows(moe_back[m])
        middle_back, gain_moe_part = norm_back(middle[m], scale_moe[m], norm_moe, moe_in_grad)
        middle_grad = out_grad[m] + middle_back
        attn_grad = gather_rows(middle_grad.astype(BF))
        out_weight_grad = dot_tn(attn_grad, heads_all[m])
        head_grad = dot_nn(attn_grad, out_t).astype(BF).reshape(-1, kv_local, head_ratio, HD)
        query_grad, key_grad, value_grad = attention_backward(
            *projections[m], head_grad, saved_all[m], score_scale
        )
        project_grad = jnp.concatenate(
            [
                query_grad.reshape(-1, q_width),
                key_grad.reshape(-1, kv_width),
                value_grad.reshape(-1, kv_width),
            ],
            axis=1,
        ).astype(BF)
        weight_grad = jnp.concatenate([dot_tn(attn_in[m], project_grad), out_weight_grad], axis=1)
        attn_grad_total = weight_grad if m == 0 else attn_grad_total + weight_grad
        attn_in_grad = scatter_rows(dot_nt(project_grad, w_project))
        in_back, gain_attn_part = norm_back(in_rows[m], scale_attn[m], norm_attn, attn_in_grad)
        input_grads.append(middle_grad + in_back)
        outputs.append((middle[m] + scatter_rows(mixed[m])).astype(BF))
        gain_attn_total = gain_attn_total + gain_attn_part
        gain_moe_total = gain_moe_total + gain_moe_part
    attn_shard = scatter_dp(attn_grad_total, depth).astype(FP)
    gain_attn_grad, gain_moe_grad = lax.psum(
        (gain_attn_total, gain_moe_total), ("z", "y", "x", "c")
    )
    return (
        jnp.stack(outputs),
        jnp.stack(input_grads),
        attn_shard[:, :q_width],
        attn_shard[:, q_width : q_width + kv_width],
        attn_shard[:, q_width + kv_width : proj_width],
        attn_shard[:, proj_width:].T,
        shard_pair,
        shard_down,
        gain_attn_grad,
        gain_moe_grad,
    )


def solution(mesh):
    dp, tensor = mesh.shape["dp"], mesh.shape["tensor"]
    fine = Mesh(mesh.devices.reshape(dp // 2, 2, tensor // 2, 2), ("z", "y", "x", "c"))
    dp_axes, tensor_axes = ("z", "y"), ("x", "c")
    rows = P(None, dp_axes + tensor_axes, None)
    return jax.shard_map(
        on_device,
        mesh=fine,
        in_specs=(
            rows,
            rows,
            P(None, dp_axes, None),
            P(None, dp_axes, None),
            P(dp_axes, tensor_axes),
            P(dp_axes, tensor_axes),
            P(dp_axes, tensor_axes),
            P(tensor_axes, dp_axes),
            P(None, dp_axes, None, tensor_axes),
            P(None, tensor_axes, dp_axes),
            P(),
            P(),
        ),
        out_specs=(
            rows,
            rows,
            P(dp_axes, tensor_axes),
            P(dp_axes, tensor_axes),
            P(dp_axes, tensor_axes),
            P(tensor_axes, dp_axes),
            P(None, dp_axes, None, tensor_axes),
            P(None, tensor_axes, dp_axes),
            P(),
            P(),
        ),
        check_vma=False,
    )
```

```python
import functools

import jax
import jax.numpy as jnp
from jax import lax
from jax.experimental import pallas as pl
from jax.experimental.pallas import tpu as pltpu
from jax.sharding import Mesh
from jax.sharding import PartitionSpec as P

HD = 64
E = 32
CHUNKS = 4

EPSILON = 1e-06
BF = jnp.bfloat16
FP = jnp.float32


def dot_nn(left, right):
    return lax.dot_general(left, right, (((1,), (0,)), ((), ())), preferred_element_type=FP)


def dot_tn(left, right):
    return lax.dot_general(left, right, (((0,), (0,)), ((), ())), preferred_element_type=FP)


def dot_nt(left, right):
    return lax.dot_general(left, right, (((1,), (1,)), ((), ())), preferred_element_type=FP)


def row_norm(in_rows, gain_vec):
    row_scale = lax.rsqrt(jnp.mean(in_rows * in_rows, axis=-1, keepdims=True) + EPSILON)
    return (in_rows * row_scale * gain_vec, row_scale)


def norm_back(in_rows, row_scale, gain_vec, grad_in):
    weighted = grad_in * gain_vec
    inner = jnp.mean(weighted * in_rows, axis=-1, keepdims=True)
    returned = row_scale * weighted - in_rows * row_scale * row_scale * row_scale * inner
    gain_part = jnp.sum(grad_in * in_rows * row_scale, axis=0)
    return (returned, gain_part)


def swap(value, axis):
    return lax.ppermute(value, axis, [(0, 1), (1, 0)])


def in_order(mine, other, axis, dim):
    first = lax.axis_index(axis) == 0
    return jnp.stack([jnp.where(first, mine, other), jnp.where(first, other, mine)], axis=dim)


def gather_rows(rows):
    pair = in_order(rows, swap(rows, "x"), "x", 0)
    whole = in_order(pair, swap(pair, "c"), "c", 1)
    return whole.reshape(4 * rows.shape[0], rows.shape[1])


def gather_pair(rows):
    both = jnp.stack([rows, swap(rows, "y")])
    pair = in_order(both, swap(both, "x"), "x", 1)
    whole = in_order(pair, swap(pair, "c"), "c", 2)
    return whole.reshape(8 * rows.shape[0], rows.shape[1])


def scatter_rows(kept, sent):
    half = (kept + swap(sent, "c").astype(FP)).reshape(2, -1, kept.shape[-1])
    chip = lax.axis_index("x")
    sent = lax.dynamic_index_in_dim(half, 1 - chip, 0, False).astype(BF)
    kept = lax.dynamic_index_in_dim(half, chip, 0, False)
    return kept + swap(sent, "x").astype(FP)


def scatter_pair(kept, sent):
    half = (kept + swap(sent, "c").astype(FP)).reshape(2, 2, -1, kept.shape[-1])
    chip = lax.axis_index("x")
    sent = lax.dynamic_index_in_dim(half, 1 - chip, 1, False).astype(BF)
    kept = lax.dynamic_index_in_dim(half, chip, 1, False)
    both = kept + swap(sent, "x").astype(FP)
    return both[0] + swap(both[1].astype(BF), "y").astype(FP)


def turns(depth):
    up = [(i, (i + 1) % depth) for i in range(depth)]
    down = [(i, (i - 1) % depth) for i in range(depth)]
    return up, down


def gather_dp(shard, depth):
    turn_up, turn_down = turns(depth)
    before, after = [], []
    piece = shard
    for _ in range(depth // 2):
        piece = lax.ppermute(piece, "z", turn_up)
        before.append(piece)
    piece = shard
    for _ in range((depth - 1) // 2):
        piece = lax.ppermute(piece, "z", turn_down)
        after.append(piece)
    line = before[::-1] + [shard] + after
    place = lax.axis_index("z")
    start = lax.rem(depth + len(before) - place, depth)
    column = lax.dynamic_slice_in_dim(jnp.stack(line + line), start, depth, 0)
    return in_order(column, swap(column, "y"), "y", 1).reshape(-1, shard.shape[-1])


def scatter_dp(partial, depth):
    blocks = partial.reshape(depth, 2, -1, partial.shape[-1])
    mine = lax.axis_index("y")
    sent = lax.dynamic_index_in_dim(blocks, 1 - mine, 1, False).astype(BF)
    kept = lax.dynamic_index_in_dim(blocks, mine, 1, False)
    column = kept + swap(sent, "y").astype(FP)
    place = lax.axis_index("z")

    def owned(distance):
        return lax.dynamic_index_in_dim(column, lax.rem(place + distance, depth), 0, False)

    turn_up, turn_down = turns(depth)
    total = owned(0)
    for turn, sign, steps in ((turn_up, 1, depth // 2), (turn_down, -1, (depth - 1) // 2)):
        carried = None
        for distance in range(steps, 0, -1):
            block = owned(depth + sign * distance)
            carried = block if carried is None else block + carried
            carried = lax.ppermute(carried.astype(BF), "z", turn).astype(FP)
        if carried is not None:
            total = total + carried
    return total


def sum_all(value, depth):
    for axis in ("c", "x", "y"):
        value = value + swap(value, axis)
    reach = 1
    while reach < depth:
        pairs = [(i, i ^ reach) for i in range(depth)]
        value = value + lax.ppermute(value, "z", pairs)
        reach *= 2
    return value


def moe_kernel(first, last, column, core_ref, x_ref, g_ref, gate_ref, w_ref, *rest):
    rest = list(rest)
    sums_in = [] if first else [rest.pop(0), rest.pop(0)]
    acc = rest.pop()
    grads_ref = rest.pop()
    sums_out = rest
    step = pl.program_id(0)
    blocks, pairs, blk, width = w_ref.shape
    model_width = blocks * blk
    half = width // 3
    hidden_local = half // 2

    @pl.when(step == 0)
    def _():
        acc[...] = jnp.zeros_like(acc)

    x = x_ref[...]
    g = g_ref[...]
    totals = [None, None]
    for p in range(pairs):
        weights = w_ref[:, p].reshape(model_width, width)
        pre = dot_nn(x, weights[:, : 2 * half])
        out_back = dot_nn(g, weights[:, 2 * half :])
        gate = pre[:, :half]
        up = pre[:, half:]
        sig = 0.5 + 0.5 * jnp.tanh(0.5 * gate)
        share = jnp.concatenate(
            [
                jnp.broadcast_to(gate_ref[:, i : i + 1], (x.shape[0], hidden_local))
                for i in (column + 2 * p, column + 2 * p + 1)
            ],
            axis=1,
        )
        silu = gate * sig
        hidden = (share * (silu * up)).astype(BF)
        hidden_grad = share * out_back
        gate_grad = (hidden_grad * up * (sig + silu * (1.0 - sig))).astype(BF)
        up_grad = (hidden_grad * silu).astype(BF)
        pair_grad = jnp.concatenate([gate_grad, up_grad], axis=1)
        terms = (
            dot_nt(hidden, weights[:, 2 * half :]),
            dot_nt(pair_grad, weights[:, : 2 * half]),
        )
        totals = [t if s is None else s + t for s, t in zip(totals, terms)]
        acc[p, :, : 2 * half] += dot_tn(x, pair_grad)
        acc[p, :, 2 * half :] += dot_tn(g, hidden)
    if not first:
        totals = [s[...] + t for s, t in zip(sums_in, totals)]
    if last:
        rows = x.shape[0] // 2
        for kept_ref, sent_ref, total in zip(sums_out[::2], sums_out[1::2], totals):

            @pl.when(core_ref[0] == 0)
            def _():
                kept_ref[...] = total[:rows]
                sent_ref[...] = total[rows:].astype(BF)

            @pl.when(core_ref[0] == 1)
            def _():
                kept_ref[...] = total[rows:]
                sent_ref[...] = total[:rows].astype(BF)
    else:
        for out_ref, total in zip(sums_out, totals):
            out_ref[...] = total

    @pl.when(step == pl.num_programs(0) - 1)
    def _():
        for p in range(pairs):
            grads_ref[:, p] = acc[p].reshape(blocks, blk, width).astype(BF)


def moe_chunk(core, x, g, gates, weights, sums, column, last):
    rows, model_width = x.shape
    tile = 512
    blocks, pairs, blk, width = weights.shape
    once = pl.Buffered(1)
    row = pl.BlockSpec((tile, model_width), lambda i, s: (i, 0))
    half = pl.BlockSpec((tile // 2, model_width), lambda i, s: (i, 0))
    gate_spec = pl.BlockSpec((tile, gates.shape[1]), lambda i, s: (i, 0))
    whole = pl.BlockSpec(weights.shape, lambda i, s: (0, 0, 0, 0), pipeline_mode=once)
    first = sums is None
    operands = [core, x, g, gates, weights] + ([] if first else list(sums))
    if last:
        out_specs = [half] * 4
        outs = [jax.ShapeDtypeStruct((rows // 2, model_width), t) for t in (FP, BF, FP, BF)]
    else:
        out_specs = [row] * 2
        outs = [jax.ShapeDtypeStruct((rows, model_width), FP)] * 2
    *sums, grads = pl.pallas_call(
        functools.partial(moe_kernel, first, last, column),
        grid_spec=pltpu.PrefetchScalarGridSpec(
            num_scalar_prefetch=1,
            grid=(rows // tile,),
            in_specs=[row, row, gate_spec, whole] + ([] if first else [row, row]),
            out_specs=out_specs + [whole],
            scratch_shapes=[pltpu.VMEM((pairs, model_width, width), FP)],
        ),
        out_shape=outs + [jax.ShapeDtypeStruct(weights.shape, BF)],
        input_output_aliases={} if first or last else {5: 0, 6: 1},
        compiler_params=pltpu.CompilerParams(vmem_limit_bytes=60 << 20),
        cost_estimate=pl.CostEstimate(
            flops=6 * rows * model_width * pairs * width,
            bytes_accessed=90 << 20,
            transcendentals=rows * pairs * width // 3,
        ),
    )(*operands)
    return sums, grads


def pack_experts(w_gate_up, w_down):
    blk, hidden_local = w_gate_up.shape[1], w_gate_up.shape[3]
    gate_up = w_gate_up.reshape(E // 2, 2, blk, 2, hidden_local).transpose(0, 2, 3, 1, 4)
    down = w_down.reshape(E // 2, 2, hidden_local, blk).transpose(0, 3, 1, 2)
    return jnp.concatenate(
        [gate_up.reshape(E // 2, blk, -1), down.reshape(E // 2, blk, -1)], axis=-1
    )


def unpack_experts(packed):
    pairs, blk, width = packed.shape
    hidden_local = width // 6
    packed = packed.astype(FP)
    gate_up = packed[:, :, : 4 * hidden_local].reshape(pairs, blk, 2, 2, hidden_local)
    down = packed[:, :, 4 * hidden_local :].reshape(pairs, blk, 2, hidden_local)
    return (
        gate_up.transpose(0, 3, 1, 2, 4).reshape(2 * pairs, blk, 2, hidden_local),
        down.transpose(0, 2, 3, 1).reshape(2 * pairs, hidden_local, blk),
    )


def split_rows(core_ref, kept_ref, sent_ref, value):
    rows = value.shape[0] // 4
    for x in range(2):
        here = pl.ds(x * rows, rows)
        even, odd = value[2 * x * rows : (2 * x + 1) * rows], value[(2 * x + 1) * rows : (2 * x + 2) * rows]

        @pl.when(core_ref[0] == 0)
        def _():
            kept_ref[here, :] = even
            sent_ref[here, :] = odd.astype(BF)

        @pl.when(core_ref[0] == 1)
        def _():
            kept_ref[here, :] = odd
            sent_ref[here, :] = even.astype(BF)


def attn_forward_kernel(kv_local, core_ref, x_ref, wp_ref, wo_ref, qkv_ref, heads_ref, kept_ref, sent_ref):
    rows = x_ref.shape[0]
    ratio = heads_ref.shape[1] // HD // kv_local
    q_width = kv_local * ratio * HD
    tile = min(256, rows)
    qkv_ref[...] = dot_nn(x_ref[...], wp_ref[...]).astype(BF)
    for kv in range(kv_local):
        keys = qkv_ref[:, q_width + kv * HD : q_width + (kv + 1) * HD]
        values = qkv_ref[:, q_width + (kv_local + kv) * HD : q_width + (kv_local + kv + 1) * HD]
        for start in range(0, rows, tile):
            stop = start + tile
            cols = [slice((kv * ratio + r) * HD, (kv * ratio + r + 1) * HD) for r in range(ratio)]
            query = jnp.concatenate([qkv_ref[start:stop, c] for c in cols], axis=0) * BF(HD**-0.5)
            near = dot_nt(query, keys[start:stop])
            row_pos = lax.broadcasted_iota(jnp.int32, near.shape, 0) & (tile - 1)
            col_pos = lax.broadcasted_iota(jnp.int32, near.shape, 1)
            scores = jnp.where(col_pos <= row_pos, near, -1e30)
            if start:
                scores = jnp.concatenate([dot_nt(query, keys[:start]), scores], axis=1)
            exponent = jnp.exp(scores - jnp.max(scores, axis=-1, keepdims=True))
            total = jnp.sum(exponent, axis=-1, keepdims=True)
            probs = (exponent * (1.0 / total)).astype(BF)
            out = dot_nn(probs, values[:stop]).astype(BF)
            for r, c in enumerate(cols):
                heads_ref[start:stop, c] = out[r * tile : (r + 1) * tile]
    split_rows(core_ref, kept_ref, sent_ref, dot_nt(heads_ref[...], wo_ref[...]))


def attn_backward_kernel(
    kv_local, first, core_ref, dy_ref, x_ref, qkv_ref, heads_ref, wp_ref, wo_ref, *rest
):
    rest = list(rest)
    earlier_ref = None if first else rest.pop(0)
    grads_ref, kept_ref, sent_ref, head_grad_ref, proj_grad_ref, key_acc, value_acc = rest
    rows = x_ref.shape[0]
    ratio = heads_ref.shape[1] // HD // kv_local
    q_width = kv_local * ratio * HD
    proj_width = q_width + 2 * kv_local * HD
    tile = min(256, rows)
    scale = BF(HD**-0.5)
    head_grad_ref[...] = dot_nn(dy_ref[...], wo_ref[...]).astype(BF)
    for kv in range(kv_local):
        key_cols = slice(q_width + kv * HD, q_width + (kv + 1) * HD)
        value_cols = slice(q_width + (kv_local + kv) * HD, q_width + (kv_local + kv + 1) * HD)
        keys = qkv_ref[:, key_cols]
        values = qkv_ref[:, value_cols]
        key_acc[...] = jnp.zeros_like(key_acc)
        value_acc[...] = jnp.zeros_like(value_acc)
        for start in range(0, rows, tile):
            stop = start + tile
            cols = [slice((kv * ratio + r) * HD, (kv * ratio + r + 1) * HD) for r in range(ratio)]
            query = jnp.concatenate([qkv_ref[start:stop, c] for c in cols], axis=0) * scale
            out_grad = jnp.concatenate([head_grad_ref[start:stop, c] for c in cols], axis=0)
            near = dot_nt(keys[start:stop], query)
            key_pos = lax.broadcasted_iota(jnp.int32, near.shape, 0)
            row_pos = lax.broadcasted_iota(jnp.int32, near.shape, 1) & (tile - 1)
            scores = jnp.where(key_pos <= row_pos, near, -1e30)
            if start:
                scores = jnp.concatenate([dot_nt(keys[:start], query), scores], axis=0)
            exponent = jnp.exp(scores - jnp.max(scores, axis=0, keepdims=True))
            probs = exponent * (1.0 / jnp.sum(exponent, axis=0, keepdims=True))
            prob_grad = dot_nt(values[:stop], out_grad)
            inner = jnp.sum(probs * prob_grad, axis=0, keepdims=True)
            score_grad = (probs * (prob_grad - inner)).astype(BF)
            value_acc[:stop] += dot_nn(probs.astype(BF), out_grad)
            key_acc[:stop] += dot_nn(score_grad, query)
            query_grad = (dot_tn(score_grad, keys[:stop]) * (HD**-0.5)).astype(BF)
            for r, c in enumerate(cols):
                proj_grad_ref[start:stop, c] = query_grad[r * tile : (r + 1) * tile]
        proj_grad_ref[:, key_cols] = key_acc[...].astype(BF)
        proj_grad_ref[:, value_cols] = value_acc[...].astype(BF)
    proj_grad = proj_grad_ref[...]
    split_rows(core_ref, kept_ref, sent_ref, dot_nt(proj_grad, wp_ref[...]))
    proj_part = dot_tn(x_ref[...], proj_grad)
    out_part = dot_tn(dy_ref[...], heads_ref[...])
    if first:
        grads_ref[:, :proj_width] = proj_part
        grads_ref[:, proj_width:] = out_part
    else:
        grads_ref[:, :proj_width] = earlier_ref[:, :proj_width] + proj_part
        grads_ref[:, proj_width:] = earlier_ref[:, proj_width:] + out_part


SMEM = pl.BlockSpec(memory_space=pltpu.SMEM)
VMEM = pl.BlockSpec(memory_space=pltpu.VMEM)


def attn_forward(core, x, w_project, out_t, kv_local):
    rows, model_width = x.shape
    heads_width = out_t.shape[1]
    return pl.pallas_call(
        functools.partial(attn_forward_kernel, kv_local),
        in_specs=[SMEM, VMEM, VMEM, VMEM],
        out_specs=[VMEM] * 4,
        out_shape=[
            jax.ShapeDtypeStruct((rows, w_project.shape[1]), BF),
            jax.ShapeDtypeStruct((rows, heads_width), BF),
            jax.ShapeDtypeStruct((rows // 2, model_width), FP),
            jax.ShapeDtypeStruct((rows // 2, model_width), BF),
        ],
        compiler_params=pltpu.CompilerParams(vmem_limit_bytes=56 << 20),
        cost_estimate=pl.CostEstimate(
            flops=14 << 30, bytes_accessed=10 << 20, transcendentals=3 << 20
        ),
    )(core, x, w_project, out_t)


def attn_backward(core, dy, x, qkv, heads, w_project, out_t, earlier, kv_local):
    rows, model_width = x.shape
    width = w_project.shape[1] + out_t.shape[1]
    first = earlier is None
    operands = [core, dy, x, qkv, heads, w_project, out_t] + ([] if first else [earlier])
    return pl.pallas_call(
        functools.partial(attn_backward_kernel, kv_local, first),
        in_specs=[SMEM] + [VMEM] * (len(operands) - 1),
        out_specs=[VMEM] * 3,
        out_shape=[
            jax.ShapeDtypeStruct((model_width, width), FP),
            jax.ShapeDtypeStruct((rows // 2, model_width), FP),
            jax.ShapeDtypeStruct((rows // 2, model_width), BF),
        ],
        scratch_shapes=[
            pltpu.VMEM(heads.shape, BF),
            pltpu.VMEM(qkv.shape, BF),
            pltpu.VMEM((rows, HD), FP),
            pltpu.VMEM((rows, HD), FP),
        ],
        compiler_params=pltpu.CompilerParams(vmem_limit_bytes=56 << 20),
        cost_estimate=pl.CostEstimate(
            flops=30 << 30, bytes_accessed=16 << 20, transcendentals=3 << 20
        ),
    )(*operands)


def on_device(
    block_input,
    cotangent,
    routes,
    gate_weights,
    w_query,
    w_key,
    w_value,
    w_out,
    w_gate_up,
    w_down,
    norm_attn,
    norm_moe,
):
    depth = lax.axis_size("z")
    micro_count, rows_local, model_width = block_input.shape
    kv_local = w_key.shape[1] // HD
    q_width, kv_width = w_query.shape[1], w_key.shape[1]
    proj_width = q_width + 2 * kv_width
    side = lax.axis_index("y")
    core = lax.axis_index("c").astype(jnp.int32).reshape(1)

    packed_attn = jnp.concatenate([w_query, w_key, w_value, w_out.T], axis=1)
    packed = pack_experts(w_gate_up, w_down)
    packed = packed.reshape(2, packed.shape[0] // 2, *packed.shape[1:])
    mine = lax.dynamic_index_in_dim(packed, side, 0, False)
    theirs = lax.dynamic_index_in_dim(packed, 1 - side, 0, False)
    per_chunk = mine.shape[0] // CHUNKS
    chunk_weights = []
    for chunk in range(CHUNKS):
        part = slice(chunk * per_chunk, (chunk + 1) * per_chunk)
        shard = in_order(mine[part], swap(theirs[part], "y"), "y", 0)
        if chunk:
            shard, _ = lax.optimization_barrier((shard, chunk_weights[-1][:1, :1, :8]))
        whole = lax.all_gather(shard, "z", axis=0)
        chunk_weights.append(whole.reshape(-1, *whole.shape[2:]))
    attn_full = gather_dp(packed_attn, depth)
    w_project, out_t = attn_full[:, :proj_width], attn_full[:, proj_width:]

    in_rows = block_input.astype(FP)
    normed_attn, scale_attn = row_norm(in_rows, norm_attn)
    normed_attn = normed_attn.astype(BF)
    attn_in, saved, middle, scale_moe, moe_in = [], [], [], [], []
    for m in range(micro_count):
        attn_in.append(gather_rows(normed_attn[m]))
        qkv, heads, kept, sent = attn_forward(core, attn_in[m], w_project, out_t, kv_local)
        saved.append((qkv, heads))
        middle.append(in_rows[m] + scatter_rows(kept, sent))
        normed_moe, scale = row_norm(middle[m], norm_moe)
        scale_moe.append(scale)
        moe_in.append(gather_pair(normed_moe.astype(BF)))
    moe_in = jnp.concatenate(moe_in)
    moe_grad = jnp.concatenate([gather_pair(cotangent[m]) for m in range(micro_count)])

    expert_ids = jnp.arange(E, dtype=jnp.int32)[:, None, None, None]
    gates = jnp.sum(jnp.where(routes == expert_ids, gate_weights, 0.0), axis=3)
    gates = gates.reshape(2, E // 2, micro_count, -1)
    gates = jnp.stack(
        [
            lax.dynamic_index_in_dim(gates, side, 0, False),
            swap(lax.dynamic_index_in_dim(gates, 1 - side, 0, False), "y"),
        ]
    )
    gates = gates.transpose(2, 0, 3, 1).reshape(-1, E // 2)

    sums = None
    shards = []
    for chunk in range(CHUNKS):
        sums, grads = moe_chunk(
            core,
            moe_in,
            moe_grad,
            gates,
            chunk_weights[chunk],
            sums,
            2 * per_chunk * chunk,
            chunk == CHUNKS - 1,
        )
        grads = grads.reshape(depth, 2, *grads.shape[1:])
        grads = lax.psum_scatter(grads, "z", scatter_dimension=0, tiled=False)
        kept = lax.dynamic_index_in_dim(grads, side, 0, False)
        sent = lax.dynamic_index_in_dim(grads, 1 - side, 0, False)
        shards.append(in_order(kept, swap(sent, "y"), "y", 0))
    packed_grads = jnp.concatenate(shards, axis=1)
    shard_pair, shard_down = unpack_experts(packed_grads.reshape(-1, *packed_grads.shape[2:]))
    mixed_kept, mixed_sent, back_kept, back_sent = (
        s.reshape(micro_count, 2, -1, model_width) for s in sums
    )

    out_grad = cotangent.astype(FP)
    outputs, input_grads = [], []
    gains = jnp.zeros((2, model_width), FP)
    attn_grads = None
    for m in range(micro_count):
        moe_in_grad = scatter_pair(back_kept[m], back_sent[m])
        middle_back, gain_moe = norm_back(middle[m], scale_moe[m], norm_moe, moe_in_grad)
        middle_grad = out_grad[m] + middle_back
        branch_grad = gather_rows(middle_grad.astype(BF))
        attn_grads, kept, sent = attn_backward(
            core, branch_grad, attn_in[m], *saved[m], w_project, out_t, attn_grads, kv_local
        )
        attn_in_grad = scatter_rows(kept, sent)
        in_back, gain_attn = norm_back(in_rows[m], scale_attn[m], norm_attn, attn_in_grad)
        input_grads.append(middle_grad + in_back)
        gains = gains + jnp.stack([gain_attn, gain_moe])
    for m in range(micro_count):
        outputs.append((middle[m] + scatter_pair(mixed_kept[m], mixed_sent[m])).astype(BF))
    attn_shard = scatter_dp(attn_grads, depth)
    gains = sum_all(gains.reshape(16, -1), depth).reshape(2, model_width)
    return (
        jnp.stack(outputs),
        jnp.stack(input_grads),
        attn_shard[:, :q_width],
        attn_shard[:, q_width : q_width + kv_width],
        attn_shard[:, q_width + kv_width : proj_width],
        attn_shard[:, proj_width:].T,
        shard_pair,
        shard_down,
        gains[0],
        gains[1],
    )


def solution(mesh):
    dp, tensor = mesh.shape["dp"], mesh.shape["tensor"]
    fine = Mesh(mesh.devices.reshape(dp // 2, 2, tensor // 2, 2), ("z", "y", "x", "c"))
    dp_axes, tensor_axes = ("z", "y"), ("x", "c")
    rows = P(None, dp_axes + tensor_axes, None)
    return jax.shard_map(
        on_device,
        mesh=fine,
        in_specs=(
            rows,
            rows,
            P(None, dp_axes, None),
            P(None, dp_axes, None),
            P(dp_axes, tensor_axes),
            P(dp_axes, tensor_axes),
            P(dp_axes, tensor_axes),
            P(tensor_axes, dp_axes),
            P(None, dp_axes, None, tensor_axes),
            P(None, tensor_axes, dp_axes),
            P(),
            P(),
        ),
        out_specs=(
            rows,
            rows,
            P(dp_axes, tensor_axes),
            P(dp_axes, tensor_axes),
            P(dp_axes, tensor_axes),
            P(tensor_axes, dp_axes),
            P(None, dp_axes, None, tensor_axes),
            P(None, tensor_axes, dp_axes),
            P(),
            P(),
        ),
        check_vma=False,
    )
```

```python
import functools

import jax
import jax.numpy as jnp
from jax import lax
from jax.experimental import pallas as pl
from jax.experimental.pallas import tpu as pltpu
from jax.sharding import Mesh
from jax.sharding import PartitionSpec as P

HD = 64
E = 32
CHUNKS = (3, 2, 2, 1)

EPSILON = 1e-06
BF = jnp.bfloat16
FP = jnp.float32


def dot_nn(left, right):
    return lax.dot_general(left, right, (((1,), (0,)), ((), ())), preferred_element_type=FP)


def dot_tn(left, right):
    return lax.dot_general(left, right, (((0,), (0,)), ((), ())), preferred_element_type=FP)


def dot_nt(left, right):
    return lax.dot_general(left, right, (((1,), (1,)), ((), ())), preferred_element_type=FP)


def row_norm(in_rows, gain_vec):
    row_scale = lax.rsqrt(jnp.mean(in_rows * in_rows, axis=-1, keepdims=True) + EPSILON)
    return (in_rows * row_scale * gain_vec, row_scale)


def norm_back(in_rows, row_scale, gain_vec, grad_in):
    weighted = grad_in * gain_vec
    inner = jnp.mean(weighted * in_rows, axis=-1, keepdims=True)
    returned = row_scale * weighted - in_rows * row_scale * row_scale * row_scale * inner
    gain_part = jnp.sum(grad_in * in_rows * row_scale, axis=0)
    return (returned, gain_part)


def swap(value, axis):
    return lax.ppermute(value, axis, [(0, 1), (1, 0)])


def after(value, *earlier):
    return lax.optimization_barrier((value, *earlier))[0]


def gather_rows(rows):
    across = swap(rows, "x")
    return [rows, across, swap(rows, "c"), swap(across, "c")]


def gather_pair(rows):
    near = swap(rows, "y")
    blocks = jnp.stack([rows, near, swap(rows, "x"), swap(near, "x")])
    return blocks, swap(blocks, "c")


def scatter_rows(kept, sent):
    got = swap(sent, "c").astype(FP)
    across = swap((kept[1] + got[1]).astype(BF), "x").astype(FP)
    return kept[0] + got[0] + across


def scatter_pair(kept, sent):
    got = swap(sent, "c").astype(FP)
    across = swap((kept[2:] + got[2:]).astype(BF), "x").astype(FP)
    near = swap((kept[1] + got[1] + across[1]).astype(BF), "y").astype(FP)
    return kept[0] + got[0] + across[0] + near


def turns(depth):
    up = [(i, (i + 1) % depth) for i in range(depth)]
    down = [(i, (i - 1) % depth) for i in range(depth)]
    return up, down


def gather_dp(shard, depth):
    turn_up, turn_down = turns(depth)
    place, side = lax.axis_index("z"), lax.axis_index("y")
    line = [(shard, place)]
    piece = shard
    for k in range(1, depth // 2 + 1):
        piece = lax.ppermute(piece, "z", turn_up)
        line.append((piece, lax.rem(place + depth - k, depth)))
    piece = shard
    for k in range(1, (depth - 1) // 2 + 1):
        piece = lax.ppermute(piece, "z", turn_down)
        line.append((piece, lax.rem(place + k, depth)))
    pieces = [p for p, _ in line] + [swap(p, "y") for p, _ in line]
    index = [2 * z + side for _, z in line] + [2 * z + 1 - side for _, z in line]
    return pieces, jnp.stack(index).astype(jnp.int32)


def scatter_dp(kept, sent, depth):
    column = kept + swap(sent, "y").astype(FP)
    turn_up, turn_down = turns(depth)
    total = column[0]
    for turn, sign, steps in ((turn_up, 1, depth // 2), (turn_down, -1, (depth - 1) // 2)):
        carried = None
        for distance in range(steps, 0, -1):
            block = column[(sign * distance) % depth]
            carried = block if carried is None else block + carried
            carried = lax.ppermute(carried.astype(BF), "z", turn).astype(FP)
        if carried is not None:
            total = total + carried
    return total


def sum_all(value, depth):
    for axis in ("c", "x", "y"):
        value = value + swap(value, axis)
    reach = 1
    while reach < depth:
        pairs = [(i, i ^ reach) for i in range(depth)]
        value = value + lax.ppermute(value, "z", pairs)
        reach *= 2
    return value


SMEM = pl.BlockSpec(memory_space=pltpu.SMEM)
VMEM = pl.BlockSpec(memory_space=pltpu.VMEM)


def pack_kernel(side_ref, gate_up_ref, down_ref, *rest):
    *outs, rows_scr = rest
    blk = down_ref.shape[2]
    offset = 0
    for mine_ref, theirs_ref in zip(outs[::2], outs[1::2]):
        pairs = mine_ref.shape[0]
        hidden_local = mine_ref.shape[2] // 6
        for out_ref, half in ((theirs_ref, 1 - side_ref[0]), (mine_ref, side_ref[0])):
            for p in range(pairs):
                for i in range(2):
                    expert = half * (E // 2) + 2 * (offset + p) + i
                    rows_scr[...] = gate_up_ref[expert].astype(FP)
                    for part in range(2):
                        cols = slice((2 * part + i) * hidden_local, (2 * part + i + 1) * hidden_local)
                        out_ref[p, :, cols] = rows_scr[pl.ds(part, blk, stride=2), :].astype(BF)
                    cols = slice((4 + i) * hidden_local, (5 + i) * hidden_local)
                    out_ref[p, :, cols] = down_ref[expert].astype(FP).T.astype(BF)
        offset += pairs


def pack_experts(side, w_gate_up, w_down):
    experts, blk, _, hidden_local = w_gate_up.shape
    shapes = [jax.ShapeDtypeStruct((pairs, blk, 6 * hidden_local), BF) for pairs in CHUNKS]
    outs = pl.pallas_call(
        pack_kernel,
        in_specs=[SMEM, VMEM, VMEM],
        out_specs=[VMEM] * (2 * len(CHUNKS)),
        out_shape=[shape for shape in shapes for _ in range(2)],
        scratch_shapes=[pltpu.VMEM((2 * blk, hidden_local), FP)],
        compiler_params=pltpu.CompilerParams(vmem_limit_bytes=32 << 20),
        cost_estimate=pl.CostEstimate(flops=1 << 20, bytes_accessed=8 << 20, transcendentals=0),
    )(side, w_gate_up.reshape(experts, 2 * blk, hidden_local), w_down)
    return list(zip(outs[::2], outs[1::2]))


def unpack_kernel(side_ref, *refs):
    *ins, gate_up_ref, down_ref = refs
    blk = down_ref.shape[2]
    offset = 0
    for kept_ref, got_ref in zip(ins[::2], ins[1::2]):
        pairs = got_ref.shape[0]
        hidden_local = got_ref.shape[2] // 6
        for mine, half in ((True, side_ref[0]), (False, 1 - side_ref[0])):
            for p in range(pairs):
                packed = (kept_ref[0, p] if mine else got_ref[p]).astype(FP)
                for i in range(2):
                    expert = half * (E // 2) + 2 * (offset + p) + i
                    for part in range(2):
                        cols = slice((2 * part + i) * hidden_local, (2 * part + i + 1) * hidden_local)
                        gate_up_ref[expert, pl.ds(part, blk, stride=2), :] = packed[:, cols]
                    down_ref[expert] = packed[:, (4 + i) * hidden_local : (5 + i) * hidden_local].T
        offset += pairs


def unpack_experts(side, shards):
    blk, width = shards[0][1].shape[1:]
    hidden_local = width // 6
    operands = [array for shard in shards for array in shard]
    gate_up, down = pl.pallas_call(
        unpack_kernel,
        in_specs=[SMEM] + [VMEM] * len(operands),
        out_specs=[VMEM, VMEM],
        out_shape=[
            jax.ShapeDtypeStruct((E, 2 * blk, hidden_local), FP),
            jax.ShapeDtypeStruct((E, hidden_local, blk), FP),
        ],
        compiler_params=pltpu.CompilerParams(vmem_limit_bytes=32 << 20),
        cost_estimate=pl.CostEstimate(flops=1 << 20, bytes_accessed=12 << 20, transcendentals=0),
    )(side, *operands)
    return gate_up.reshape(E, blk, 2, hidden_local), down


def pack_attn_kernel(query_ref, key_ref, value_ref, out_ref, packed_ref):
    start = 0
    for ref in (query_ref, key_ref, value_ref):
        packed_ref[:, start : start + ref.shape[1]] = ref[...]
        start += ref.shape[1]
    packed_ref[:, start:] = out_ref[...].astype(FP).T.astype(BF)


def pack_attn(w_query, w_key, w_value, w_out):
    width = w_query.shape[1] + w_key.shape[1] + w_value.shape[1] + w_out.shape[0]
    return pl.pallas_call(
        pack_attn_kernel,
        in_specs=[VMEM] * 4,
        out_specs=VMEM,
        out_shape=jax.ShapeDtypeStruct((w_query.shape[0], width), BF),
        cost_estimate=pl.CostEstimate(flops=1 << 20, bytes_accessed=1 << 20, transcendentals=0),
    )(w_query, w_key, w_value, w_out)


def moe_kernel(first, last, start, column, side_ref, xa_ref, xb_ref, ga_ref, gb_ref, gate_ref, w_ref, *rest):
    rest = list(rest)
    sums_in = [] if first else [rest.pop(0), rest.pop(0)]
    earlier_ref = None if start else rest.pop(0)
    acc = rest.pop()
    grads_ref = rest.pop()
    sums_out = rest
    step = pl.program_id(0)
    blocks, pairs, blk, width = w_ref.shape
    model_width = blocks * blk
    half = width // 3
    hidden_local = half // 2

    def spot(block):
        place = (block // 2) * 2 + (side_ref[0] + block % 2) % 2
        return pl.ds(pl.multiple_of(place * blk, blk), blk)

    @pl.when(step == 0)
    def _():
        if start:
            acc[...] = jnp.zeros_like(acc)
        else:
            for p in range(pairs):
                for block in range(blocks):
                    acc[p, spot(block), :] = earlier_ref[block, p].astype(FP)

    x = jnp.concatenate([xa_ref[...], xb_ref[...]], axis=0)
    g = jnp.concatenate([ga_ref[...], gb_ref[...]], axis=0)
    totals = [None, None]
    for p in range(pairs):
        weights = w_ref[:, p].reshape(model_width, width)
        pre = dot_nn(x, weights[:, : 2 * half])
        out_back = dot_nn(g, weights[:, 2 * half :])
        gate = pre[:, :half]
        up = pre[:, half:]
        sig = 0.5 + 0.5 * jnp.tanh(0.5 * gate)
        share = jnp.concatenate(
            [
                jnp.broadcast_to(gate_ref[:, i : i + 1], (x.shape[0], hidden_local))
                for i in (column + 2 * p, column + 2 * p + 1)
            ],
            axis=1,
        )
        silu = gate * sig
        hidden = (share * (silu * up)).astype(BF)
        hidden_grad = share * out_back
        gate_grad = (hidden_grad * up * (sig + silu * (1.0 - sig))).astype(BF)
        up_grad = (hidden_grad * silu).astype(BF)
        pair_grad = jnp.concatenate([gate_grad, up_grad], axis=1)
        terms = (
            dot_nt(hidden, weights[:, 2 * half :]),
            dot_nt(pair_grad, weights[:, : 2 * half]),
        )
        totals = [t if s is None else s + t for s, t in zip(totals, terms)]
        acc[p, :, : 2 * half] += dot_tn(x, pair_grad)
        acc[p, :, 2 * half :] += dot_tn(g, hidden)
    if not first:
        totals = [s[...] + t for s, t in zip(sums_in, totals)]
    if last:
        rows = xa_ref.shape[0]
        for kept_ref, sent_ref, total in zip(sums_out[::2], sums_out[1::2], totals):
            kept_ref[...] = total[:rows]
            sent_ref[...] = total[rows:].astype(BF)
    else:
        for out_ref, total in zip(sums_out, totals):
            out_ref[...] = total

    @pl.when(step == pl.num_programs(0) - 1)
    def _():
        for p in range(pairs):
            for block in range(blocks):
                grads_ref[block, p] = acc[p, spot(block), :].astype(BF)


def moe_chunk(side, x, g, gates, weights, sums, earlier, micro, column, last):
    count, rows, model_width = x[0].shape
    blocks, pairs, blk, width = weights.shape
    once = pl.Buffered(1)
    row = pl.BlockSpec((None, 2 * rows, model_width), lambda i: (i, 0, 0))
    half = pl.BlockSpec((None, rows, model_width), lambda i: (i, 0, 0))
    g_spec = pl.BlockSpec((None, None, rows, model_width), lambda i: (i, micro, 0, 0))
    gate_spec = pl.BlockSpec((None, None, 2 * rows, gates.shape[-1]), lambda i: (micro, i, 0, 0))
    whole = pl.BlockSpec(weights.shape, lambda i: (0, 0, 0, 0), pipeline_mode=once)
    first, start = sums is None, earlier is None
    operands = [side, *x, *g, gates, weights] + ([] if first else list(sums))
    operands += [] if start else [earlier]
    if last:
        out_specs = [half] * 4
        outs = [jax.ShapeDtypeStruct((count, rows, model_width), t) for t in (FP, BF, FP, BF)]
    else:
        out_specs = [row] * 2
        outs = [jax.ShapeDtypeStruct((count, 2 * rows, model_width), FP)] * 2
    *sums, grads = pl.pallas_call(
        functools.partial(moe_kernel, first, last, start, column),
        grid=(count,),
        in_specs=[SMEM, half, half, g_spec, g_spec, gate_spec, whole]
        + ([] if first else [row, row])
        + ([] if start else [whole]),
        out_specs=out_specs + [whole],
        scratch_shapes=[pltpu.VMEM((pairs, model_width, width), FP)],
        out_shape=outs + [jax.ShapeDtypeStruct(weights.shape, BF)],
        input_output_aliases={} if first or last else {7: 0, 8: 1},
        compiler_params=pltpu.CompilerParams(vmem_limit_bytes=60 << 20),
        cost_estimate=pl.CostEstimate(
            flops=12 * count * rows * model_width * pairs * width,
            bytes_accessed=48 << 20,
            transcendentals=2 * count * rows * pairs * width // 3,
        ),
    )(*operands)
    return sums, grads


def place_rows(spots_ref, pieces, whole_ref):
    rows = pieces[0].shape[0]
    for i, piece in enumerate(pieces):
        whole_ref[pl.ds(pl.multiple_of(spots_ref[i] * rows, rows), rows), :] = piece[...]


def product_rows(spots_ref, left_ref, right, kept_ref, sent_ref):
    rows = kept_ref.shape[1]
    for i in range(4):
        here = pl.ds(pl.multiple_of(spots_ref[i] * rows, rows), rows)
        value = dot_nt(left_ref[here, :], right)
        if i < 2:
            kept_ref[i] = value
        else:
            sent_ref[i - 2] = value.astype(BF)


def attn_forward_kernel(widths, n_weights, spots_ref, weight_spots_ref, *rest):
    q_width, kv_width = widths
    x_pieces, rest = rest[:4], rest[4:]
    w_pieces, rest = rest[:n_weights], rest[n_weights:]
    if n_weights > 1:
        qkv_ref, heads_ref, kept_ref, sent_ref, w_ref, x_scr = rest
        place_rows(weight_spots_ref, w_pieces, w_ref)
    else:
        qkv_ref, heads_ref, kept_ref, sent_ref, x_scr = rest
        w_ref = w_pieces[0]
    place_rows(spots_ref, x_pieces, x_scr)
    rows = x_scr.shape[0]
    proj_width = q_width + 2 * kv_width
    ratio = q_width // kv_width
    tile = min(256, rows)
    qkv_ref[...] = dot_nn(x_scr[...], w_ref[:, :proj_width]).astype(BF)
    for kv in range(kv_width // HD):
        keys = qkv_ref[:, q_width + kv * HD : q_width + (kv + 1) * HD]
        values = qkv_ref[:, q_width + kv_width + kv * HD : q_width + kv_width + (kv + 1) * HD]
        cols = [slice((kv * ratio + r) * HD, (kv * ratio + r + 1) * HD) for r in range(ratio)]
        for start in range(0, rows, tile):
            stop = start + tile
            query = jnp.concatenate([qkv_ref[start:stop, c] for c in cols], axis=0) * BF(HD**-0.5)
            near = dot_nt(query, keys[start:stop])
            row_pos = lax.broadcasted_iota(jnp.int32, near.shape, 0) & (tile - 1)
            col_pos = lax.broadcasted_iota(jnp.int32, near.shape, 1)
            scores = jnp.where(col_pos <= row_pos, near, -1e30)
            if start:
                scores = jnp.concatenate([dot_nt(query, keys[:start]), scores], axis=1)
            exponent = jnp.exp(scores - jnp.max(scores, axis=-1, keepdims=True))
            total = jnp.sum(exponent, axis=-1, keepdims=True)
            probs = (exponent * (1.0 / total)).astype(BF)
            out = dot_nn(probs, values[:stop]).astype(BF)
            for r, c in enumerate(cols):
                heads_ref[start:stop, c] = out[r * tile : (r + 1) * tile]
    product_rows(spots_ref, heads_ref, w_ref[:, proj_width:], kept_ref, sent_ref)


def attn_backward_kernel(widths, first, spots_ref, block_spots_ref, *rest):
    q_width, kv_width = widths
    proj_width = q_width + 2 * kv_width
    dy_pieces, x_pieces, rest = rest[:4], rest[4:8], list(rest[8:])
    qkv_ref, heads_ref, w_ref = rest[:3]
    rest = rest[3:]
    if first:
        grads_ref, kept_ref, sent_ref = rest[:3]
        rest = rest[3:]
    else:
        earlier_ref, grads_kept_ref, grads_sent_ref, kept_ref, sent_ref = rest[:5]
        grads_ref = rest[5]
        rest = rest[6:]
    dy_scr, x_scr, head_grad_ref, proj_grad_ref, key_acc, value_acc = rest
    place_rows(spots_ref, dy_pieces, dy_scr)
    place_rows(spots_ref, x_pieces, x_scr)
    rows = x_scr.shape[0]
    ratio = q_width // kv_width
    tile = min(256, rows)
    head_grad_ref[...] = dot_nn(dy_scr[...], w_ref[:, proj_width:]).astype(BF)
    for kv in range(kv_width // HD):
        key_cols = slice(q_width + kv * HD, q_width + (kv + 1) * HD)
        value_cols = slice(q_width + kv_width + kv * HD, q_width + kv_width + (kv + 1) * HD)
        cols = [slice((kv * ratio + r) * HD, (kv * ratio + r + 1) * HD) for r in range(ratio)]
        keys = qkv_ref[:, key_cols]
        values = qkv_ref[:, value_cols]
        key_acc[...] = jnp.zeros_like(key_acc)
        value_acc[...] = jnp.zeros_like(value_acc)
        for start in range(0, rows, tile):
            stop = start + tile
            query = jnp.concatenate([qkv_ref[start:stop, c] for c in cols], axis=0) * BF(HD**-0.5)
            out_grad = jnp.concatenate([head_grad_ref[start:stop, c] for c in cols], axis=0)
            near = dot_nt(keys[start:stop], query)
            key_pos = lax.broadcasted_iota(jnp.int32, near.shape, 0)
            row_pos = lax.broadcasted_iota(jnp.int32, near.shape, 1) & (tile - 1)
            scores = jnp.where(key_pos <= row_pos, near, -1e30)
            if start:
                scores = jnp.concatenate([dot_nt(keys[:start], query), scores], axis=0)
            exponent = jnp.exp(scores - jnp.max(scores, axis=0, keepdims=True))
            probs = exponent * (1.0 / jnp.sum(exponent, axis=0, keepdims=True))
            prob_grad = dot_nt(values[:stop], out_grad)
            inner = jnp.sum(probs * prob_grad, axis=0, keepdims=True)
            score_grad = (probs * (prob_grad - inner)).astype(BF)
            value_acc[:stop] += dot_nn(probs.astype(BF), out_grad)
            key_acc[:stop] += dot_nn(score_grad, query)
            query_grad = (dot_tn(score_grad, keys[:stop]) * (HD**-0.5)).astype(BF)
            for r, c in enumerate(cols):
                proj_grad_ref[start:stop, c] = query_grad[r * tile : (r + 1) * tile]
        proj_grad_ref[:, key_cols] = key_acc[...].astype(BF)
        proj_grad_ref[:, value_cols] = value_acc[...].astype(BF)
    product_rows(spots_ref, proj_grad_ref, w_ref[:, :proj_width], kept_ref, sent_ref)
    proj_part = dot_tn(x_scr[...], proj_grad_ref[...])
    out_part = dot_tn(dy_scr[...], heads_ref[...])
    if first:
        grads_ref[:, :proj_width] = proj_part
        grads_ref[:, proj_width:] = out_part
    else:
        grads_ref[:, :proj_width] = earlier_ref[:, :proj_width] + proj_part
        grads_ref[:, proj_width:] = earlier_ref[:, proj_width:] + out_part
        depth, blk, _ = grads_kept_ref.shape
        for r in range(depth):
            here = pl.ds(pl.multiple_of(block_spots_ref[r] * blk, blk), blk)
            grads_kept_ref[r] = grads_ref[here, :]
            here = pl.ds(pl.multiple_of(block_spots_ref[depth + r] * blk, blk), blk)
            grads_sent_ref[r] = grads_ref[here, :].astype(BF)


def attn_forward(spots, weight_spots, pieces, weights, widths):
    rows, model_width = pieces[0].shape
    width = weights[0].shape[1]
    whole = len(weights) == 1
    outs = [
        jax.ShapeDtypeStruct((4 * rows, widths[0] + 2 * widths[1]), BF),
        jax.ShapeDtypeStruct((4 * rows, widths[0]), BF),
        jax.ShapeDtypeStruct((2, rows, model_width), FP),
        jax.ShapeDtypeStruct((2, rows, model_width), BF),
    ] + ([] if whole else [jax.ShapeDtypeStruct((model_width, width), BF)])
    results = pl.pallas_call(
        functools.partial(attn_forward_kernel, widths, len(weights)),
        in_specs=[SMEM] * 2 + [VMEM] * (4 + len(weights)),
        out_specs=[VMEM] * len(outs),
        out_shape=outs,
        scratch_shapes=[pltpu.VMEM((4 * rows, model_width), BF)],
        compiler_params=pltpu.CompilerParams(vmem_limit_bytes=56 << 20),
        cost_estimate=pl.CostEstimate(
            flops=14 << 30, bytes_accessed=10 << 20, transcendentals=3 << 20
        ),
    )(spots, weight_spots, *pieces, *weights)
    return results if not whole else [*results, weights[0]]


def attn_backward(spots, block_spots, dy, x, qkv, heads, weights, earlier, widths):
    rows, model_width = x[0].shape
    width = weights.shape[1]
    first = earlier is None
    operands = [*dy, *x, qkv, heads, weights] + ([] if first else [earlier])
    depth = block_spots.shape[0] // 2
    whole = (model_width, width)
    blocks = (depth, model_width // depth // 2, width)
    scratch = [
        pltpu.VMEM((4 * rows, model_width), BF),
        pltpu.VMEM((4 * rows, model_width), BF),
        pltpu.VMEM(heads.shape, BF),
        pltpu.VMEM(qkv.shape, BF),
        pltpu.VMEM((4 * rows, HD), FP),
        pltpu.VMEM((4 * rows, HD), FP),
    ]
    if first:
        outs = [jax.ShapeDtypeStruct(whole, FP)]
    else:
        outs = [jax.ShapeDtypeStruct(blocks, FP), jax.ShapeDtypeStruct(blocks, BF)]
        scratch = [pltpu.VMEM(whole, FP)] + scratch
    outs += [jax.ShapeDtypeStruct((2, rows, model_width), t) for t in (FP, BF)]
    return pl.pallas_call(
        functools.partial(attn_backward_kernel, widths, first),
        in_specs=[SMEM] * 2 + [VMEM] * len(operands),
        out_specs=[VMEM] * len(outs),
        out_shape=outs,
        scratch_shapes=scratch,
        compiler_params=pltpu.CompilerParams(vmem_limit_bytes=58 << 20),
        cost_estimate=pl.CostEstimate(
            flops=30 << 30, bytes_accessed=16 << 20, transcendentals=3 << 20
        ),
    )(spots, block_spots, *operands)


def on_device(
    block_input,
    cotangent,
    routes,
    gate_weights,
    w_query,
    w_key,
    w_value,
    w_out,
    w_gate_up,
    w_down,
    norm_attn,
    norm_moe,
):
    depth = lax.axis_size("z")
    micro_count, rows_local, model_width = block_input.shape
    q_width, kv_width = w_query.shape[1], w_key.shape[1]
    widths = (q_width, kv_width)
    proj_width = q_width + 2 * kv_width
    side, chip, core = lax.axis_index("y"), lax.axis_index("x"), lax.axis_index("c")
    side_at = side.astype(jnp.int32).reshape(1)
    spots = jnp.stack([2 * x + c for c in (core, 1 - core) for x in (chip, 1 - chip)])
    spots = spots.astype(jnp.int32)
    place = lax.axis_index("z")
    block_spots = jnp.stack(
        [2 * lax.rem(place + r, depth) + s for s in (side, 1 - side) for r in range(depth)]
    ).astype(jnp.int32)

    in_rows = block_input.astype(FP)
    normed_attn, scale_attn = row_norm(in_rows, norm_attn)
    normed_attn = normed_attn.astype(BF)
    attn_in = [gather_rows(normed_attn[m]) for m in range(micro_count)]
    attn_pieces, weight_spots = gather_dp(pack_attn(w_query, w_key, w_value, w_out), depth)

    packed = pack_experts(side_at, w_gate_up, w_down)
    chunk_weights = []
    for mine, theirs in packed:
        got = swap(theirs, "y")
        if chunk_weights:
            got = after(got, chunk_weights[-1][:1, :1, :8, :128])
        first = side == 0
        shard = jnp.stack([jnp.where(first, mine, got), jnp.where(first, got, mine)])
        whole = lax.all_gather(shard, "z", axis=0)
        chunk_weights.append(whole.reshape(-1, *whole.shape[2:]))

    expert_ids = jnp.arange(E, dtype=jnp.int32)[:, None, None, None]
    gates = jnp.sum(jnp.where(routes == expert_ids, gate_weights, 0.0), axis=3)
    gates = gates.reshape(2, E // 2, micro_count, 2, 2, rows_local)
    gates = jnp.where(chip == 0, gates, gates[:, :, :, ::-1])
    gates = jnp.where(core == 0, gates, gates[:, :, :, :, ::-1])
    mine = lax.dynamic_index_in_dim(gates, side, 0, False)
    theirs = lax.dynamic_index_in_dim(gates, 1 - side, 0, False)
    gates = jnp.stack([mine, swap(theirs.reshape(E // 2, -1), "y").reshape(mine.shape)])
    gates = gates.transpose(2, 3, 0, 4, 5, 1).reshape(micro_count, 4, 2 * rows_local, E // 2)

    moe_grad = gather_pair(after(cotangent, attn_in[-1][1]))
    saved, middle, scale_moe, moe_in = [], [], [], []
    weights = attn_pieces
    for m in range(micro_count):
        qkv, heads, kept, sent, whole = attn_forward(
            spots, weight_spots, attn_in[m], weights, widths
        )
        weights = [whole]
        saved.append((qkv, heads))
        middle.append(in_rows[m] + scatter_rows(kept, sent))
        normed_moe, scale = row_norm(middle[m], norm_moe)
        scale_moe.append(scale)
        moe_in.append(gather_pair(normed_moe.astype(BF)))

    sums = [None] * micro_count
    shards = []
    column = 0
    for chunk, pairs in enumerate(CHUNKS):
        grads = None
        for m in range(micro_count):
            sums[m], grads = moe_chunk(
                side_at,
                moe_in[m],
                moe_grad,
                gates,
                chunk_weights[chunk],
                sums[m],
                grads,
                m,
                column,
                chunk == len(CHUNKS) - 1,
            )
        column += 2 * pairs
        grads = grads.reshape(depth, 2, *grads.shape[1:])
        grads = lax.psum_scatter(grads, "z", scatter_dimension=0, tiled=False)
        shards.append((grads, swap(grads[1], "y")))
    shard_pair, shard_down = unpack_experts(side_at, shards)

    out_grad = cotangent.astype(FP)
    outputs, input_grads = [], []
    gains = jnp.zeros((2, model_width), FP)
    middle_grad, branch_grad = [], []
    for m in range(micro_count):
        moe_in_grad = scatter_pair(*sums[m][2:])
        middle_back, gain_moe = norm_back(middle[m], scale_moe[m], norm_moe, moe_in_grad)
        middle_grad.append(out_grad[m] + middle_back)
        branch_grad.append(gather_rows(middle_grad[m].astype(BF)))
        gains = gains.at[1].add(gain_moe)
    results = None
    for m in range(micro_count):
        results = attn_backward(
            spots,
            block_spots,
            branch_grad[m],
            attn_in[m],
            *saved[m],
            weights[0],
            None if results is None else results[0],
            widths,
        )
        attn_in_grad = scatter_rows(*results[-2:])
        in_back, gain_attn = norm_back(in_rows[m], scale_attn[m], norm_attn, attn_in_grad)
        input_grads.append(middle_grad[m] + in_back)
        gains = gains.at[0].add(gain_attn)
    for m in range(micro_count):
        kept, sent = sums[m][:2]
        sent = after(sent, branch_grad[-1][1])
        outputs.append((middle[m] + scatter_pair(kept, sent)).astype(BF))
    attn_shard = scatter_dp(results[0], results[1], depth)
    gains = sum_all(gains.reshape(16, -1), depth).reshape(2, model_width)
    return (
        jnp.stack(outputs),
        jnp.stack(input_grads),
        attn_shard[:, :q_width],
        attn_shard[:, q_width : q_width + kv_width],
        attn_shard[:, q_width + kv_width : proj_width],
        attn_shard[:, proj_width:].T,
        shard_pair,
        shard_down,
        gains[0],
        gains[1],
    )


def solution(mesh):
    dp, tensor = mesh.shape["dp"], mesh.shape["tensor"]
    fine = Mesh(mesh.devices.reshape(dp // 2, 2, tensor // 2, 2), ("z", "y", "x", "c"))
    dp_axes, tensor_axes = ("z", "y"), ("x", "c")
    rows = P(None, dp_axes + tensor_axes, None)
    return jax.shard_map(
        on_device,
        mesh=fine,
        in_specs=(
            rows,
            rows,
            P(None, dp_axes, None),
            P(None, dp_axes, None),
            P(dp_axes, tensor_axes),
            P(dp_axes, tensor_axes),
            P(dp_axes, tensor_axes),
            P(tensor_axes, dp_axes),
            P(None, dp_axes, None, tensor_axes),
            P(None, tensor_axes, dp_axes),
            P(),
            P(),
        ),
        out_specs=(
            rows,
            rows,
            P(dp_axes, tensor_axes),
            P(dp_axes, tensor_axes),
            P(dp_axes, tensor_axes),
            P(tensor_axes, dp_axes),
            P(None, dp_axes, None, tensor_axes),
            P(None, tensor_axes, dp_axes),
            P(),
            P(),
        ),
        check_vma=False,
    )
```

```python
import functools

import jax
import jax.numpy as jnp
from jax import lax
from jax.experimental import pallas as pl
from jax.experimental.pallas import tpu as pltpu
from jax.sharding import Mesh
from jax.sharding import PartitionSpec as P

HD = 64
E = 32
CHUNKS = (4, 4)

EPSILON = 1e-06
BF = jnp.bfloat16
FP = jnp.float32


def dot_nn(left, right):
    return lax.dot_general(left, right, (((1,), (0,)), ((), ())), preferred_element_type=FP)


def dot_tn(left, right):
    return lax.dot_general(left, right, (((0,), (0,)), ((), ())), preferred_element_type=FP)


def dot_nt(left, right):
    return lax.dot_general(left, right, (((1,), (1,)), ((), ())), preferred_element_type=FP)


def row_norm(in_rows, gain_vec):
    row_scale = lax.rsqrt(jnp.mean(in_rows * in_rows, axis=-1, keepdims=True) + EPSILON)
    return (in_rows * row_scale * gain_vec, row_scale)


def norm_back(in_rows, row_scale, gain_vec, grad_in):
    weighted = grad_in * gain_vec
    inner = jnp.mean(weighted * in_rows, axis=-1, keepdims=True)
    returned = row_scale * weighted - in_rows * row_scale * row_scale * row_scale * inner
    gain_part = jnp.sum(grad_in * in_rows * row_scale, axis=0)
    return (returned, gain_part)


def swap(value, axis):
    return lax.ppermute(value, axis, [(0, 1), (1, 0)])


def after(value, *earlier):
    return lax.optimization_barrier((value, *earlier))[0]


def together(*values):
    return lax.optimization_barrier(values)


def cross(value):
    return lax.ppermute(value, ("y", "x"), [(i, 3 - i) for i in range(4)])


def plus(left, right):
    return left + right.astype(FP)


def scatter_pair(kept, sent):
    got = swap(sent, "c")
    sent = [plus(kept[i], got[i]).astype(BF) for i in (1, 2, 3)]
    return plus(kept[0], got[0]), sent, [swap(sent[0], "y"), swap(sent[1], "x"), cross(sent[2])]


def sum_of(total, parts):
    for part in parts:
        total = plus(total, part)
    return total


def along_z(shard, depth):
    place = lax.axis_index("z")
    turns_taken = [k for k in range(-((depth - 1) // 2), depth // 2 + 1) if k]
    pieces = [shard]
    for k in turns_taken:
        pieces.append(lax.ppermute(shard, "z", [(i, (i + k) % depth) for i in range(depth)]))
    return pieces, [lax.rem(place + depth - k, depth) for k in [0, *turns_taken]]


def scatter_dp(kept, sent, depth):
    column = kept + swap(sent, "y").astype(FP)
    total = column[0]
    for r in range(1, depth):
        turn = [(i, (i + r) % depth) for i in range(depth)]
        total = plus(total, lax.ppermute(column[r].astype(BF), "z", turn))
    return total


def sum_all(value, depth):
    for axis in ("c", "x", "y"):
        value = value + swap(value, axis)
    reach = 1
    while reach < depth:
        pairs = [(i, i ^ reach) for i in range(depth)]
        value = value + lax.ppermute(value, "z", pairs)
        reach *= 2
    return value


def cost(flops):
    return pl.CostEstimate(flops=flops, bytes_accessed=1 << 20, transcendentals=0)


SMALL = cost(1 << 30)
SMEM = pl.BlockSpec(memory_space=pltpu.SMEM)
VMEM = pl.BlockSpec(memory_space=pltpu.VMEM)


def pack_kernel(side_ref, gate_up_ref, down_ref, *rest):
    *outs, rows_scr = rest
    blk = down_ref.shape[2]
    offset = 0
    for mine_ref, theirs_ref in zip(outs[::2], outs[1::2]):
        pairs = mine_ref.shape[0]
        hidden_local = mine_ref.shape[2] // 6
        for out_ref, half in ((theirs_ref, 1 - side_ref[0]), (mine_ref, side_ref[0])):
            for p in range(pairs):
                for i in range(2):
                    expert = half * (E // 2) + 2 * (offset + p) + i
                    rows_scr[...] = gate_up_ref[expert].astype(FP)
                    for part in range(2):
                        cols = slice((2 * part + i) * hidden_local, (2 * part + i + 1) * hidden_local)
                        out_ref[p, :, cols] = rows_scr[pl.ds(part, blk, stride=2), :].astype(BF)
                    cols = slice((4 + i) * hidden_local, (5 + i) * hidden_local)
                    out_ref[p, :, cols] = down_ref[expert].astype(FP).T.astype(BF)
        offset += pairs


def pack_experts(side, w_gate_up, w_down):
    experts, blk, _, hidden_local = w_gate_up.shape
    shapes = [jax.ShapeDtypeStruct((pairs, blk, 6 * hidden_local), BF) for pairs in CHUNKS]
    outs = pl.pallas_call(
        pack_kernel,
        in_specs=[SMEM, VMEM, VMEM],
        out_specs=[VMEM] * (2 * len(CHUNKS)),
        out_shape=[shape for shape in shapes for _ in range(2)],
        scratch_shapes=[pltpu.VMEM((2 * blk, hidden_local), FP)],
        compiler_params=pltpu.CompilerParams(vmem_limit_bytes=32 << 20),
        cost_estimate=SMALL,
    )(side, w_gate_up.reshape(experts, 2 * blk, hidden_local), w_down)
    return list(zip(outs[::2], outs[1::2]))


def unpack_kernel(side_ref, *refs):
    *ins, gate_up_ref, down_ref = refs
    blk = down_ref.shape[2]
    offset = 0
    for kept_ref, got_ref in zip(ins[::2], ins[1::2]):
        pairs = got_ref.shape[0]
        hidden_local = got_ref.shape[2] // 6
        for mine, half in ((True, side_ref[0]), (False, 1 - side_ref[0])):
            for p in range(pairs):
                packed = (kept_ref[0, p] if mine else got_ref[p]).astype(FP)
                for i in range(2):
                    expert = half * (E // 2) + 2 * (offset + p) + i
                    for part in range(2):
                        cols = slice((2 * part + i) * hidden_local, (2 * part + i + 1) * hidden_local)
                        gate_up_ref[expert, pl.ds(part, blk, stride=2), :] = packed[:, cols]
                    down_ref[expert] = packed[:, (4 + i) * hidden_local : (5 + i) * hidden_local].T
        offset += pairs


def unpack_experts(side, shards):
    blk, width = shards[0][1].shape[1:]
    hidden_local = width // 6
    operands = [array for shard in shards for array in shard]
    gate_up, down = pl.pallas_call(
        unpack_kernel,
        in_specs=[SMEM] + [VMEM] * len(operands),
        out_specs=[VMEM, VMEM],
        out_shape=[
            jax.ShapeDtypeStruct((E, 2 * blk, hidden_local), FP),
            jax.ShapeDtypeStruct((E, hidden_local, blk), FP),
        ],
        compiler_params=pltpu.CompilerParams(vmem_limit_bytes=32 << 20),
        cost_estimate=SMALL,
    )(side, *operands)
    return gate_up.reshape(E, blk, 2, hidden_local), down


def pack_attn_kernel(query_ref, key_ref, value_ref, out_ref, packed_ref):
    start = 0
    for ref in (query_ref, key_ref, value_ref):
        packed_ref[:, start : start + ref.shape[1]] = ref[...]
        start += ref.shape[1]
    packed_ref[:, start:] = out_ref[...].astype(FP).T.astype(BF)


def pack_attn(w_query, w_key, w_value, w_out):
    width = w_query.shape[1] + w_key.shape[1] + w_value.shape[1] + w_out.shape[0]
    return pl.pallas_call(
        pack_attn_kernel,
        in_specs=[VMEM] * 4,
        out_specs=VMEM,
        out_shape=jax.ShapeDtypeStruct((w_query.shape[0], width), BF),
        cost_estimate=SMALL,
    )(w_query, w_key, w_value, w_out)


def moe_kernel(first, last, start, column, side_ref, xa_ref, xb_ref, ga_ref, gb_ref, gate_ref, w_ref, *rest):
    rest = list(rest)
    sums_in = [] if first else [rest.pop(0), rest.pop(0)]
    earlier_ref = None if start else rest.pop(0)
    acc = rest.pop()
    grads_ref = rest.pop()
    sums_out = rest
    step = pl.program_id(0)
    blocks, pairs, blk, width = w_ref.shape
    model_width = blocks * blk
    half = width // 3
    hidden_local = half // 2

    def spot(block):
        place = (block // 2) * 2 + (side_ref[0] + block % 2) % 2
        return pl.ds(pl.multiple_of(place * blk, blk), blk)

    @pl.when(step == 0)
    def _():
        if start:
            acc[...] = jnp.zeros_like(acc)
        else:
            for p in range(pairs):
                for block in range(blocks):
                    acc[p, spot(block), :] = earlier_ref[block, p].astype(FP)

    x = jnp.concatenate([xa_ref[...], xb_ref[...]], axis=0)
    g = jnp.concatenate([ga_ref[...], gb_ref[...]], axis=0)
    gates = gate_ref[...].reshape(x.shape[0], gate_ref.shape[-1])
    totals = [None, None]
    for p in range(pairs):
        weights = w_ref[:, p].reshape(model_width, width)
        pre = dot_nn(x, weights[:, : 2 * half])
        out_back = dot_nn(g, weights[:, 2 * half :])
        gate = pre[:, :half]
        up = pre[:, half:]
        sig = 0.5 + 0.5 * jnp.tanh(0.5 * gate)
        share = jnp.concatenate(
            [
                jnp.broadcast_to(gates[:, i : i + 1], (x.shape[0], hidden_local))
                for i in (column + 2 * p, column + 2 * p + 1)
            ],
            axis=1,
        )
        silu = gate * sig
        hidden = (share * (silu * up)).astype(BF)
        hidden_grad = share * out_back
        gate_grad = (hidden_grad * up * (sig + silu * (1.0 - sig))).astype(BF)
        up_grad = (hidden_grad * silu).astype(BF)
        pair_grad = jnp.concatenate([gate_grad, up_grad], axis=1)
        terms = (
            dot_nt(hidden, weights[:, 2 * half :]),
            dot_nt(pair_grad, weights[:, : 2 * half]),
        )
        totals = [t if s is None else s + t for s, t in zip(totals, terms)]
        acc[p, :, : 2 * half] += dot_tn(x, pair_grad)
        acc[p, :, 2 * half :] += dot_tn(g, hidden)
    if not first:
        totals = [s[...].reshape(t.shape) + t for s, t in zip(sums_in, totals)]
    if last:
        rows = xa_ref.shape[0]
        for kept_ref, sent_ref, total in zip(sums_out[::2], sums_out[1::2], totals):
            kept_ref[...] = total[:rows]
            sent_ref[...] = total[rows:].astype(BF)
    else:
        for out_ref, total in zip(sums_out, totals):
            out_ref[...] = total.reshape(out_ref.shape)

    @pl.when(step == pl.num_programs(0) - 1)
    def _():
        for p in range(pairs):
            for block in range(blocks):
                grads_ref[block, p] = acc[p, spot(block), :].astype(BF)


def moe_chunk(side, rows_in, gates, weights, sums, earlier, micro, column, last):
    count, rows, model_width = rows_in[0].shape
    count //= 2
    blocks, pairs, blk, width = weights.shape
    once = pl.Buffered(1)
    tile = min(128, rows)
    parts = rows // tile
    row = pl.BlockSpec((None, 2, tile, model_width), lambda i: (i // parts, 0, i % parts, 0))
    half = pl.BlockSpec((None, tile, model_width), lambda i: (i // parts, i % parts, 0))
    g_half = pl.BlockSpec((None, tile, model_width), lambda i: (count + i // parts, i % parts, 0))
    gate_spec = pl.BlockSpec(
        (None, None, 2, tile, gates.shape[-1]), lambda i: (micro, i // parts, 0, i % parts, 0)
    )
    whole = pl.BlockSpec(weights.shape, lambda i: (0, 0, 0, 0), pipeline_mode=once)
    first, start = sums is None, earlier is None
    operands = [side, *rows_in, *rows_in, gates, weights] + ([] if first else list(sums))
    operands += [] if start else [earlier]
    if last:
        out_specs = [half] * 4
        outs = [jax.ShapeDtypeStruct((count, rows, model_width), t) for t in (FP, BF, FP, BF)]
    else:
        out_specs = [row] * 2
        outs = [jax.ShapeDtypeStruct((count, 2, rows, model_width), FP)] * 2
    *sums, grads = pl.pallas_call(
        functools.partial(moe_kernel, first, last, start, column),
        grid=(count * parts,),
        in_specs=[SMEM, half, half, g_half, g_half, gate_spec, whole]
        + ([] if first else [row, row])
        + ([] if start else [whole]),
        out_specs=out_specs + [whole],
        scratch_shapes=[pltpu.VMEM((pairs, model_width, width), FP)],
        out_shape=outs + [jax.ShapeDtypeStruct(weights.shape, BF)],
        input_output_aliases={} if first or last else {7: 0, 8: 1},
        compiler_params=pltpu.CompilerParams(vmem_limit_bytes=60 << 20),
        cost_estimate=cost(6 << 30),
    )(*operands)
    return sums, grads


def place_rows(spots_ref, pieces, whole_ref):
    rows = pieces[0].shape[0]
    for i, piece in enumerate(pieces):
        whole_ref[pl.ds(pl.multiple_of(spots_ref[i] * rows, rows), rows), :] = piece[...]


def product_rows(spots_ref, left_ref, right, kept_ref, sent_ref):
    rows = kept_ref.shape[1]
    for i in range(4):
        here = pl.ds(pl.multiple_of(spots_ref[i] * rows, rows), rows)
        value = dot_nt(left_ref[here, :], right)
        if i < 2:
            kept_ref[i] = value
        else:
            sent_ref[i - 2] = value.astype(BF)


def attn_forward_kernel(widths, n_weights, spots_ref, weight_spots_ref, *rest):
    q_width, kv_width = widths
    x_pieces, rest = rest[:4], rest[4:]
    w_pieces, rest = rest[:n_weights], rest[n_weights:]
    if n_weights > 1:
        qkv_ref, heads_ref, kept_ref, sent_ref, w_ref, x_scr = rest
        place_rows(weight_spots_ref, w_pieces, w_ref)
    else:
        qkv_ref, heads_ref, kept_ref, sent_ref, x_scr = rest
        w_ref = w_pieces[0]
    place_rows(spots_ref, x_pieces, x_scr)
    rows = x_scr.shape[0]
    proj_width = q_width + 2 * kv_width
    ratio = q_width // kv_width
    tile = min(256, rows)
    qkv_ref[...] = dot_nn(x_scr[...], w_ref[:, :proj_width]).astype(BF)
    for kv in range(kv_width // HD):
        keys = qkv_ref[:, q_width + kv * HD : q_width + (kv + 1) * HD]
        values = qkv_ref[:, q_width + kv_width + kv * HD : q_width + kv_width + (kv + 1) * HD]
        cols = [slice((kv * ratio + r) * HD, (kv * ratio + r + 1) * HD) for r in range(ratio)]
        for start in range(0, rows, tile):
            stop = start + tile
            query = jnp.concatenate([qkv_ref[start:stop, c] for c in cols], axis=0) * BF(HD**-0.5)
            near = dot_nt(query, keys[start:stop])
            row_pos = lax.broadcasted_iota(jnp.int32, near.shape, 0) & (tile - 1)
            col_pos = lax.broadcasted_iota(jnp.int32, near.shape, 1)
            scores = jnp.where(col_pos <= row_pos, near, -1e30)
            if start:
                scores = jnp.concatenate([dot_nt(query, keys[:start]), scores], axis=1)
            exponent = jnp.exp(scores - jnp.max(scores, axis=-1, keepdims=True))
            total = jnp.sum(exponent, axis=-1, keepdims=True)
            probs = (exponent * (1.0 / total)).astype(BF)
            out = dot_nn(probs, values[:stop]).astype(BF)
            for r, c in enumerate(cols):
                heads_ref[start:stop, c] = out[r * tile : (r + 1) * tile]
    product_rows(spots_ref, heads_ref, w_ref[:, proj_width:], kept_ref, sent_ref)


def attn_backward_kernel(widths, first, spots_ref, block_spots_ref, *rest):
    q_width, kv_width = widths
    proj_width = q_width + 2 * kv_width
    dy_pieces, x_pieces, rest = rest[:4], rest[4:8], list(rest[8:])
    qkv_ref, heads_ref, w_ref = rest[:3]
    rest = rest[3:]
    if first:
        grads_ref, kept_ref, sent_ref = rest[:3]
        rest = rest[3:]
    else:
        earlier_ref, grads_kept_ref, grads_sent_ref, kept_ref, sent_ref = rest[:5]
        grads_ref = rest[5]
        rest = rest[6:]
    dy_scr, x_scr, head_grad_ref, proj_grad_ref, key_acc, value_acc = rest
    place_rows(spots_ref, dy_pieces, dy_scr)
    place_rows(spots_ref, x_pieces, x_scr)
    rows = x_scr.shape[0]
    ratio = q_width // kv_width
    tile = min(256, rows)
    head_grad_ref[...] = dot_nn(dy_scr[...], w_ref[:, proj_width:]).astype(BF)
    for kv in range(kv_width // HD):
        key_cols = slice(q_width + kv * HD, q_width + (kv + 1) * HD)
        value_cols = slice(q_width + kv_width + kv * HD, q_width + kv_width + (kv + 1) * HD)
        cols = [slice((kv * ratio + r) * HD, (kv * ratio + r + 1) * HD) for r in range(ratio)]
        keys = qkv_ref[:, key_cols]
        values = qkv_ref[:, value_cols]
        key_acc[...] = jnp.zeros_like(key_acc)
        value_acc[...] = jnp.zeros_like(value_acc)
        for start in range(0, rows, tile):
            stop = start + tile
            query = jnp.concatenate([qkv_ref[start:stop, c] for c in cols], axis=0) * BF(HD**-0.5)
            out_grad = jnp.concatenate([head_grad_ref[start:stop, c] for c in cols], axis=0)
            near = dot_nt(keys[start:stop], query)
            key_pos = lax.broadcasted_iota(jnp.int32, near.shape, 0)
            row_pos = lax.broadcasted_iota(jnp.int32, near.shape, 1) & (tile - 1)
            scores = jnp.where(key_pos <= row_pos, near, -1e30)
            if start:
                scores = jnp.concatenate([dot_nt(keys[:start], query), scores], axis=0)
            exponent = jnp.exp(scores - jnp.max(scores, axis=0, keepdims=True))
            probs = exponent * (1.0 / jnp.sum(exponent, axis=0, keepdims=True))
            prob_grad = dot_nt(values[:stop], out_grad)
            inner = jnp.sum(probs * prob_grad, axis=0, keepdims=True)
            score_grad = (probs * (prob_grad - inner)).astype(BF)
            value_acc[:stop] += dot_nn(probs.astype(BF), out_grad)
            key_acc[:stop] += dot_nn(score_grad, query)
            query_grad = (dot_tn(score_grad, keys[:stop]) * (HD**-0.5)).astype(BF)
            for r, c in enumerate(cols):
                proj_grad_ref[start:stop, c] = query_grad[r * tile : (r + 1) * tile]
        proj_grad_ref[:, key_cols] = key_acc[...].astype(BF)
        proj_grad_ref[:, value_cols] = value_acc[...].astype(BF)
    product_rows(spots_ref, proj_grad_ref, w_ref[:, :proj_width], kept_ref, sent_ref)
    proj_part = dot_tn(x_scr[...], proj_grad_ref[...])
    out_part = dot_tn(dy_scr[...], heads_ref[...])
    if first:
        grads_ref[:, :proj_width] = proj_part
        grads_ref[:, proj_width:] = out_part
    else:
        grads_ref[:, :proj_width] = earlier_ref[:, :proj_width] + proj_part
        grads_ref[:, proj_width:] = earlier_ref[:, proj_width:] + out_part
        depth, blk, _ = grads_kept_ref.shape
        for r in range(depth):
            here = pl.ds(pl.multiple_of(block_spots_ref[r] * blk, blk), blk)
            grads_kept_ref[r] = grads_ref[here, :]
            here = pl.ds(pl.multiple_of(block_spots_ref[depth + r] * blk, blk), blk)
            grads_sent_ref[r] = grads_ref[here, :].astype(BF)


def attn_forward(spots, weight_spots, pieces, weights, widths):
    rows, model_width = pieces[0].shape
    width = weights[0].shape[1]
    whole = len(weights) == 1
    outs = [
        jax.ShapeDtypeStruct((4 * rows, widths[0] + 2 * widths[1]), BF),
        jax.ShapeDtypeStruct((4 * rows, widths[0]), BF),
        jax.ShapeDtypeStruct((2, rows, model_width), FP),
        jax.ShapeDtypeStruct((2, rows, model_width), BF),
    ] + ([] if whole else [jax.ShapeDtypeStruct((model_width, width), BF)])
    results = pl.pallas_call(
        functools.partial(attn_forward_kernel, widths, len(weights)),
        in_specs=[SMEM] * 2 + [VMEM] * (4 + len(weights)),
        out_specs=[VMEM] * len(outs),
        out_shape=outs,
        scratch_shapes=[pltpu.VMEM((4 * rows, model_width), BF)],
        compiler_params=pltpu.CompilerParams(vmem_limit_bytes=56 << 20),
        cost_estimate=cost(14 << 30),
    )(spots, weight_spots, *pieces, *weights)
    return results if not whole else [*results, weights[0]]


def attn_backward(spots, block_spots, dy, x, qkv, heads, weights, earlier, widths):
    rows, model_width = x[0].shape
    width = weights.shape[1]
    first = earlier is None
    operands = [*dy, *x, qkv, heads, weights] + ([] if first else [earlier])
    depth = block_spots.shape[0] // 2
    whole = (model_width, width)
    blocks = (depth, model_width // depth // 2, width)
    scratch = [
        pltpu.VMEM((4 * rows, model_width), BF),
        pltpu.VMEM((4 * rows, model_width), BF),
        pltpu.VMEM(heads.shape, BF),
        pltpu.VMEM(qkv.shape, BF),
        pltpu.VMEM((4 * rows, HD), FP),
        pltpu.VMEM((4 * rows, HD), FP),
    ]
    if first:
        outs = [jax.ShapeDtypeStruct(whole, FP)]
    else:
        outs = [jax.ShapeDtypeStruct(blocks, FP), jax.ShapeDtypeStruct(blocks, BF)]
        scratch = [pltpu.VMEM(whole, FP)] + scratch
    outs += [jax.ShapeDtypeStruct((2, rows, model_width), t) for t in (FP, BF)]
    return pl.pallas_call(
        functools.partial(attn_backward_kernel, widths, first),
        in_specs=[SMEM] * 2 + [VMEM] * len(operands),
        out_specs=[VMEM] * len(outs),
        out_shape=outs,
        scratch_shapes=scratch,
        compiler_params=pltpu.CompilerParams(vmem_limit_bytes=58 << 20),
        cost_estimate=cost(24 << 30),
    )(spots, block_spots, *operands)


def on_device(
    block_input,
    cotangent,
    routes,
    gate_weights,
    w_query,
    w_key,
    w_value,
    w_out,
    w_gate_up,
    w_down,
    norm_attn,
    norm_moe,
):
    depth = lax.axis_size("z")
    micro_count, rows_local, model_width = block_input.shape
    q_width, kv_width = w_query.shape[1], w_key.shape[1]
    widths = (q_width, kv_width)
    proj_width = q_width + 2 * kv_width
    side, chip, core = lax.axis_index("y"), lax.axis_index("x"), lax.axis_index("c")
    side_at = side.astype(jnp.int32).reshape(1)
    spots = jnp.stack([2 * x + c for c in (core, 1 - core) for x in (chip, 1 - chip)])
    spots = spots.astype(jnp.int32)
    place = lax.axis_index("z")
    block_spots = jnp.stack(
        [2 * lax.rem(place + r, depth) + s for s in (side, 1 - side) for r in range(depth)]
    ).astype(jnp.int32)

    packed_attn = pack_attn(w_query, w_key, w_value, w_out)
    packed = pack_experts(after(side_at, packed_attn), w_gate_up, w_down)
    in_rows = block_input.astype(FP)
    normed_attn, scale_attn = row_norm(in_rows, norm_attn)
    normed = [normed_attn[m].astype(BF) for m in range(micro_count)]
    cots = [cotangent[m] for m in range(micro_count)]

    def shard_of(chunk, got):
        mine = packed[chunk][0]
        first = side == 0
        return jnp.stack([jnp.where(first, mine, got), jnp.where(first, got, mine)])

    def whole_of(shard):
        whole = lax.all_gather(shard, "z", axis=0)
        return whole.reshape(-1, *whole.shape[2:])

    column, places = along_z(packed_attn, depth)
    weight_spots = jnp.stack([2 * z + s for s in (side, 1 - side) for z in places])
    weight_spots = weight_spots.astype(jnp.int32)
    across = swap(normed[0], "x")
    got = swap(packed[0][1], "y")
    own_across = swap(packed_attn, "y")
    *column, across, next_normed = together(*column, across, normed[1])

    weights = column + [own_across] + [swap(piece, "y") for piece in column[1:]]
    near_rows, far_rows = swap(normed[0], "c"), swap(across, "c")
    next_across = swap(next_normed, "x")
    *weights, near_rows, far_rows, got, cot, next_across = together(
        *weights, near_rows, far_rows, got, cots[0], next_across
    )
    attn_in = [[normed[0], across, near_rows, far_rows]]
    shards = [shard_of(0, got)]
    chunk_weights = [whole_of(shards[0])]

    cot_near, cot_across = swap(cot, "y"), swap(cot, "x")
    turn = after(spots, shards[0])
    qkv, heads, kept, sent, whole = attn_forward(turn, weight_spots, attn_in[0], weights, widths)
    weights = [whole]
    saved = [(qkv, heads)]
    sent, cot_near, cot_across, across = together(sent, cot_near, cot_across, next_across)

    got = swap(sent, "c")
    near_rows, far_rows = swap(normed[1], "c"), swap(across, "c")
    along = plus(kept[1], got[1]).astype(BF)
    own = plus(kept[0], got[0])
    along, near_rows, far_rows, theirs, turn = together(
        along, near_rows, far_rows, packed[1][1], spots
    )
    attn_in.append([normed[1], across, near_rows, far_rows])

    came = swap(along, "x")
    theirs = swap(theirs, "y")
    qkv, heads, kept, sent, _ = attn_forward(turn, weight_spots, attn_in[1], weights, widths)
    saved.append((qkv, heads))
    sent, came = together(sent, came)

    def moe_rows(middle):
        normed, scale = row_norm(middle, norm_moe)
        return normed.astype(BF), scale

    got = swap(sent, "c")
    middle = [in_rows[0] + plus(own, came)]
    low, scale = moe_rows(middle[0])
    normed, scale_moe = [low], [scale]
    along = plus(kept[1], got[1]).astype(BF)
    own = plus(kept[0], got[0])
    along, low, cot = together(along, low, cots[0])

    came = swap(along, "x")
    near, across = swap(low, "y"), swap(low, "x")
    expert_ids = jnp.arange(E, dtype=jnp.int32)[:, None, None, None]
    gates = jnp.sum(jnp.where(routes == expert_ids, gate_weights, 0.0), axis=3)
    gates = gates.reshape(2, E // 2, micro_count, 2, 2, rows_local)
    gates = jnp.where(chip == 0, gates, gates[:, :, :, ::-1])
    gates = jnp.where(core == 0, gates, gates[:, :, :, :, ::-1])
    mine = lax.dynamic_index_in_dim(gates, side, 0, False)
    other = lax.dynamic_index_in_dim(gates, 1 - side, 0, False)
    gates = jnp.stack([mine, swap(other.reshape(E // 2, -1), "y").reshape(mine.shape)])
    gates = gates.transpose(2, 3, 0, 4, 5, 1).reshape(micro_count, 4, 2, rows_local, E // 2)
    came, near, across, gates, theirs, low, cot = together(
        came, near, across, gates, theirs, low, cot
    )

    diagonal, cot_diagonal = cross(low), cross(cot)
    shards.append(shard_of(1, theirs))
    chunk_weights.append(whole_of(shards[1]))
    middle.append(in_rows[1] + plus(own, came))
    low, scale = moe_rows(middle[1])
    normed.append(low)
    scale_moe.append(scale)
    diagonal, cot_diagonal, low, cot = together(diagonal, cot_diagonal, low, cots[1])
    blocks = jnp.stack(
        [normed[0], near, across, diagonal, cots[0], cot_near, cot_across, cot_diagonal]
    )
    experts_in = [(blocks, swap(blocks, "c"))]
    neighbours = [f(v) for v in (low, cot) for f in (lambda r: swap(r, "y"), lambda r: swap(r, "x"), cross)]

    sums = [None] * micro_count
    turn = after(side_at, shards[1])
    all_grads = []
    back = []
    first_expert = 0
    for chunk, pairs in enumerate(CHUNKS):
        last = chunk == len(CHUNKS) - 1
        grads = None
        for m in range(micro_count):
            sums[m], grads = moe_chunk(
                turn,
                experts_in[m],
                gates,
                chunk_weights[chunk],
                sums[m],
                grads,
                m,
                first_expert,
                last,
            )
            waited = [grads]
            if m == 0 and chunk == 0:
                *neighbours, _ = together(*neighbours, grads)
                blocks = jnp.stack([low, *neighbours[:3], cot, *neighbours[3:]])
                experts_in.append((blocks, swap(blocks, "c")))
            if m == 0 and last:
                back.append(scatter_pair(*sums[m][2:]))
                waited += back[0][1]
            turn = after(side_at, *waited)
        first_expert += 2 * pairs
        all_grads.append(grads.reshape(depth, 2, *grads.shape[1:]))

    def reduce_grads(grads):
        return lax.psum_scatter(grads, "z", scatter_dimension=0, tiled=False)

    grad_shards = [reduce_grads(all_grads[0])]

    out_grad = cotangent.astype(FP)
    input_grads = []
    gains = [0.0, 0.0]
    middle_grad, branch_grad, outputs = [], [], []
    results = None
    turn = spots
    ends = grads
    for m in range(micro_count):
        if m:
            kept, sent = sums[m][2:]
            back.append(scatter_pair(kept, after(sent, middle_low)))
            ends = results[0]
        own, _, came = back[m]
        *came, _ = together(*came, ends)
        moe_in_grad = sum_of(own, came)
        middle_back, gain_moe = norm_back(middle[m], scale_moe[m], norm_moe, moe_in_grad)
        middle_grad.append(out_grad[m] + middle_back)
        middle_low = middle_grad[m].astype(BF)
        if m == 0:
            grads, _ = together(all_grads[1], grad_shards[0])
            grad_shards.append(reduce_grads(grads))
        across = swap(middle_low, "x")
        branch_grad.append([middle_low, across, swap(middle_low, "c"), swap(across, "c")])
        gains[1] = gains[1] + gain_moe
        results = attn_backward(
            turn,
            block_spots,
            branch_grad[m],
            attn_in[m],
            *saved[m],
            weights[0],
            None if results is None else results[0],
            widths,
        )
        kept, sent = results[-2:]
        got = swap(sent, "c")
        along = plus(kept[1], got[1]).astype(BF)
        attn_in_grad = sum_of(plus(kept[0], got[0]), [swap(along, "x")])
        turn = after(spots, along)
        in_back, gain_attn = norm_back(in_rows[m], scale_attn[m], norm_attn, attn_in_grad)
        input_grads.append(middle_grad[m] + in_back)
        gains[0] = gains[0] + gain_attn
    for m in range(micro_count):
        kept, sent = sums[m][:2]
        own, _, came = scatter_pair(kept, after(sent, along if m else branch_grad[-1][1]))
        outputs.append((middle[m] + sum_of(own, came)).astype(BF))
    shard_pair, shard_down = unpack_experts(side_at, [(g, swap(g[1], "y")) for g in grad_shards])
    attn_shard = scatter_dp(results[0], results[1], depth)
    gains = sum_all(jnp.concatenate(gains).reshape(16, -1), depth).reshape(2, model_width)
    return (
        jnp.stack(outputs),
        jnp.stack(input_grads),
        attn_shard[:, :q_width],
        attn_shard[:, q_width : q_width + kv_width],
        attn_shard[:, q_width + kv_width : proj_width],
        attn_shard[:, proj_width:].T,
        shard_pair,
        shard_down,
        gains[0],
        gains[1],
    )


def solution(mesh):
    dp, tensor = mesh.shape["dp"], mesh.shape["tensor"]
    fine = Mesh(mesh.devices.reshape(dp // 2, 2, tensor // 2, 2), ("z", "y", "x", "c"))
    dp_axes, tensor_axes = ("z", "y"), ("x", "c")
    rows = P(None, dp_axes + tensor_axes, None)
    return jax.shard_map(
        on_device,
        mesh=fine,
        in_specs=(
            rows,
            rows,
            P(None, dp_axes, None),
            P(None, dp_axes, None),
            P(dp_axes, tensor_axes),
            P(dp_axes, tensor_axes),
            P(dp_axes, tensor_axes),
            P(tensor_axes, dp_axes),
            P(None, dp_axes, None, tensor_axes),
            P(None, tensor_axes, dp_axes),
            P(),
            P(),
        ),
        out_specs=(
            rows,
            rows,
            P(dp_axes, tensor_axes),
            P(dp_axes, tensor_axes),
            P(dp_axes, tensor_axes),
            P(tensor_axes, dp_axes),
            P(None, dp_axes, None, tensor_axes),
            P(None, tensor_axes, dp_axes),
            P(),
            P(),
        ),
        check_vma=False,
    )
```

```python
import functools

import jax
import jax.numpy as jnp
from jax import lax
from jax.experimental import pallas as pl
from jax.experimental.pallas import tpu as pltpu
from jax.sharding import Mesh
from jax.sharding import PartitionSpec as P

HD = 64
E = 32
CHUNKS = (4, 4)

EPSILON = 1e-06
BF = jnp.bfloat16
FP = jnp.float32


def dot_nn(left, right):
    return lax.dot_general(left, right, (((1,), (0,)), ((), ())), preferred_element_type=FP)


def dot_tn(left, right):
    return lax.dot_general(left, right, (((0,), (0,)), ((), ())), preferred_element_type=FP)


def dot_nt(left, right):
    return lax.dot_general(left, right, (((1,), (1,)), ((), ())), preferred_element_type=FP)


def row_norm(in_rows, gain_vec):
    row_scale = lax.rsqrt(jnp.mean(in_rows * in_rows, axis=-1, keepdims=True) + EPSILON)
    return (in_rows * row_scale * gain_vec, row_scale)


def norm_back(in_rows, row_scale, gain_vec, grad_in):
    weighted = grad_in * gain_vec
    inner = jnp.mean(weighted * in_rows, axis=-1, keepdims=True)
    return row_scale * weighted - in_rows * row_scale * row_scale * row_scale * inner


def swap(value, axis):
    return lax.ppermute(value, axis, [(0, 1), (1, 0)])


def after(value, *earlier):
    return lax.optimization_barrier((value, *earlier))[0]


def together(*values):
    return lax.optimization_barrier(values)


def cross(value):
    return lax.ppermute(value, ("y", "x"), [(i, 3 - i) for i in range(4)])


def to_neighbours(rows):
    return [swap(rows[0], "y"), swap(rows[1], "x"), cross(rows[2])]


def plus(left, right):
    return left + right.astype(FP)


def half_sums(kept, sent):
    got = swap(sent, "c")
    low = [plus(kept[i], got[i]).astype(BF) for i in range(1, kept.shape[0])]
    return plus(kept[0], got[0]), low


def sum_of(total, parts):
    for part in parts:
        total = plus(total, part)
    return total


def along_z(shard, depth):
    place = lax.axis_index("z")
    turns_taken = [k for k in range(-((depth - 1) // 2), depth // 2 + 1) if k]
    pieces = [shard]
    for k in turns_taken:
        pieces.append(lax.ppermute(shard, "z", [(i, (i + k) % depth) for i in range(depth)]))
    return pieces, [lax.rem(place + depth - k, depth) for k in [0, *turns_taken]]


def along_z_sent(column, depth):
    return [
        lax.ppermute(column[r].astype(BF), "z", [(i, (i + r) % depth) for i in range(depth)])
        for r in range(1, depth)
    ]


def sum_over_z(value, depth):
    reach = 1
    while reach < depth:
        pairs = [(i, i ^ reach) for i in range(depth)]
        value = value + lax.ppermute(value, "z", pairs)
        reach *= 2
    return value


def cost(flops):
    return pl.CostEstimate(flops=flops, bytes_accessed=1 << 20, transcendentals=0)


SMALL = cost(1 << 30)
SMEM = pl.BlockSpec(memory_space=pltpu.SMEM)
VMEM = pl.BlockSpec(memory_space=pltpu.VMEM)


def stack_kernel(*refs):
    *ins, out_ref, sems = refs
    copies = [pltpu.make_async_copy(ref, out_ref.at[i], sems.at[i]) for i, ref in enumerate(ins)]
    for copy in copies:
        copy.start()
    for copy in copies:
        copy.wait()


def stacked(arrays):
    return pl.pallas_call(
        stack_kernel,
        in_specs=[pl.BlockSpec(memory_space=pl.ANY)] * len(arrays),
        out_specs=VMEM,
        out_shape=jax.ShapeDtypeStruct((len(arrays), *arrays[0].shape), arrays[0].dtype),
        scratch_shapes=[pltpu.SemaphoreType.DMA((len(arrays),))],
        compiler_params=pltpu.CompilerParams(vmem_limit_bytes=32 << 20),
        cost_estimate=cost(1 << 30),
    )(*arrays)


def pack_kernel(side_ref, gate_up_ref, down_ref, *rest):
    *outs, rows_scr = rest
    blk = down_ref.shape[2]
    offset = 0
    for mine_ref, theirs_ref in zip(outs[::2], outs[1::2]):
        pairs = mine_ref.shape[0]
        hidden_local = mine_ref.shape[2] // 6
        for out_ref, half in ((theirs_ref, 1 - side_ref[0]), (mine_ref, side_ref[0])):
            for p in range(pairs):
                for i in range(2):
                    expert = half * (E // 2) + 2 * (offset + p) + i
                    rows_scr[...] = gate_up_ref[expert].astype(FP)
                    for part in range(2):
                        cols = slice((2 * part + i) * hidden_local, (2 * part + i + 1) * hidden_local)
                        out_ref[p, :, cols] = rows_scr[pl.ds(part, blk, stride=2), :].astype(BF)
                    cols = slice((4 + i) * hidden_local, (5 + i) * hidden_local)
                    out_ref[p, :, cols] = down_ref[expert].astype(FP).T.astype(BF)
        offset += pairs


def pack_experts(side, w_gate_up, w_down):
    experts, blk, _, hidden_local = w_gate_up.shape
    shapes = [jax.ShapeDtypeStruct((pairs, blk, 6 * hidden_local), BF) for pairs in CHUNKS]
    outs = pl.pallas_call(
        pack_kernel,
        in_specs=[SMEM, VMEM, VMEM],
        out_specs=[VMEM] * (2 * len(CHUNKS)),
        out_shape=[shape for shape in shapes for _ in range(2)],
        scratch_shapes=[pltpu.VMEM((2 * blk, hidden_local), FP)],
        compiler_params=pltpu.CompilerParams(vmem_limit_bytes=32 << 20),
        cost_estimate=SMALL,
    )(side, w_gate_up.reshape(experts, 2 * blk, hidden_local), w_down)
    return list(zip(outs[::2], outs[1::2]))


def unpack_kernel(side_ref, *refs):
    *ins, gate_up_ref, down_ref = refs
    blk = down_ref.shape[2]
    offset = 0
    for kept_ref, got_ref in zip(ins[::2], ins[1::2]):
        pairs = got_ref.shape[0]
        hidden_local = got_ref.shape[2] // 6
        for mine, half in ((True, side_ref[0]), (False, 1 - side_ref[0])):
            for p in range(pairs):
                packed = (kept_ref[0, p] if mine else got_ref[p]).astype(FP)
                for i in range(2):
                    expert = half * (E // 2) + 2 * (offset + p) + i
                    for part in range(2):
                        cols = slice((2 * part + i) * hidden_local, (2 * part + i + 1) * hidden_local)
                        gate_up_ref[expert, pl.ds(part, blk, stride=2), :] = packed[:, cols]
                    down_ref[expert] = packed[:, (4 + i) * hidden_local : (5 + i) * hidden_local].T
        offset += pairs


def unpack_experts(side, shards):
    blk, width = shards[0][1].shape[1:]
    hidden_local = width // 6
    operands = [array for shard in shards for array in shard]
    gate_up, down = pl.pallas_call(
        unpack_kernel,
        in_specs=[SMEM] + [VMEM] * len(operands),
        out_specs=[VMEM, VMEM],
        out_shape=[
            jax.ShapeDtypeStruct((E, 2 * blk, hidden_local), FP),
            jax.ShapeDtypeStruct((E, hidden_local, blk), FP),
        ],
        compiler_params=pltpu.CompilerParams(vmem_limit_bytes=32 << 20),
        cost_estimate=SMALL,
    )(side, *operands)
    return gate_up.reshape(E, blk, 2, hidden_local), down


def pack_attn_kernel(query_ref, key_ref, value_ref, out_ref, packed_ref):
    start = 0
    for ref in (query_ref, key_ref, value_ref):
        packed_ref[:, start : start + ref.shape[1]] = ref[...]
        start += ref.shape[1]
    packed_ref[:, start:] = out_ref[...].astype(FP).T.astype(BF)


def pack_attn(w_query, w_key, w_value, w_out):
    width = w_query.shape[1] + w_key.shape[1] + w_value.shape[1] + w_out.shape[0]
    return pl.pallas_call(
        pack_attn_kernel,
        in_specs=[VMEM] * 4,
        out_specs=VMEM,
        out_shape=jax.ShapeDtypeStruct((w_query.shape[0], width), BF),
        cost_estimate=SMALL,
    )(w_query, w_key, w_value, w_out)


def moe_kernel(first, last, start, column, side_ref, xa_ref, xb_ref, ga_ref, gb_ref, gate_ref, w_ref, *rest):
    rest = list(rest)
    sums_in = [] if first else [rest.pop(0), rest.pop(0)]
    earlier_ref = None if start else rest.pop(0)
    acc = rest.pop()
    grads_ref = rest.pop()
    sums_out = rest
    step = pl.program_id(0)
    blocks, pairs, blk, width = w_ref.shape
    model_width = blocks * blk
    half = width // 3
    hidden_local = half // 2

    def spot(block):
        place = (block // 2) * 2 + (side_ref[0] + block % 2) % 2
        return pl.ds(pl.multiple_of(place * blk, blk), blk)

    @pl.when(step == 0)
    def _():
        if start:
            acc[...] = jnp.zeros_like(acc)
        else:
            for p in range(pairs):
                for block in range(blocks):
                    acc[p, spot(block), :] = earlier_ref[block, p].astype(FP)

    x = jnp.concatenate([xa_ref[...], xb_ref[...]], axis=0)
    g = jnp.concatenate([ga_ref[...], gb_ref[...]], axis=0)
    gates = gate_ref[...].reshape(x.shape[0], gate_ref.shape[-1])
    totals = [None, None]
    for p in range(pairs):
        weights = w_ref[:, p].reshape(model_width, width)
        pre = dot_nn(x, weights[:, : 2 * half])
        out_back = dot_nn(g, weights[:, 2 * half :])
        gate = pre[:, :half]
        up = pre[:, half:]
        sig = 0.5 + 0.5 * jnp.tanh(0.5 * gate)
        share = jnp.concatenate(
            [
                jnp.broadcast_to(gates[:, i : i + 1], (x.shape[0], hidden_local))
                for i in (column + 2 * p, column + 2 * p + 1)
            ],
            axis=1,
        )
        silu = gate * sig
        hidden = (share * (silu * up)).astype(BF)
        hidden_grad = share * out_back
        gate_grad = (hidden_grad * up * (sig + silu * (1.0 - sig))).astype(BF)
        up_grad = (hidden_grad * silu).astype(BF)
        pair_grad = jnp.concatenate([gate_grad, up_grad], axis=1)
        terms = (
            dot_nt(hidden, weights[:, 2 * half :]),
            dot_nt(pair_grad, weights[:, : 2 * half]),
        )
        totals = [t if s is None else s + t for s, t in zip(totals, terms)]
        acc[p, :, : 2 * half] += dot_tn(x, pair_grad)
        acc[p, :, 2 * half :] += dot_tn(g, hidden)
    if not first:
        totals = [s[...].reshape(t.shape) + t for s, t in zip(sums_in, totals)]
    if last:
        rows = xa_ref.shape[0]
        for kept_ref, sent_ref, total in zip(sums_out[::2], sums_out[1::2], totals):
            kept_ref[...] = total[:rows]
            sent_ref[...] = total[rows:].astype(BF)
    else:
        for out_ref, total in zip(sums_out, totals):
            out_ref[...] = total.reshape(out_ref.shape)

    @pl.when(step == pl.num_programs(0) - 1)
    def _():
        for p in range(pairs):
            for block in range(blocks):
                grads_ref[block, p] = acc[p, spot(block), :].astype(BF)


def moe_chunk(side, rows_in, gates, weights, sums, earlier, micro, column, last):
    count, rows, model_width = rows_in[0].shape
    count //= 2
    blocks, pairs, blk, width = weights.shape
    once = pl.Buffered(1)
    tile = min(128, rows)
    parts = rows // tile
    row = pl.BlockSpec((None, 2, tile, model_width), lambda i: (i // parts, 0, i % parts, 0))
    half = pl.BlockSpec((None, tile, model_width), lambda i: (i // parts, i % parts, 0))
    x_half = pl.BlockSpec((None, tile, model_width), lambda i: (2 * (i // parts), i % parts, 0))
    g_half = pl.BlockSpec((None, tile, model_width), lambda i: (2 * (i // parts) + 1, i % parts, 0))
    gate_spec = pl.BlockSpec(
        (None, None, 2, tile, gates.shape[-1]), lambda i: (micro, i // parts, 0, i % parts, 0)
    )
    whole = pl.BlockSpec(weights.shape, lambda i: (0, 0, 0, 0), pipeline_mode=once)
    first, start = sums is None, earlier is None
    operands = [side, *rows_in, *rows_in, gates, weights] + ([] if first else list(sums))
    operands += [] if start else [earlier]
    if last:
        out_specs = [half] * 4
        outs = [jax.ShapeDtypeStruct((count, rows, model_width), t) for t in (FP, BF, FP, BF)]
    else:
        out_specs = [row] * 2
        outs = [jax.ShapeDtypeStruct((count, 2, rows, model_width), FP)] * 2
    *sums, grads = pl.pallas_call(
        functools.partial(moe_kernel, first, last, start, column),
        grid=(count * parts,),
        in_specs=[SMEM, x_half, x_half, g_half, g_half, gate_spec, whole]
        + ([] if first else [row, row])
        + ([] if start else [whole]),
        out_specs=out_specs + [whole],
        scratch_shapes=[pltpu.VMEM((pairs, model_width, width), FP)],
        out_shape=outs + [jax.ShapeDtypeStruct(weights.shape, BF)],
        input_output_aliases={} if first or last else {7: 0, 8: 1},
        compiler_params=pltpu.CompilerParams(vmem_limit_bytes=60 << 20),
        cost_estimate=cost(6 << 30),
    )(*operands)
    return sums, grads


def place_rows(spots_ref, pieces, whole_ref):
    rows = pieces[0].shape[0]
    for i, piece in enumerate(pieces):
        whole_ref[pl.ds(pl.multiple_of(spots_ref[i] * rows, rows), rows), :] = piece[...]


def product_rows(spots_ref, left_ref, right, kept_ref, sent_ref, x_ref=None, gain_ref=None):
    rows = kept_ref.shape[1]
    gain = 0.0
    for i in range(4):
        here = pl.ds(pl.multiple_of(spots_ref[i] * rows, rows), rows)
        value = dot_nt(left_ref[here, :], right)
        if i < 2:
            kept_ref[i] = value
        else:
            sent_ref[i - 2] = value.astype(BF)
        if x_ref is not None:
            gain += jnp.sum(value * x_ref[here, :].astype(FP), axis=0, keepdims=True)
    if x_ref is not None:
        gain_ref[...] = gain


def attn_forward_kernel(widths, n_weights, spots_ref, weight_spots_ref, *rest):
    q_width, kv_width = widths
    x_pieces, rest = rest[:4], rest[4:]
    w_pieces, rest = rest[:n_weights], rest[n_weights:]
    if n_weights > 1:
        qkv_ref, heads_ref, kept_ref, sent_ref, w_ref, x_scr = rest
        place_rows(weight_spots_ref, w_pieces, w_ref)
    else:
        qkv_ref, heads_ref, kept_ref, sent_ref, x_scr = rest
        w_ref = w_pieces[0]
    place_rows(spots_ref, x_pieces, x_scr)
    rows = x_scr.shape[0]
    proj_width = q_width + 2 * kv_width
    ratio = q_width // kv_width
    tile = min(256, rows)
    qkv_ref[...] = dot_nn(x_scr[...], w_ref[:, :proj_width]).astype(BF)
    for kv in range(kv_width // HD):
        keys = qkv_ref[:, q_width + kv * HD : q_width + (kv + 1) * HD]
        values = qkv_ref[:, q_width + kv_width + kv * HD : q_width + kv_width + (kv + 1) * HD]
        cols = [slice((kv * ratio + r) * HD, (kv * ratio + r + 1) * HD) for r in range(ratio)]
        for start in range(0, rows, tile):
            stop = start + tile
            query = jnp.concatenate([qkv_ref[start:stop, c] for c in cols], axis=0) * BF(HD**-0.5)
            near = dot_nt(query, keys[start:stop])
            row_pos = lax.broadcasted_iota(jnp.int32, near.shape, 0) & (tile - 1)
            col_pos = lax.broadcasted_iota(jnp.int32, near.shape, 1)
            scores = jnp.where(col_pos <= row_pos, near, -1e30)
            if start:
                scores = jnp.concatenate([dot_nt(query, keys[:start]), scores], axis=1)
            exponent = jnp.exp(scores - jnp.max(scores, axis=-1, keepdims=True))
            total = jnp.sum(exponent, axis=-1, keepdims=True)
            probs = (exponent * (1.0 / total)).astype(BF)
            out = dot_nn(probs, values[:stop]).astype(BF)
            for r, c in enumerate(cols):
                heads_ref[start:stop, c] = out[r * tile : (r + 1) * tile]
    product_rows(spots_ref, heads_ref, w_ref[:, proj_width:], kept_ref, sent_ref)


def attn_backward_kernel(widths, first, spots_ref, block_spots_ref, *rest):
    q_width, kv_width = widths
    proj_width = q_width + 2 * kv_width
    dy_pieces, x_pieces, rest = rest[:4], rest[4:8], list(rest[8:])
    qkv_ref, heads_ref, w_ref = rest[:3]
    rest = rest[3:]
    if first:
        grads_ref, kept_ref, sent_ref, gain_ref = rest[:4]
        rest = rest[4:]
    else:
        earlier_ref, grads_kept_ref, grads_sent_ref, kept_ref, sent_ref, gain_ref = rest[:6]
        grads_ref = rest[6]
        rest = rest[7:]
    dy_scr, x_scr, head_grad_ref, proj_grad_ref, key_acc, value_acc = rest
    place_rows(spots_ref, dy_pieces, dy_scr)
    place_rows(spots_ref, x_pieces, x_scr)
    rows = x_scr.shape[0]
    ratio = q_width // kv_width
    tile = min(256, rows)
    head_grad_ref[...] = dot_nn(dy_scr[...], w_ref[:, proj_width:]).astype(BF)
    for kv in range(kv_width // HD):
        key_cols = slice(q_width + kv * HD, q_width + (kv + 1) * HD)
        value_cols = slice(q_width + kv_width + kv * HD, q_width + kv_width + (kv + 1) * HD)
        cols = [slice((kv * ratio + r) * HD, (kv * ratio + r + 1) * HD) for r in range(ratio)]
        keys = qkv_ref[:, key_cols]
        values = qkv_ref[:, value_cols]
        key_acc[...] = jnp.zeros_like(key_acc)
        value_acc[...] = jnp.zeros_like(value_acc)
        for start in range(0, rows, tile):
            stop = start + tile
            query = jnp.concatenate([qkv_ref[start:stop, c] for c in cols], axis=0) * BF(HD**-0.5)
            out_grad = jnp.concatenate([head_grad_ref[start:stop, c] for c in cols], axis=0)
            near = dot_nt(keys[start:stop], query)
            key_pos = lax.broadcasted_iota(jnp.int32, near.shape, 0)
            row_pos = lax.broadcasted_iota(jnp.int32, near.shape, 1) & (tile - 1)
            scores = jnp.where(key_pos <= row_pos, near, -1e30)
            if start:
                scores = jnp.concatenate([dot_nt(keys[:start], query), scores], axis=0)
            exponent = jnp.exp(scores - jnp.max(scores, axis=0, keepdims=True))
            probs = exponent * (1.0 / jnp.sum(exponent, axis=0, keepdims=True))
            prob_grad = dot_nt(values[:stop], out_grad)
            inner = jnp.sum(probs * prob_grad, axis=0, keepdims=True)
            score_grad = (probs * (prob_grad - inner)).astype(BF)
            value_acc[:stop] += dot_nn(probs.astype(BF), out_grad)
            key_acc[:stop] += dot_nn(score_grad, query)
            query_grad = (dot_tn(score_grad, keys[:stop]) * (HD**-0.5)).astype(BF)
            for r, c in enumerate(cols):
                proj_grad_ref[start:stop, c] = query_grad[r * tile : (r + 1) * tile]
        proj_grad_ref[:, key_cols] = key_acc[...].astype(BF)
        proj_grad_ref[:, value_cols] = value_acc[...].astype(BF)
    product_rows(spots_ref, proj_grad_ref, w_ref[:, :proj_width], kept_ref, sent_ref, x_scr, gain_ref)
    proj_part = dot_tn(x_scr[...], proj_grad_ref[...])
    out_part = dot_tn(dy_scr[...], heads_ref[...])
    if first:
        grads_ref[:, :proj_width] = proj_part
        grads_ref[:, proj_width:] = out_part
    else:
        grads_ref[:, :proj_width] = earlier_ref[:, :proj_width] + proj_part
        grads_ref[:, proj_width:] = earlier_ref[:, proj_width:] + out_part
        depth, blk, _ = grads_kept_ref.shape
        for r in range(depth):
            here = pl.ds(pl.multiple_of(block_spots_ref[r] * blk, blk), blk)
            grads_kept_ref[r] = grads_ref[here, :]
            here = pl.ds(pl.multiple_of(block_spots_ref[depth + r] * blk, blk), blk)
            grads_sent_ref[r] = grads_ref[here, :].astype(BF)


def attn_forward(spots, weight_spots, pieces, weights, widths):
    rows, model_width = pieces[0].shape
    width = weights[0].shape[1]
    whole = len(weights) == 1
    outs = [
        jax.ShapeDtypeStruct((4 * rows, widths[0] + 2 * widths[1]), BF),
        jax.ShapeDtypeStruct((4 * rows, widths[0]), BF),
        jax.ShapeDtypeStruct((2, rows, model_width), FP),
        jax.ShapeDtypeStruct((2, rows, model_width), BF),
    ] + ([] if whole else [jax.ShapeDtypeStruct((model_width, width), BF)])
    results = pl.pallas_call(
        functools.partial(attn_forward_kernel, widths, len(weights)),
        in_specs=[SMEM] * 2 + [VMEM] * (4 + len(weights)),
        out_specs=[VMEM] * len(outs),
        out_shape=outs,
        scratch_shapes=[pltpu.VMEM((4 * rows, model_width), BF)],
        compiler_params=pltpu.CompilerParams(vmem_limit_bytes=56 << 20),
        cost_estimate=cost(14 << 30),
    )(spots, weight_spots, *pieces, *weights)
    return results if not whole else [*results, weights[0]]


def attn_backward(spots, block_spots, dy, x, qkv, heads, weights, earlier, widths):
    rows, model_width = x[0].shape
    width = weights.shape[1]
    first = earlier is None
    operands = [*dy, *x, qkv, heads, weights] + ([] if first else [earlier])
    depth = block_spots.shape[0] // 2
    whole = (model_width, width)
    blocks = (depth, model_width // depth // 2, width)
    scratch = [
        pltpu.VMEM((4 * rows, model_width), BF),
        pltpu.VMEM((4 * rows, model_width), BF),
        pltpu.VMEM(heads.shape, BF),
        pltpu.VMEM(qkv.shape, BF),
        pltpu.VMEM((4 * rows, HD), FP),
        pltpu.VMEM((4 * rows, HD), FP),
    ]
    if first:
        outs = [jax.ShapeDtypeStruct(whole, FP)]
    else:
        outs = [jax.ShapeDtypeStruct(blocks, FP), jax.ShapeDtypeStruct(blocks, BF)]
        scratch = [pltpu.VMEM(whole, FP)] + scratch
    outs += [jax.ShapeDtypeStruct((2, rows, model_width), t) for t in (FP, BF)]
    outs += [jax.ShapeDtypeStruct((1, model_width), FP)]
    return pl.pallas_call(
        functools.partial(attn_backward_kernel, widths, first),
        in_specs=[SMEM] * 2 + [VMEM] * len(operands),
        out_specs=[VMEM] * len(outs),
        out_shape=outs,
        scratch_shapes=scratch,
        compiler_params=pltpu.CompilerParams(vmem_limit_bytes=58 << 20),
        cost_estimate=cost(4 << 30),
    )(spots, block_spots, *operands)


def on_device(
    block_input,
    cotangent,
    routes,
    gate_weights,
    w_query,
    w_key,
    w_value,
    w_out,
    w_gate_up,
    w_down,
    norm_attn,
    norm_moe,
):
    depth = lax.axis_size("z")
    micro_count, rows_local, model_width = block_input.shape
    q_width, kv_width = w_query.shape[1], w_key.shape[1]
    widths = (q_width, kv_width)
    proj_width = q_width + 2 * kv_width
    side, chip, core = lax.axis_index("y"), lax.axis_index("x"), lax.axis_index("c")
    side_at = side.astype(jnp.int32).reshape(1)
    spots = jnp.stack([2 * x + c for c in (core, 1 - core) for x in (chip, 1 - chip)])
    spots = spots.astype(jnp.int32)
    place = lax.axis_index("z")
    block_spots = jnp.stack(
        [2 * lax.rem(place + r, depth) + s for s in (side, 1 - side) for r in range(depth)]
    ).astype(jnp.int32)

    packed = pack_experts(side_at, w_gate_up, w_down)
    packed_attn = pack_attn(after(w_query, packed[0][1]), w_key, w_value, w_out)
    in_rows = after(block_input, packed_attn).astype(FP)
    normed_attn, scale_attn = row_norm(in_rows, norm_attn)
    normed = [normed_attn[m].astype(BF) for m in range(micro_count)]
    cots = [cotangent[m] for m in range(micro_count)]

    def shard_of(chunk, got):
        mine = packed[chunk][0]
        first = side == 0
        return jnp.stack([jnp.where(first, mine, got), jnp.where(first, got, mine)])

    def whole_of(shard):
        whole = lax.all_gather(shard, "z", axis=0)
        return whole.reshape(-1, *whole.shape[2:])

    column, places = along_z(packed_attn, depth)
    weight_spots = jnp.stack([2 * z + s for s in (side, 1 - side) for z in places])
    weight_spots = weight_spots.astype(jnp.int32)
    across = swap(normed[0], "x")
    got = swap(packed[0][1], "y")
    own_across = swap(packed_attn, "y")
    *column, across, got = together(*column, across, got)
    shards = [shard_of(0, got)]
    chunk_weights = [whole_of(shards[0])]
    *column, across, next_normed, cot, _ = together(
        *column, across, normed[1], cots[0], shards[0]
    )

    weights = column + [own_across] + [swap(piece, "y") for piece in column[1:]]
    near_rows, far_rows = swap(normed[0], "c"), swap(across, "c")
    next_across, cot_across = swap(next_normed, "x"), swap(cot, "x")
    *weights, near_rows, far_rows, cot, next_across = together(
        *weights, near_rows, far_rows, cots[0], next_across
    )
    attn_in = [[normed[0], across, near_rows, far_rows]]

    cot_diagonal = cross(cot)
    turn = after(spots, shards[0])
    qkv, heads, kept, sent, whole = attn_forward(turn, weight_spots, attn_in[0], weights, widths)
    weights = [whole]
    saved = [(qkv, heads)]
    sent, cot_diagonal, cot_across, across = together(
        sent, cot_diagonal, cot_across, next_across
    )

    got = swap(sent, "c")
    near_rows, far_rows = swap(normed[1], "c"), swap(across, "c")
    along = plus(kept[1], got[1]).astype(BF)
    own = plus(kept[0], got[0])
    along, near_rows, far_rows, cot, theirs, turn = together(
        along, near_rows, far_rows, cots[0], packed[1][1], spots
    )
    attn_in.append([normed[1], across, near_rows, far_rows])

    came, cot_near = swap(along, "x"), swap(cot, "y")
    theirs = swap(theirs, "y")
    qkv, heads, kept, sent, _ = attn_forward(turn, weight_spots, attn_in[1], weights, widths)
    saved.append((qkv, heads))
    sent, came, cot_near = together(sent, came, cot_near)

    def moe_rows(middle):
        normed, scale = row_norm(middle, norm_moe)
        return normed.astype(BF), scale

    got = swap(sent, "c")
    middle = [in_rows[0] + plus(own, came)]
    low, scale = moe_rows(middle[0])
    normed, scale_moe = [low], [scale]
    along = plus(kept[1], got[1]).astype(BF)
    own = plus(kept[0], got[0])
    along, low = together(along, low)

    came = swap(along, "x")
    near, across = swap(low, "y"), swap(low, "x")
    expert_ids = jnp.arange(E, dtype=jnp.int32)[:, None, None, None]
    gates = jnp.sum(jnp.where(routes == expert_ids, gate_weights, 0.0), axis=3)
    gates = gates.reshape(2, E // 2, micro_count, 2, 2, rows_local)
    gates = jnp.where(chip == 0, gates, gates[:, :, :, ::-1])
    gates = jnp.where(core == 0, gates, gates[:, :, :, :, ::-1])
    mine = lax.dynamic_index_in_dim(gates, side, 0, False)
    other = lax.dynamic_index_in_dim(gates, 1 - side, 0, False)
    gates = jnp.stack([mine, swap(other.reshape(E // 2, -1), "y").reshape(mine.shape)])
    gates = gates.transpose(2, 3, 0, 4, 5, 1).reshape(micro_count, 4, 2, rows_local, E // 2)
    came, near, across, gates, theirs, low = together(came, near, across, gates, theirs, low)

    diagonal = cross(low)
    shards.append(shard_of(1, theirs))
    chunk_weights.append(whole_of(shards[1]))
    middle.append(in_rows[1] + plus(own, came))
    low, scale = moe_rows(middle[1])
    normed.append(low)
    scale_moe.append(scale)
    pair = stacked([low, cots[1]])
    diagonal, pair, _ = together(diagonal, pair, shards[1])
    blocks = stacked(
        [normed[0], cots[0], near, cot_near, across, cot_across, diagonal, cot_diagonal]
    )
    experts_in = [(blocks, swap(blocks, "c"))]
    neighbours = to_neighbours([pair] * 3)

    sums = [None] * micro_count
    turn = after(side_at, shards[1])
    all_grads = []
    first_expert = 0
    for chunk, pairs in enumerate(CHUNKS):
        last = chunk == len(CHUNKS) - 1
        grads = None
        for m in range(micro_count):
            sums[m], grads = moe_chunk(
                turn,
                experts_in[m],
                gates,
                chunk_weights[chunk],
                sums[m],
                grads,
                m,
                first_expert,
                last,
            )
            waited = [grads]
            if m == 0 and chunk == 0:
                *neighbours, _ = together(*neighbours, grads)
                blocks = stacked([pair, *neighbours])
                blocks = blocks.reshape(-1, *blocks.shape[2:])
                experts_in.append((blocks, swap(blocks, "c")))
            if m == 0 and last:
                mixed_own, mixed_along = half_sums(*sums[0][:2])
                own, along = half_sums(*sums[0][2:])
                along = [jnp.stack(both) for both in zip(along, mixed_along)]
                *along, turn, _ = together(*along, side_at, *waited)
                came = to_neighbours(along)
            else:
                turn = after(side_at, *waited)
        first_expert += 2 * pairs
        all_grads.append(grads.reshape(depth, 2, *grads.shape[1:]))

    def reduce_grads(grads):
        return lax.psum_scatter(grads, "z", scatter_dimension=0, tiled=False)

    grad_shards = [reduce_grads(all_grads[0])]

    def middle_back(m, own, came):
        moe_in_grad = sum_of(own, came)
        back = norm_back(middle[m], scale_moe[m], norm_moe, moe_in_grad)
        gain = jnp.sum(moe_in_grad * middle[m] * scale_moe[m], axis=0)
        grad = cots[m].astype(FP) + back
        return grad, grad.astype(BF), gain

    def input_back(m, middle_grad, own, came):
        return middle_grad + norm_back(in_rows[m], scale_attn[m], norm_attn, plus(own, came))

    def backward(m, turn, rows, earlier):
        return attn_backward(
            turn, block_spots, rows, attn_in[m], *saved[m], weights[0], earlier, widths
        )

    *came, grads, kept, sent, last_mixed_kept, last_mixed_sent, first_shard = together(
        *came, all_grads[1], sums[1][2], sums[1][3], *sums[1][:2], grad_shards[0]
    )
    grad_shards = [first_shard, reduce_grads(grads)]
    outputs = [(middle[0] + sum_of(mixed_own, [c[1] for c in came])).astype(BF)]
    middle_grad, low, gain_moe = middle_back(0, own, [c[0] for c in came])
    shard_got = [swap(first_shard[1], "y")]
    across, near_rows = swap(low, "x"), swap(low, "c")
    own, along = half_sums(kept, after(sent, low))
    across, near_rows, *along = together(across, near_rows, *along)
    far_rows = swap(across, "c")
    came = to_neighbours(along)
    results = backward(0, spots, [low, across, near_rows, far_rows], None)
    *came, earlier, kept, sent, gain_attn = together(*came, *results)

    middle_grads = [middle_grad]
    middle_grad, low, gain = middle_back(1, own, came)
    middle_grads.append(middle_grad)
    gain_moe = gain_moe + gain
    across, near_rows = swap(low, "x"), swap(low, "c")
    input_own, input_along = half_sums(kept, sent)
    mixed_own, mixed_along = half_sums(last_mixed_kept, after(last_mixed_sent, low))
    across, near_rows, *mixed_along, input_along, shard_got[0], outputs[0] = together(
        across, near_rows, *mixed_along, *input_along, shard_got[0], outputs[0]
    )
    far_rows = swap(across, "c")
    input_came = swap(input_along, "x")
    mixed_came = [swap(mixed_along[0], "y"), swap(mixed_along[1], "x")]
    results = backward(1, spots, [low, across, near_rows, far_rows], earlier)
    input_came, *mixed_came, grads_kept, grads_sent, kept, sent, gain = together(
        input_came, *mixed_came, *results
    )

    gains = jnp.concatenate([(gain_attn + gain)[0] / norm_attn, gain_moe]).reshape(16, -1)
    own, along = half_sums(kept, sent)
    first_input = input_back(0, middle_grads[0], input_own, input_came)
    for axis in ("c", "x", "y"):
        gains = gains + swap(gains, axis)
    along, gains, first_input, grads_sent, diagonal = together(
        along[0], gains, first_input, grads_sent, mixed_along[2]
    )
    input_came, grads_got = swap(along, "x"), swap(grads_sent, "y")
    gains = sum_over_z(gains, depth).reshape(2, model_width)
    input_came, grads_got, gains, last_shard, diagonal = together(
        input_came, grads_got, gains, grad_shards[1], diagonal
    )
    shard_got.append(swap(last_shard[1], "y"))
    diagonal = cross(diagonal)
    column = grads_kept + grads_got.astype(FP)
    pieces = along_z_sent(column, depth)
    last_input = input_back(1, middle_grads[1], own, input_came)
    shard_got[1], diagonal, last_input, *pieces = together(
        shard_got[1], diagonal, last_input, *pieces
    )
    shard_pair, shard_down = unpack_experts(
        side_at, list(zip([grad_shards[0], last_shard], shard_got))
    )
    attn_shard = sum_of(column[0], pieces)
    outputs.append((middle[1] + sum_of(mixed_own, [*mixed_came, diagonal])).astype(BF))
    input_grads = [first_input, last_input]
    return (
        jnp.stack(outputs),
        jnp.stack(input_grads),
        attn_shard[:, :q_width],
        attn_shard[:, q_width : q_width + kv_width],
        attn_shard[:, q_width + kv_width : proj_width],
        attn_shard[:, proj_width:].T,
        shard_pair,
        shard_down,
        gains[0],
        gains[1],
    )


def solution(mesh):
    dp, tensor = mesh.shape["dp"], mesh.shape["tensor"]
    fine = Mesh(mesh.devices.reshape(dp // 2, 2, tensor // 2, 2), ("z", "y", "x", "c"))
    dp_axes, tensor_axes = ("z", "y"), ("x", "c")
    rows = P(None, dp_axes + tensor_axes, None)
    return jax.shard_map(
        on_device,
        mesh=fine,
        in_specs=(
            rows,
            rows,
            P(None, dp_axes, None),
            P(None, dp_axes, None),
            P(dp_axes, tensor_axes),
            P(dp_axes, tensor_axes),
            P(dp_axes, tensor_axes),
            P(tensor_axes, dp_axes),
            P(None, dp_axes, None, tensor_axes),
            P(None, tensor_axes, dp_axes),
            P(),
            P(),
        ),
        out_specs=(
            rows,
            rows,
            P(dp_axes, tensor_axes),
            P(dp_axes, tensor_axes),
            P(dp_axes, tensor_axes),
            P(tensor_axes, dp_axes),
            P(None, dp_axes, None, tensor_axes),
            P(None, tensor_axes, dp_axes),
            P(),
            P(),
        ),
        check_vma=False,
    )
```

```python
import functools

import jax
import jax.numpy as jnp
from jax import lax
from jax.experimental import pallas as pl
from jax.experimental.pallas import tpu as pltpu
from jax.sharding import Mesh
from jax.sharding import PartitionSpec as P

HD = 64
E = 32
CHUNKS = (8, 8)

EPSILON = 1e-06
BF = jnp.bfloat16
FP = jnp.float32


def dot_nn(left, right):
    return lax.dot_general(left, right, (((1,), (0,)), ((), ())), preferred_element_type=FP)


def dot_tn(left, right):
    return lax.dot_general(left, right, (((0,), (0,)), ((), ())), preferred_element_type=FP)


def dot_nt(left, right):
    return lax.dot_general(left, right, (((1,), (1,)), ((), ())), preferred_element_type=FP)


def row_norm(in_rows, gain_vec):
    row_scale = lax.rsqrt(jnp.mean(in_rows * in_rows, axis=-1, keepdims=True) + EPSILON)
    return (in_rows * row_scale * gain_vec, row_scale)


def norm_back(in_rows, row_scale, gain_vec, grad_in):
    weighted = grad_in * gain_vec
    inner = jnp.mean(weighted * in_rows, axis=-1, keepdims=True)
    return row_scale * weighted - in_rows * row_scale * row_scale * row_scale * inner


def swap(value, axis):
    return lax.ppermute(value, axis, [(0, 1), (1, 0)])


def after(value, *earlier):
    return lax.optimization_barrier((value, *earlier))[0]


def together(*values):
    return lax.optimization_barrier(values)


def cross(value):
    return lax.ppermute(value, ("y", "x"), [(i, 3 - i) for i in range(4)])


def to_neighbours(rows):
    return [swap(rows[0], "y"), swap(rows[1], "x"), cross(rows[2])]


def plus(left, right):
    return left + right.astype(FP)


def half_sums(kept, sent):
    got = swap(sent, "c")
    low = [plus(kept[i], got[i]).astype(BF) for i in range(1, kept.shape[0])]
    return plus(kept[0], got[0]), low


def sum_of(total, parts):
    for part in parts:
        total = plus(total, part)
    return total


def along_z(shard, depth):
    place = lax.axis_index("z")
    turns_taken = [k for k in range(-((depth - 1) // 2), depth // 2 + 1) if k]
    pieces = [shard]
    for k in turns_taken:
        pieces.append(lax.ppermute(shard, "z", [(i, (i + k) % depth) for i in range(depth)]))
    return pieces, [lax.rem(place + depth - k, depth) for k in [0, *turns_taken]]


def along_z_sent(column, depth):
    return [
        lax.ppermute(column[r].astype(BF), "z", [(i, (i + r) % depth) for i in range(depth)])
        for r in range(1, depth)
    ]


def sum_over_z(value, depth):
    reach = 1
    while reach < depth:
        pairs = [(i, i ^ reach) for i in range(depth)]
        value = value + lax.ppermute(value, "z", pairs)
        reach *= 2
    return value


def cost(flops):
    return pl.CostEstimate(flops=flops, bytes_accessed=1 << 20, transcendentals=0)


SMALL = cost(1 << 30)
SMEM = pl.BlockSpec(memory_space=pltpu.SMEM)
VMEM = pl.BlockSpec(memory_space=pltpu.VMEM)


def stack_kernel(*refs):
    *ins, out_ref, sems = refs
    copies = [pltpu.make_async_copy(ref, out_ref.at[i], sems.at[i]) for i, ref in enumerate(ins)]
    for copy in copies:
        copy.start()
    for copy in copies:
        copy.wait()


def stacked(arrays):
    return pl.pallas_call(
        stack_kernel,
        in_specs=[pl.BlockSpec(memory_space=pl.ANY)] * len(arrays),
        out_specs=VMEM,
        out_shape=jax.ShapeDtypeStruct((len(arrays), *arrays[0].shape), arrays[0].dtype),
        scratch_shapes=[pltpu.SemaphoreType.DMA((len(arrays),))],
        compiler_params=pltpu.CompilerParams(vmem_limit_bytes=32 << 20),
        cost_estimate=cost(1 << 30),
    )(*arrays)


def pack_kernel(side_ref, gate_up_ref, down_ref, *rest):
    *outs, rows_scr = rest
    hidden_local, blk = down_ref.shape[1:]
    offset = 0
    for mine_ref, theirs_ref in zip(outs[::2], outs[1::2]):
        count = mine_ref.shape[1] // (3 * hidden_local)
        for out_ref, half in ((theirs_ref, 1 - side_ref[0]), (mine_ref, side_ref[0])):
            for i in range(count):
                expert = half * (E // 2) + offset + i
                rows_scr[...] = gate_up_ref[expert].astype(FP)
                values = [rows_scr[pl.ds(part, blk, stride=2), :] for part in range(2)]
                values.append(down_ref[expert].astype(FP).T)
                for part, value in enumerate(values):
                    start = (part * count + i) * hidden_local
                    out_ref[:, start : start + hidden_local] = value.astype(BF)
        offset += count


def pack_experts(side, w_gate_up, w_down):
    experts, blk, _, hidden_local = w_gate_up.shape
    shapes = [jax.ShapeDtypeStruct((blk, 3 * count * hidden_local), BF) for count in CHUNKS]
    outs = pl.pallas_call(
        pack_kernel,
        in_specs=[SMEM, VMEM, VMEM],
        out_specs=[VMEM] * (2 * len(CHUNKS)),
        out_shape=[shape for shape in shapes for _ in range(2)],
        scratch_shapes=[pltpu.VMEM((2 * blk, hidden_local), FP)],
        compiler_params=pltpu.CompilerParams(vmem_limit_bytes=32 << 20),
        cost_estimate=SMALL,
    )(side, w_gate_up.reshape(experts, 2 * blk, hidden_local), w_down)
    return list(zip(outs[::2], outs[1::2]))


def unpack_kernel(side_ref, *refs):
    *ins, gate_up_ref, down_ref = refs
    hidden_local, blk = down_ref.shape[1:]
    offset = 0
    for kept_ref, got_ref in zip(ins[::2], ins[1::2]):
        count = got_ref.shape[1] // (3 * hidden_local)
        for mine, half in ((True, side_ref[0]), (False, 1 - side_ref[0])):
            for i in range(count):
                expert = half * (E // 2) + offset + i
                values = []
                for part in range(3):
                    start = (part * count + i) * hidden_local
                    cols = slice(start, start + hidden_local)
                    values.append((kept_ref[0, :, cols] if mine else got_ref[:, cols]).astype(FP))
                for part in range(2):
                    gate_up_ref[expert, pl.ds(part, blk, stride=2), :] = values[part]
                down_ref[expert] = values[2].T
        offset += count


def unpack_experts(side, hidden_local, shards):
    blk = shards[0][1].shape[0]
    operands = [array for shard in shards for array in shard]
    gate_up, down = pl.pallas_call(
        unpack_kernel,
        in_specs=[SMEM] + [VMEM] * len(operands),
        out_specs=[VMEM, VMEM],
        out_shape=[
            jax.ShapeDtypeStruct((E, 2 * blk, hidden_local), FP),
            jax.ShapeDtypeStruct((E, hidden_local, blk), FP),
        ],
        compiler_params=pltpu.CompilerParams(vmem_limit_bytes=32 << 20),
        cost_estimate=SMALL,
    )(side, *operands)
    return gate_up.reshape(E, blk, 2, hidden_local), down


def pack_attn_kernel(query_ref, key_ref, value_ref, out_ref, packed_ref):
    start = 0
    for ref in (query_ref, key_ref, value_ref):
        packed_ref[:, start : start + ref.shape[1]] = ref[...]
        start += ref.shape[1]
    packed_ref[:, start:] = out_ref[...].astype(FP).T.astype(BF)


def pack_attn(w_query, w_key, w_value, w_out):
    width = w_query.shape[1] + w_key.shape[1] + w_value.shape[1] + w_out.shape[0]
    return pl.pallas_call(
        pack_attn_kernel,
        in_specs=[VMEM] * 4,
        out_specs=VMEM,
        out_shape=jax.ShapeDtypeStruct((w_query.shape[0], width), BF),
        cost_estimate=SMALL,
    )(w_query, w_key, w_value, w_out)


def moe_kernel(first, last, start, column, side_ref, xa_ref, xb_ref, ga_ref, gb_ref, gate_ref, w_ref, *rest):
    rest = list(rest)
    sums_in = [] if first else [rest.pop(0), rest.pop(0)]
    earlier_ref = None if start else rest.pop(0)
    sums_out, (grads_ref, acc, hidden_scr, pair_scr, sem) = rest[:-5], rest[-5:]
    step = pl.program_id(0)
    blocks, blk, width = w_ref.shape
    third = width // 3
    hidden_local = third // CHUNKS[0]
    part = min(2 * hidden_local, third)

    def spot(block):
        place = (block // 2) * 2 + (side_ref[0] + block % 2) % 2
        return pl.ds(pl.multiple_of(place * blk, blk), blk)

    @pl.when(step == 0)
    def _():
        if not start:
            pltpu.make_async_copy(earlier_ref, grads_ref, sem).start()
        acc[...] = jnp.zeros_like(acc)

    x = jnp.concatenate([xa_ref[...], xb_ref[...]], axis=0)
    g = jnp.concatenate([ga_ref[...], gb_ref[...]], axis=0)
    gates = gate_ref[...].reshape(x.shape[0], gate_ref.shape[-1])
    weights = w_ref.reshape(blocks * blk, width)
    for p in range(0, third, part):
        own, up_cols = slice(p, p + part), slice(third + p, third + p + part)
        gate = dot_nn(x, weights[:, own])
        up = dot_nn(x, weights[:, up_cols])
        out_back = dot_nn(g, weights[:, 2 * third + p : 2 * third + p + part])
        sig = 0.5 + 0.5 * jnp.tanh(0.5 * gate)
        share = jnp.concatenate(
            [
                jnp.broadcast_to(gates[:, i : i + 1], (x.shape[0], hidden_local))
                for i in range(column + p // hidden_local, column + (p + part) // hidden_local)
            ],
            axis=1,
        )
        silu = gate * sig
        hidden_grad = share * out_back
        hidden_scr[:, own] = (share * (silu * up)).astype(BF)
        pair_scr[:, own] = (hidden_grad * up * (sig + silu * (1.0 - sig))).astype(BF)
        pair_scr[:, up_cols] = (hidden_grad * silu).astype(BF)
    hidden = hidden_scr[...]
    pair_grad = pair_scr[...]
    totals = [
        dot_nt(hidden, weights[:, 2 * third :]),
        dot_nt(pair_grad, weights[:, : 2 * third]),
    ]
    acc[:, : 2 * third] += dot_tn(x, pair_grad)
    acc[:, 2 * third :] += dot_tn(g, hidden)
    if not first:
        totals = [s[...].reshape(t.shape) + t for s, t in zip(sums_in, totals)]
    if last:
        rows = xa_ref.shape[0]
        for kept_ref, sent_ref, total in zip(sums_out[::2], sums_out[1::2], totals):
            kept_ref[...] = total[:rows]
            sent_ref[...] = total[rows:].astype(BF)
    else:
        for out_ref, total in zip(sums_out, totals):
            out_ref[...] = total.reshape(out_ref.shape)

    @pl.when(step == pl.num_programs(0) - 1)
    def _():
        if not start:
            pltpu.make_async_copy(earlier_ref, grads_ref, sem).wait()
        for block in range(blocks):
            value = acc[spot(block), :]
            if not start:
                value = value + grads_ref[block].astype(FP)
            grads_ref[block] = value.astype(BF)


def moe_chunk(side, rows_in, gates, weights, sums, earlier, micro, column, last):
    count, rows, model_width = rows_in[0].shape
    count //= 2
    blocks, blk, width = weights.shape
    once = pl.Buffered(1)
    tile = min(128, rows)
    parts = rows // tile
    row = pl.BlockSpec((None, 2, tile, model_width), lambda i: (i // parts, 0, i % parts, 0))
    half = pl.BlockSpec((None, tile, model_width), lambda i: (i // parts, i % parts, 0))
    x_half = pl.BlockSpec((None, tile, model_width), lambda i: (2 * (i // parts), i % parts, 0))
    g_half = pl.BlockSpec((None, tile, model_width), lambda i: (2 * (i // parts) + 1, i % parts, 0))
    gate_spec = pl.BlockSpec(
        (None, None, 2, tile, gates.shape[-1]), lambda i: (micro, i // parts, 0, i % parts, 0)
    )
    whole = pl.BlockSpec(weights.shape, lambda i: (0, 0, 0), pipeline_mode=once)
    first, start = sums is None, earlier is None
    operands = [side, *rows_in, *rows_in, gates, weights] + ([] if first else list(sums))
    operands += [] if start else [earlier]
    if last:
        out_specs = [half] * 4
        outs = [jax.ShapeDtypeStruct((count, rows, model_width), t) for t in (FP, BF, FP, BF)]
    else:
        out_specs = [row] * 2
        outs = [jax.ShapeDtypeStruct((count, 2, rows, model_width), FP)] * 2
    *sums, grads = pl.pallas_call(
        functools.partial(moe_kernel, first, last, start, column),
        grid=(count * parts,),
        in_specs=[SMEM, x_half, x_half, g_half, g_half, gate_spec, whole]
        + ([] if first else [row, row])
        + ([] if start else [pl.BlockSpec(memory_space=pl.ANY)]),
        out_specs=out_specs + [whole],
        scratch_shapes=[
            pltpu.VMEM((model_width, width), FP),
            pltpu.VMEM((2 * tile, width // 3), BF),
            pltpu.VMEM((2 * tile, 2 * width // 3), BF),
            pltpu.SemaphoreType.DMA,
        ],
        out_shape=outs + [jax.ShapeDtypeStruct(weights.shape, BF)],
        input_output_aliases={} if first or last else {7: 0, 8: 1},
        compiler_params=pltpu.CompilerParams(vmem_limit_bytes=60 << 20),
        cost_estimate=cost(6 << 30),
    )(*operands)
    return sums, grads


def place_rows(spots_ref, pieces, whole_ref):
    rows = pieces[0].shape[0]
    for i, piece in enumerate(pieces):
        whole_ref[pl.ds(pl.multiple_of(spots_ref[i] * rows, rows), rows), :] = piece[...]


def product_rows(spots_ref, left_ref, right, kept_ref, sent_ref, x_ref=None, gain_ref=None):
    rows = kept_ref.shape[1]
    gain = 0.0
    for i in range(4):
        here = pl.ds(pl.multiple_of(spots_ref[i] * rows, rows), rows)
        value = dot_nt(left_ref[here, :], right)
        if i < 2:
            kept_ref[i] = value
        else:
            sent_ref[i - 2] = value.astype(BF)
        if x_ref is not None:
            gain += jnp.sum(value * x_ref[here, :].astype(FP), axis=0, keepdims=True)
    if x_ref is not None:
        gain_ref[...] = gain


def attn_forward_kernel(widths, n_weights, spots_ref, weight_spots_ref, *rest):
    q_width, kv_width = widths
    x_pieces, rest = rest[:4], rest[4:]
    w_pieces, rest = rest[:n_weights], rest[n_weights:]
    if n_weights > 1:
        qkv_ref, heads_ref, kept_ref, sent_ref, w_ref, x_scr = rest
        place_rows(weight_spots_ref, w_pieces, w_ref)
    else:
        qkv_ref, heads_ref, kept_ref, sent_ref, x_scr = rest
        w_ref = w_pieces[0]
    place_rows(spots_ref, x_pieces, x_scr)
    rows = x_scr.shape[0]
    proj_width = q_width + 2 * kv_width
    ratio = q_width // kv_width
    tile = min(256, rows)
    qkv_ref[...] = dot_nn(x_scr[...], w_ref[:, :proj_width]).astype(BF)
    for kv in range(kv_width // HD):
        keys = qkv_ref[:, q_width + kv * HD : q_width + (kv + 1) * HD]
        values = qkv_ref[:, q_width + kv_width + kv * HD : q_width + kv_width + (kv + 1) * HD]
        cols = [slice((kv * ratio + r) * HD, (kv * ratio + r + 1) * HD) for r in range(ratio)]
        for start in range(0, rows, tile):
            stop = start + tile
            query = jnp.concatenate([qkv_ref[start:stop, c] for c in cols], axis=0) * BF(HD**-0.5)
            near = dot_nt(query, keys[start:stop])
            row_pos = lax.broadcasted_iota(jnp.int32, near.shape, 0) & (tile - 1)
            col_pos = lax.broadcasted_iota(jnp.int32, near.shape, 1)
            scores = jnp.where(col_pos <= row_pos, near, -1e30)
            if start:
                scores = jnp.concatenate([dot_nt(query, keys[:start]), scores], axis=1)
            exponent = jnp.exp(scores - jnp.max(scores, axis=-1, keepdims=True))
            total = jnp.sum(exponent, axis=-1, keepdims=True)
            probs = (exponent * (1.0 / total)).astype(BF)
            out = dot_nn(probs, values[:stop]).astype(BF)
            for r, c in enumerate(cols):
                heads_ref[start:stop, c] = out[r * tile : (r + 1) * tile]
    product_rows(spots_ref, heads_ref, w_ref[:, proj_width:], kept_ref, sent_ref)


def attn_backward_kernel(widths, first, spots_ref, block_spots_ref, *rest):
    q_width, kv_width = widths
    proj_width = q_width + 2 * kv_width
    dy_pieces, x_pieces, rest = rest[:4], rest[4:8], list(rest[8:])
    qkv_ref, heads_ref, w_ref = rest[:3]
    rest = rest[3:]
    if first:
        grads_ref, kept_ref, sent_ref, gain_ref = rest[:4]
        rest = rest[4:]
    else:
        earlier_ref, grads_kept_ref, grads_sent_ref, kept_ref, sent_ref, gain_ref = rest[:6]
        grads_ref = rest[6]
        rest = rest[7:]
    dy_scr, x_scr, head_grad_ref, proj_grad_ref, key_acc, value_acc = rest
    place_rows(spots_ref, dy_pieces, dy_scr)
    place_rows(spots_ref, x_pieces, x_scr)
    rows = x_scr.shape[0]
    ratio = q_width // kv_width
    tile = min(256, rows)
    head_grad_ref[...] = dot_nn(dy_scr[...], w_ref[:, proj_width:]).astype(BF)
    for kv in range(kv_width // HD):
        key_cols = slice(q_width + kv * HD, q_width + (kv + 1) * HD)
        value_cols = slice(q_width + kv_width + kv * HD, q_width + kv_width + (kv + 1) * HD)
        cols = [slice((kv * ratio + r) * HD, (kv * ratio + r + 1) * HD) for r in range(ratio)]
        keys = qkv_ref[:, key_cols]
        values = qkv_ref[:, value_cols]
        key_acc[...] = jnp.zeros_like(key_acc)
        value_acc[...] = jnp.zeros_like(value_acc)
        for start in range(0, rows, tile):
            stop = start + tile
            query = jnp.concatenate([qkv_ref[start:stop, c] for c in cols], axis=0) * BF(HD**-0.5)
            out_grad = jnp.concatenate([head_grad_ref[start:stop, c] for c in cols], axis=0)
            near = dot_nt(keys[start:stop], query)
            key_pos = lax.broadcasted_iota(jnp.int32, near.shape, 0)
            row_pos = lax.broadcasted_iota(jnp.int32, near.shape, 1) & (tile - 1)
            scores = jnp.where(key_pos <= row_pos, near, -1e30)
            if start:
                scores = jnp.concatenate([dot_nt(keys[:start], query), scores], axis=0)
            exponent = jnp.exp(scores - jnp.max(scores, axis=0, keepdims=True))
            probs = exponent * (1.0 / jnp.sum(exponent, axis=0, keepdims=True))
            prob_grad = dot_nt(values[:stop], out_grad)
            inner = jnp.sum(probs * prob_grad, axis=0, keepdims=True)
            score_grad = (probs * (prob_grad - inner)).astype(BF)
            value_acc[:stop] += dot_nn(probs.astype(BF), out_grad)
            key_acc[:stop] += dot_nn(score_grad, query)
            query_grad = (dot_tn(score_grad, keys[:stop]) * (HD**-0.5)).astype(BF)
            for r, c in enumerate(cols):
                proj_grad_ref[start:stop, c] = query_grad[r * tile : (r + 1) * tile]
        proj_grad_ref[:, key_cols] = key_acc[...].astype(BF)
        proj_grad_ref[:, value_cols] = value_acc[...].astype(BF)
    product_rows(spots_ref, proj_grad_ref, w_ref[:, :proj_width], kept_ref, sent_ref, x_scr, gain_ref)
    proj_part = dot_tn(x_scr[...], proj_grad_ref[...])
    out_part = dot_tn(dy_scr[...], heads_ref[...])
    if first:
        grads_ref[:, :proj_width] = proj_part
        grads_ref[:, proj_width:] = out_part
    else:
        grads_ref[:, :proj_width] = earlier_ref[:, :proj_width] + proj_part
        grads_ref[:, proj_width:] = earlier_ref[:, proj_width:] + out_part
        depth, blk, _ = grads_kept_ref.shape
        for r in range(depth):
            here = pl.ds(pl.multiple_of(block_spots_ref[r] * blk, blk), blk)
            grads_kept_ref[r] = grads_ref[here, :]
            here = pl.ds(pl.multiple_of(block_spots_ref[depth + r] * blk, blk), blk)
            grads_sent_ref[r] = grads_ref[here, :].astype(BF)


def attn_forward(spots, weight_spots, pieces, weights, widths):
    rows, model_width = pieces[0].shape
    width = weights[0].shape[1]
    whole = len(weights) == 1
    outs = [
        jax.ShapeDtypeStruct((4 * rows, widths[0] + 2 * widths[1]), BF),
        jax.ShapeDtypeStruct((4 * rows, widths[0]), BF),
        jax.ShapeDtypeStruct((2, rows, model_width), FP),
        jax.ShapeDtypeStruct((2, rows, model_width), BF),
    ] + ([] if whole else [jax.ShapeDtypeStruct((model_width, width), BF)])
    results = pl.pallas_call(
        functools.partial(attn_forward_kernel, widths, len(weights)),
        in_specs=[SMEM] * 2 + [VMEM] * (4 + len(weights)),
        out_specs=[VMEM] * len(outs),
        out_shape=outs,
        scratch_shapes=[pltpu.VMEM((4 * rows, model_width), BF)],
        compiler_params=pltpu.CompilerParams(vmem_limit_bytes=56 << 20),
        cost_estimate=cost(14 << 30),
    )(spots, weight_spots, *pieces, *weights)
    return results if not whole else [*results, weights[0]]


def attn_backward(spots, block_spots, dy, x, qkv, heads, weights, earlier, widths):
    rows, model_width = x[0].shape
    width = weights.shape[1]
    first = earlier is None
    operands = [*dy, *x, qkv, heads, weights] + ([] if first else [earlier])
    depth = block_spots.shape[0] // 2
    whole = (model_width, width)
    blocks = (depth, model_width // depth // 2, width)
    scratch = [
        pltpu.VMEM((4 * rows, model_width), BF),
        pltpu.VMEM((4 * rows, model_width), BF),
        pltpu.VMEM(heads.shape, BF),
        pltpu.VMEM(qkv.shape, BF),
        pltpu.VMEM((4 * rows, HD), FP),
        pltpu.VMEM((4 * rows, HD), FP),
    ]
    if first:
        outs = [jax.ShapeDtypeStruct(whole, FP)]
    else:
        outs = [jax.ShapeDtypeStruct(blocks, FP), jax.ShapeDtypeStruct(blocks, BF)]
        scratch = [pltpu.VMEM(whole, FP)] + scratch
    outs += [jax.ShapeDtypeStruct((2, rows, model_width), t) for t in (FP, BF)]
    outs += [jax.ShapeDtypeStruct((1, model_width), FP)]
    return pl.pallas_call(
        functools.partial(attn_backward_kernel, widths, first),
        in_specs=[SMEM] * 2 + [VMEM] * len(operands),
        out_specs=[VMEM] * len(outs),
        out_shape=outs,
        scratch_shapes=scratch,
        compiler_params=pltpu.CompilerParams(vmem_limit_bytes=58 << 20),
        cost_estimate=cost(4 << 30),
    )(spots, block_spots, *operands)


def on_device(
    block_input,
    cotangent,
    routes,
    gate_weights,
    w_query,
    w_key,
    w_value,
    w_out,
    w_gate_up,
    w_down,
    norm_attn,
    norm_moe,
):
    depth = lax.axis_size("z")
    micro_count, rows_local, model_width = block_input.shape
    q_width, kv_width = w_query.shape[1], w_key.shape[1]
    widths = (q_width, kv_width)
    proj_width = q_width + 2 * kv_width
    side, chip, core = lax.axis_index("y"), lax.axis_index("x"), lax.axis_index("c")
    side_at = side.astype(jnp.int32).reshape(1)
    spots = jnp.stack([2 * x + c for c in (core, 1 - core) for x in (chip, 1 - chip)])
    spots = spots.astype(jnp.int32)
    place = lax.axis_index("z")
    block_spots = jnp.stack(
        [2 * lax.rem(place + r, depth) + s for s in (side, 1 - side) for r in range(depth)]
    ).astype(jnp.int32)

    packed = pack_experts(side_at, w_gate_up, w_down)
    packed_attn = pack_attn(after(w_query, packed[0][1]), w_key, w_value, w_out)
    in_rows = after(block_input, packed_attn).astype(FP)
    normed_attn, scale_attn = row_norm(in_rows, norm_attn)
    normed = [normed_attn[m].astype(BF) for m in range(micro_count)]
    cots = [cotangent[m] for m in range(micro_count)]

    def shard_of(chunk, got):
        mine = packed[chunk][0]
        first = side == 0
        return jnp.stack([jnp.where(first, mine, got), jnp.where(first, got, mine)])

    def whole_of(shard):
        whole = lax.all_gather(shard, "z", axis=0)
        return whole.reshape(-1, *whole.shape[2:])

    column, places = along_z(packed_attn, depth)
    weight_spots = jnp.stack([2 * z + s for s in (side, 1 - side) for z in places])
    weight_spots = weight_spots.astype(jnp.int32)
    across = swap(normed[0], "x")
    got = swap(packed[0][1], "y")
    own_across = swap(packed_attn, "y")
    *column, across, got = together(*column, across, got)
    shards = [shard_of(0, got)]
    chunk_weights = [whole_of(shards[0])]
    *column, across, next_normed, cot, _ = together(
        *column, across, normed[1], cots[0], shards[0]
    )

    weights = column + [own_across] + [swap(piece, "y") for piece in column[1:]]
    near_rows, far_rows = swap(normed[0], "c"), swap(across, "c")
    next_across, cot_across = swap(next_normed, "x"), swap(cot, "x")
    *weights, near_rows, far_rows, cot, next_across = together(
        *weights, near_rows, far_rows, cots[0], next_across
    )
    attn_in = [[normed[0], across, near_rows, far_rows]]

    cot_diagonal = cross(cot)
    turn = after(spots, shards[0])
    qkv, heads, kept, sent, whole = attn_forward(turn, weight_spots, attn_in[0], weights, widths)
    weights = [whole]
    saved = [(qkv, heads)]
    sent, cot_diagonal, cot_across, across = together(
        sent, cot_diagonal, cot_across, next_across
    )

    got = swap(sent, "c")
    near_rows, far_rows = swap(normed[1], "c"), swap(across, "c")
    along = plus(kept[1], got[1]).astype(BF)
    own = plus(kept[0], got[0])
    along, near_rows, far_rows, cot, theirs, turn = together(
        along, near_rows, far_rows, cots[0], packed[1][1], spots
    )
    attn_in.append([normed[1], across, near_rows, far_rows])

    came, cot_near = swap(along, "x"), swap(cot, "y")
    theirs = swap(theirs, "y")
    qkv, heads, kept, sent, _ = attn_forward(turn, weight_spots, attn_in[1], weights, widths)
    saved.append((qkv, heads))
    sent, came, cot_near = together(sent, came, cot_near)

    def moe_rows(middle):
        normed, scale = row_norm(middle, norm_moe)
        return normed.astype(BF), scale

    got = swap(sent, "c")
    middle = [in_rows[0] + plus(own, came)]
    low, scale = moe_rows(middle[0])
    normed, scale_moe = [low], [scale]
    along = plus(kept[1], got[1]).astype(BF)
    own = plus(kept[0], got[0])
    along, low = together(along, low)

    came = swap(along, "x")
    near, across = swap(low, "y"), swap(low, "x")
    expert_ids = jnp.arange(E, dtype=jnp.int32)[:, None, None, None]
    gates = jnp.sum(jnp.where(routes == expert_ids, gate_weights, 0.0), axis=3)
    gates = gates.reshape(2, E // 2, micro_count, 2, 2, rows_local)
    gates = jnp.where(chip == 0, gates, gates[:, :, :, ::-1])
    gates = jnp.where(core == 0, gates, gates[:, :, :, :, ::-1])
    mine = lax.dynamic_index_in_dim(gates, side, 0, False)
    other = lax.dynamic_index_in_dim(gates, 1 - side, 0, False)
    gates = jnp.stack([mine, swap(other.reshape(E // 2, -1), "y").reshape(mine.shape)])
    gates = gates.transpose(2, 3, 0, 4, 5, 1).reshape(micro_count, 4, 2, rows_local, E // 2)
    came, near, across, gates, theirs, low = together(came, near, across, gates, theirs, low)

    diagonal = cross(low)
    shards.append(shard_of(1, theirs))
    chunk_weights.append(whole_of(shards[1]))
    middle.append(in_rows[1] + plus(own, came))
    low, scale = moe_rows(middle[1])
    normed.append(low)
    scale_moe.append(scale)
    pair = stacked([low, cots[1]])
    diagonal, pair, _ = together(diagonal, pair, shards[1])
    blocks = stacked(
        [normed[0], cots[0], near, cot_near, across, cot_across, diagonal, cot_diagonal]
    )
    experts_in = [(blocks, swap(blocks, "c"))]
    neighbours = to_neighbours([pair] * 3)

    sums = [None] * micro_count
    turn = after(side_at, shards[1])
    all_grads = []
    first_expert = 0
    for chunk, count in enumerate(CHUNKS):
        last = chunk == len(CHUNKS) - 1
        grads = None
        for m in range(micro_count):
            sums[m], grads = moe_chunk(
                turn,
                experts_in[m],
                gates,
                chunk_weights[chunk],
                sums[m],
                grads,
                m,
                first_expert,
                last,
            )
            waited = [grads]
            if m == 0 and chunk == 0:
                *neighbours, _ = together(*neighbours, grads)
                blocks = stacked([pair, *neighbours])
                blocks = blocks.reshape(-1, *blocks.shape[2:])
                experts_in.append((blocks, swap(blocks, "c")))
            if m == 0 and last:
                mixed_own, mixed_along = half_sums(*sums[0][:2])
                own, along = half_sums(*sums[0][2:])
                along = [jnp.stack(both) for both in zip(along, mixed_along)]
                *along, turn, _ = together(*along, side_at, *waited)
                came = to_neighbours(along)
            else:
                turn = after(side_at, *waited)
        first_expert += count
        all_grads.append(grads.reshape(depth, 2, *grads.shape[1:]))

    def reduce_grads(grads):
        return lax.psum_scatter(grads, "z", scatter_dimension=0, tiled=False)

    grad_shards = [reduce_grads(all_grads[0])]

    def middle_back(m, own, came):
        moe_in_grad = sum_of(own, came)
        back = norm_back(middle[m], scale_moe[m], norm_moe, moe_in_grad)
        gain = jnp.sum(moe_in_grad * middle[m] * scale_moe[m], axis=0)
        grad = cots[m].astype(FP) + back
        return grad, grad.astype(BF), gain

    def input_back(m, middle_grad, own, came):
        return middle_grad + norm_back(in_rows[m], scale_attn[m], norm_attn, plus(own, came))

    def backward(m, turn, rows, earlier):
        return attn_backward(
            turn, block_spots, rows, attn_in[m], *saved[m], weights[0], earlier, widths
        )

    *came, grads, kept, sent, last_mixed_kept, last_mixed_sent, first_shard = together(
        *came, all_grads[1], sums[1][2], sums[1][3], *sums[1][:2], grad_shards[0]
    )
    grad_shards = [first_shard, reduce_grads(grads)]
    first_came, first_mixed_own = came, mixed_own
    middle_grad, low, gain_moe = middle_back(0, own, [c[0] for c in came])
    shard_got = [swap(first_shard[1], "y")]
    across, near_rows = swap(low, "x"), swap(low, "c")
    last_mixed_sent, sent, _ = together(last_mixed_sent, sent, low)
    own, along = half_sums(kept, sent)
    mixed_own, mixed_along = half_sums(last_mixed_kept, last_mixed_sent)
    across, near_rows, shard_got[0], *along = together(
        across, near_rows, shard_got[0], *along, *mixed_along
    )
    along, mixed_along = along[:3], along[3:]
    far_rows = swap(across, "c")
    came = to_neighbours(along)
    results = backward(0, spots, [low, across, near_rows, far_rows], None)
    *came, earlier, kept, sent, gain_attn = together(*came, *results)

    middle_grads = [middle_grad]
    middle_grad, low, gain = middle_back(1, own, came)
    middle_grads.append(middle_grad)
    gain_moe = gain_moe + gain
    across, near_rows = swap(low, "x"), swap(low, "c")
    input_own, input_along = half_sums(kept, sent)
    across, near_rows, input_along, *mixed_along = together(
        across, near_rows, *input_along, *mixed_along
    )
    far_rows = swap(across, "c")
    input_came = swap(input_along, "x")
    mixed_came = [swap(mixed_along[0], "y"), cross(mixed_along[2])]
    results = backward(1, spots, [low, across, near_rows, far_rows], earlier)
    input_came, (mixed_came, results, first_came) = together(
        input_came, (mixed_came, results, first_came)
    )
    grads_kept, grads_sent, kept, sent, gain = results

    gains = jnp.concatenate([(gain_attn + gain)[0] / norm_attn, gain_moe]).reshape(16, -1)
    grads_got = swap(grads_sent, "y")
    own, along = half_sums(kept, sent)
    first_input = input_back(0, middle_grads[0], input_own, input_came)
    outputs = [(middle[0] + sum_of(first_mixed_own, [c[1] for c in first_came])).astype(BF)]
    for axis in ("c", "x"):
        gains = gains + swap(gains, axis)
    gains, mixed_along = together(gains, mixed_along[1])
    mixed_came.append(swap(mixed_along, "x"))
    gains = sum_over_z(gains, depth)
    along, gains, first_input, outputs[0], grads_got, last_shard, mixed_came[2] = together(
        along[0], gains, first_input, outputs[0], grads_got, grad_shards[1], mixed_came[2]
    )
    input_came = swap(along, "x")
    shard_got.append(swap(last_shard[1], "y"))
    column = grads_kept + grads_got.astype(FP)
    pieces = along_z_sent(column, depth)
    last_input = input_back(1, middle_grads[1], own, input_came)
    outputs.append((middle[1] + sum_of(mixed_own, mixed_came)).astype(BF))
    last_input, outputs[1], shard_got[1], gains, *pieces = together(
        last_input, outputs[1], shard_got[1], gains, *pieces
    )
    gains = (gains + swap(gains, "y")).reshape(2, model_width)
    shard_pair, shard_down = unpack_experts(
        side_at, w_down.shape[1], list(zip([grad_shards[0], last_shard], shard_got))
    )
    attn_shard = sum_of(column[0], pieces)
    input_grads = [first_input, last_input]
    return (
        jnp.stack(outputs),
        jnp.stack(input_grads),
        attn_shard[:, :q_width],
        attn_shard[:, q_width : q_width + kv_width],
        attn_shard[:, q_width + kv_width : proj_width],
        attn_shard[:, proj_width:].T,
        shard_pair,
        shard_down,
        gains[0],
        gains[1],
    )


def solution(mesh):
    dp, tensor = mesh.shape["dp"], mesh.shape["tensor"]
    fine = Mesh(mesh.devices.reshape(dp // 2, 2, tensor // 2, 2), ("z", "y", "x", "c"))
    dp_axes, tensor_axes = ("z", "y"), ("x", "c")
    rows = P(None, dp_axes + tensor_axes, None)
    return jax.shard_map(
        on_device,
        mesh=fine,
        in_specs=(
            rows,
            rows,
            P(None, dp_axes, None),
            P(None, dp_axes, None),
            P(dp_axes, tensor_axes),
            P(dp_axes, tensor_axes),
            P(dp_axes, tensor_axes),
            P(tensor_axes, dp_axes),
            P(None, dp_axes, None, tensor_axes),
            P(None, tensor_axes, dp_axes),
            P(),
            P(),
        ),
        out_specs=(
            rows,
            rows,
            P(dp_axes, tensor_axes),
            P(dp_axes, tensor_axes),
            P(dp_axes, tensor_axes),
            P(tensor_axes, dp_axes),
            P(None, dp_axes, None, tensor_axes),
            P(None, tensor_axes, dp_axes),
            P(),
            P(),
        ),
        check_vma=False,
    )
```

```python
import functools

import jax
import jax.numpy as jnp
from jax import lax
from jax.experimental import pallas as pl
from jax.experimental.pallas import tpu as pltpu
from jax.sharding import Mesh
from jax.sharding import PartitionSpec as P

HD = 64
E = 32
CHUNKS = (8, 8)

EPSILON = 1e-06
BF = jnp.bfloat16
FP = jnp.float32


def dot_nn(left, right):
    return lax.dot_general(left, right, (((1,), (0,)), ((), ())), preferred_element_type=FP)


def dot_tn(left, right):
    return lax.dot_general(left, right, (((0,), (0,)), ((), ())), preferred_element_type=FP)


def dot_nt(left, right):
    return lax.dot_general(left, right, (((1,), (1,)), ((), ())), preferred_element_type=FP)


def row_norm(in_rows, gain_vec):
    row_scale = lax.rsqrt(jnp.mean(in_rows * in_rows, axis=-1, keepdims=True) + EPSILON)
    return (in_rows * row_scale * gain_vec, row_scale)


def norm_back(in_rows, row_scale, gain_vec, grad_in):
    weighted = grad_in * gain_vec
    inner = jnp.mean(weighted * in_rows, axis=-1, keepdims=True)
    return row_scale * weighted - in_rows * row_scale * row_scale * row_scale * inner


def swap(value, axis):
    return lax.ppermute(value, axis, [(0, 1), (1, 0)])


def after(value, *earlier):
    return lax.optimization_barrier((value, *earlier))[0]


def together(*values):
    return lax.optimization_barrier(values)


def cross(value):
    return lax.ppermute(value, ("y", "x"), [(i, 3 - i) for i in range(4)])


def to_neighbours(rows):
    return [swap(rows[0], "y"), swap(rows[1], "x"), cross(rows[2])]


def plus(left, right):
    return left + right.astype(FP)


def half_sums(kept, sent):
    got = swap(sent, "c")
    low = [plus(kept[i], got[i]).astype(BF) for i in range(1, kept.shape[0])]
    return plus(kept[0], got[0]), low


def sum_of(total, parts):
    for part in parts:
        total = plus(total, part)
    return total


def along_z(shard, depth):
    place = lax.axis_index("z")
    turns_taken = [k for k in range(-((depth - 1) // 2), depth // 2 + 1) if k]
    pieces = [shard]
    for k in turns_taken:
        pieces.append(lax.ppermute(shard, "z", [(i, (i + k) % depth) for i in range(depth)]))
    return pieces, [lax.rem(place + depth - k, depth) for k in [0, *turns_taken]]


def along_z_sent(column, depth):
    return [
        lax.ppermute(column[r].astype(BF), "z", [(i, (i + r) % depth) for i in range(depth)])
        for r in range(1, depth)
    ]


def sum_over_z(value, depth):
    reach = 1
    while reach < depth:
        pairs = [(i, i ^ reach) for i in range(depth)]
        value = value + lax.ppermute(value, "z", pairs)
        reach *= 2
    return value


def cost(flops):
    return pl.CostEstimate(flops=flops, bytes_accessed=1 << 20, transcendentals=0)


SMALL = cost(1 << 30)
SMEM = pl.BlockSpec(memory_space=pltpu.SMEM)
VMEM = pl.BlockSpec(memory_space=pltpu.VMEM)


def stack_kernel(*refs):
    *ins, out_ref, sems = refs
    copies = [pltpu.make_async_copy(ref, out_ref.at[i], sems.at[i]) for i, ref in enumerate(ins)]
    for copy in copies:
        copy.start()
    for copy in copies:
        copy.wait()


def stacked(arrays):
    return pl.pallas_call(
        stack_kernel,
        in_specs=[pl.BlockSpec(memory_space=pl.ANY)] * len(arrays),
        out_specs=VMEM,
        out_shape=jax.ShapeDtypeStruct((len(arrays), *arrays[0].shape), arrays[0].dtype),
        scratch_shapes=[pltpu.SemaphoreType.DMA((len(arrays),))],
        compiler_params=pltpu.CompilerParams(vmem_limit_bytes=32 << 20),
        cost_estimate=cost(1 << 30),
    )(*arrays)


def pack_kernel(side_ref, gate_up_ref, down_ref, *rest):
    *outs, rows_scr = rest
    hidden_local, blk = down_ref.shape[1:]
    offset = 0
    for mine_ref, theirs_ref in zip(outs[::2], outs[1::2]):
        count = mine_ref.shape[1] // (3 * hidden_local)
        for out_ref, half in ((theirs_ref, 1 - side_ref[0]), (mine_ref, side_ref[0])):
            for i in range(count):
                expert = half * (E // 2) + offset + i
                rows_scr[...] = gate_up_ref[expert].astype(FP)
                values = [rows_scr[pl.ds(part, blk, stride=2), :] for part in range(2)]
                values.append(down_ref[expert].astype(FP).T)
                for part, value in enumerate(values):
                    start = (part * count + i) * hidden_local
                    out_ref[:, start : start + hidden_local] = value.astype(BF)
        offset += count


def pack_experts(side, w_gate_up, w_down):
    experts, blk, _, hidden_local = w_gate_up.shape
    shapes = [jax.ShapeDtypeStruct((blk, 3 * count * hidden_local), BF) for count in CHUNKS]
    outs = pl.pallas_call(
        pack_kernel,
        in_specs=[SMEM, VMEM, VMEM],
        out_specs=[VMEM] * (2 * len(CHUNKS)),
        out_shape=[shape for shape in shapes for _ in range(2)],
        scratch_shapes=[pltpu.VMEM((2 * blk, hidden_local), FP)],
        compiler_params=pltpu.CompilerParams(vmem_limit_bytes=32 << 20),
        cost_estimate=SMALL,
    )(side, w_gate_up.reshape(experts, 2 * blk, hidden_local), w_down)
    return list(zip(outs[::2], outs[1::2]))


def unpack_kernel(side_ref, *refs):
    *ins, gate_up_ref, down_ref = refs
    hidden_local, blk = down_ref.shape[1:]
    offset = 0
    for kept_ref, got_ref in zip(ins[::2], ins[1::2]):
        count = got_ref.shape[1] // (3 * hidden_local)
        for mine, half in ((True, side_ref[0]), (False, 1 - side_ref[0])):
            for i in range(count):
                expert = half * (E // 2) + offset + i
                values = []
                for part in range(3):
                    start = (part * count + i) * hidden_local
                    cols = slice(start, start + hidden_local)
                    values.append((kept_ref[0, :, cols] if mine else got_ref[:, cols]).astype(FP))
                for part in range(2):
                    gate_up_ref[expert, pl.ds(part, blk, stride=2), :] = values[part]
                down_ref[expert] = values[2].T
        offset += count


def unpack_experts(side, hidden_local, shards):
    blk = shards[0][1].shape[0]
    operands = [array for shard in shards for array in shard]
    gate_up, down = pl.pallas_call(
        unpack_kernel,
        in_specs=[SMEM] + [VMEM] * len(operands),
        out_specs=[VMEM, VMEM],
        out_shape=[
            jax.ShapeDtypeStruct((E, 2 * blk, hidden_local), FP),
            jax.ShapeDtypeStruct((E, hidden_local, blk), FP),
        ],
        compiler_params=pltpu.CompilerParams(vmem_limit_bytes=32 << 20),
        cost_estimate=SMALL,
    )(side, *operands)
    return gate_up.reshape(E, blk, 2, hidden_local), down


def pack_attn_kernel(query_ref, key_ref, value_ref, out_ref, packed_ref):
    start = 0
    for ref in (query_ref, key_ref, value_ref):
        packed_ref[:, start : start + ref.shape[1]] = ref[...]
        start += ref.shape[1]
    packed_ref[:, start:] = out_ref[...].astype(FP).T.astype(BF)


def pack_attn(w_query, w_key, w_value, w_out):
    width = w_query.shape[1] + w_key.shape[1] + w_value.shape[1] + w_out.shape[0]
    return pl.pallas_call(
        pack_attn_kernel,
        in_specs=[VMEM] * 4,
        out_specs=VMEM,
        out_shape=jax.ShapeDtypeStruct((w_query.shape[0], width), BF),
        cost_estimate=SMALL,
    )(w_query, w_key, w_value, w_out)


def moe_kernel(first, last, start, column, side_ref, xa_ref, xb_ref, ga_ref, gb_ref, gate_ref, w_ref, *rest):
    rest = list(rest)
    sums_in = [] if first else [rest.pop(0), rest.pop(0)]
    earlier_ref = None if start else rest.pop(0)
    sums_out, (grads_ref, acc, hidden_scr, pair_scr, sem) = rest[:-5], rest[-5:]
    step = pl.program_id(0)
    blocks, blk, width = w_ref.shape
    third = width // 3
    hidden_local = third // CHUNKS[0]
    part = min(2 * hidden_local, third)

    def spot(block):
        place = (block // 2) * 2 + (side_ref[0] + block % 2) % 2
        return pl.ds(pl.multiple_of(place * blk, blk), blk)

    @pl.when(step == 0)
    def _():
        if not start:
            pltpu.make_async_copy(earlier_ref, grads_ref, sem).start()
        acc[...] = jnp.zeros_like(acc)

    x = jnp.concatenate([xa_ref[...], xb_ref[...]], axis=0)
    g = jnp.concatenate([ga_ref[...], gb_ref[...]], axis=0)
    gates = gate_ref[...].reshape(x.shape[0], gate_ref.shape[-1])
    weights = w_ref.reshape(blocks * blk, width)
    for p in range(0, third, part):
        own, up_cols = slice(p, p + part), slice(third + p, third + p + part)
        gate = dot_nn(x, weights[:, own])
        up = dot_nn(x, weights[:, up_cols])
        out_back = dot_nn(g, weights[:, 2 * third + p : 2 * third + p + part])
        sig = 0.5 + 0.5 * jnp.tanh(0.5 * gate)
        share = jnp.concatenate(
            [
                jnp.broadcast_to(gates[:, i : i + 1], (x.shape[0], hidden_local))
                for i in range(column + p // hidden_local, column + (p + part) // hidden_local)
            ],
            axis=1,
        )
        silu = gate * sig
        hidden_grad = share * out_back
        hidden_scr[:, own] = (share * (silu * up)).astype(BF)
        pair_scr[:, own] = (hidden_grad * up * (sig + silu * (1.0 - sig))).astype(BF)
        pair_scr[:, up_cols] = (hidden_grad * silu).astype(BF)
    hidden = hidden_scr[...]
    pair_grad = pair_scr[...]
    totals = [
        dot_nt(hidden, weights[:, 2 * third :]),
        dot_nt(pair_grad, weights[:, : 2 * third]),
    ]
    acc[:, : 2 * third] += dot_tn(x, pair_grad)
    acc[:, 2 * third :] += dot_tn(g, hidden)
    if not first:
        totals = [s[...].reshape(t.shape) + t for s, t in zip(sums_in, totals)]
    if last:
        rows = xa_ref.shape[0]
        for kept_ref, sent_ref, total in zip(sums_out[::2], sums_out[1::2], totals):
            kept_ref[...] = total[:rows]
            sent_ref[...] = total[rows:].astype(BF)
    else:
        for out_ref, total in zip(sums_out, totals):
            out_ref[...] = total.reshape(out_ref.shape)

    @pl.when(step == pl.num_programs(0) - 1)
    def _():
        if not start:
            pltpu.make_async_copy(earlier_ref, grads_ref, sem).wait()
        for block in range(blocks):
            value = acc[spot(block), :]
            if not start:
                value = value + grads_ref[block].astype(FP)
            grads_ref[block] = value.astype(BF)


def moe_chunk(side, rows_in, gates, weights, sums, earlier, micro, column, last):
    count, rows, model_width = rows_in[0].shape
    count //= 2
    blocks, blk, width = weights.shape
    once = pl.Buffered(1)
    tile = min(128, rows)
    parts = rows // tile
    row = pl.BlockSpec((None, 2, tile, model_width), lambda i: (i // parts, 0, i % parts, 0))
    half = pl.BlockSpec((None, tile, model_width), lambda i: (i // parts, i % parts, 0))
    x_half = pl.BlockSpec((None, tile, model_width), lambda i: (2 * (i // parts), i % parts, 0))
    g_half = pl.BlockSpec((None, tile, model_width), lambda i: (2 * (i // parts) + 1, i % parts, 0))
    gate_spec = pl.BlockSpec(
        (None, None, 2, tile, gates.shape[-1]), lambda i: (micro, i // parts, 0, i % parts, 0)
    )
    whole = pl.BlockSpec(weights.shape, lambda i: (0, 0, 0), pipeline_mode=once)
    first, start = sums is None, earlier is None
    operands = [side, *rows_in, *rows_in, gates, weights] + ([] if first else list(sums))
    operands += [] if start else [earlier]
    if last:
        out_specs = [half] * 4
        outs = [jax.ShapeDtypeStruct((count, rows, model_width), t) for t in (FP, BF, FP, BF)]
    else:
        out_specs = [row] * 2
        outs = [jax.ShapeDtypeStruct((count, 2, rows, model_width), FP)] * 2
    *sums, grads = pl.pallas_call(
        functools.partial(moe_kernel, first, last, start, column),
        grid=(count * parts,),
        in_specs=[SMEM, x_half, x_half, g_half, g_half, gate_spec, whole]
        + ([] if first else [row, row])
        + ([] if start else [pl.BlockSpec(memory_space=pl.ANY)]),
        out_specs=out_specs + [whole],
        scratch_shapes=[
            pltpu.VMEM((model_width, width), FP),
            pltpu.VMEM((2 * tile, width // 3), BF),
            pltpu.VMEM((2 * tile, 2 * width // 3), BF),
            pltpu.SemaphoreType.DMA,
        ],
        out_shape=outs + [jax.ShapeDtypeStruct(weights.shape, BF)],
        input_output_aliases={} if first or last else {7: 0, 8: 1},
        compiler_params=pltpu.CompilerParams(vmem_limit_bytes=60 << 20),
        cost_estimate=cost(6 << 30),
    )(*operands)
    return sums, grads


def place_rows(spots_ref, pieces, whole_ref):
    rows = pieces[0].shape[0]
    for i, piece in enumerate(pieces):
        whole_ref[pl.ds(pl.multiple_of(spots_ref[i] * rows, rows), rows), :] = piece[...]


def product_rows(spots_ref, left_ref, right, kept_ref, sent_ref, x_ref=None, gain_ref=None):
    rows = kept_ref.shape[1]
    gain = 0.0
    for i in range(4):
        here = pl.ds(pl.multiple_of(spots_ref[i] * rows, rows), rows)
        value = dot_nt(left_ref[here, :], right)
        if i < 2:
            kept_ref[i] = value
        else:
            sent_ref[i - 2] = value.astype(BF)
        if x_ref is not None:
            gain += jnp.sum(value * x_ref[here, :].astype(FP), axis=0, keepdims=True)
    if x_ref is not None:
        gain_ref[...] = gain


def attn_forward_kernel(widths, n_weights, spots_ref, weight_spots_ref, *rest):
    q_width, kv_width = widths
    x_pieces, rest = rest[:4], rest[4:]
    w_pieces, rest = rest[:n_weights], rest[n_weights:]
    if n_weights > 1:
        qkv_ref, heads_ref, kept_ref, sent_ref, lse_ref, w_ref, x_scr = rest
        place_rows(weight_spots_ref, w_pieces, w_ref)
    else:
        qkv_ref, heads_ref, kept_ref, sent_ref, lse_ref, x_scr = rest
        w_ref = w_pieces[0]
    place_rows(spots_ref, x_pieces, x_scr)
    rows = x_scr.shape[0]
    proj_width = q_width + 2 * kv_width
    ratio = q_width // kv_width
    tile = min(256, rows)
    qkv_ref[...] = dot_nn(x_scr[...], w_ref[:, :proj_width]).astype(BF)
    for kv in range(kv_width // HD):
        keys = qkv_ref[:, q_width + kv * HD : q_width + (kv + 1) * HD]
        values = qkv_ref[:, q_width + kv_width + kv * HD : q_width + kv_width + (kv + 1) * HD]
        cols = [slice((kv * ratio + r) * HD, (kv * ratio + r + 1) * HD) for r in range(ratio)]
        for start in range(0, rows, tile):
            stop = start + tile
            query = jnp.concatenate([qkv_ref[start:stop, c] for c in cols], axis=0) * BF(HD**-0.5)
            near = dot_nt(query, keys[start:stop])
            row_pos = lax.broadcasted_iota(jnp.int32, near.shape, 0) & (tile - 1)
            col_pos = lax.broadcasted_iota(jnp.int32, near.shape, 1)
            scores = jnp.where(col_pos <= row_pos, near, -1e30)
            if start:
                scores = jnp.concatenate([dot_nt(query, keys[:start]), scores], axis=1)
            highest = jnp.max(scores, axis=-1, keepdims=True)
            exponent = jnp.exp(scores - highest)
            total = jnp.sum(exponent, axis=-1, keepdims=True)
            logs = jnp.broadcast_to(highest + jnp.log(total), (ratio * tile, 128))
            lse_ref[pl.ds(kv * (rows // tile) + start // tile, 1), :] = logs.T[:1]
            probs = (exponent * (1.0 / total)).astype(BF)
            out = dot_nn(probs, values[:stop]).astype(BF)
            for r, c in enumerate(cols):
                heads_ref[start:stop, c] = out[r * tile : (r + 1) * tile]
    product_rows(spots_ref, heads_ref, w_ref[:, proj_width:], kept_ref, sent_ref)


def attn_backward_kernel(widths, first, spots_ref, block_spots_ref, *rest):
    q_width, kv_width = widths
    proj_width = q_width + 2 * kv_width
    dy_pieces, x_pieces, rest = rest[:4], rest[4:8], list(rest[8:])
    qkv_ref, heads_ref, lse_ref, w_ref = rest[:4]
    rest = rest[4:]
    if first:
        grads_ref, kept_ref, sent_ref, gain_ref = rest[:4]
        rest = rest[4:]
    else:
        earlier_ref, grads_kept_ref, grads_sent_ref, kept_ref, sent_ref, gain_ref = rest[:6]
        grads_ref = rest[6]
        rest = rest[7:]
    dy_scr, x_scr, head_grad_ref, proj_grad_ref, key_acc, value_acc = rest
    place_rows(spots_ref, dy_pieces, dy_scr)
    place_rows(spots_ref, x_pieces, x_scr)
    rows = x_scr.shape[0]
    ratio = q_width // kv_width
    tile = min(256, rows)
    head_grad_ref[...] = dot_nn(dy_scr[...], w_ref[:, proj_width:]).astype(BF)
    for kv in range(kv_width // HD):
        key_cols = slice(q_width + kv * HD, q_width + (kv + 1) * HD)
        value_cols = slice(q_width + kv_width + kv * HD, q_width + kv_width + (kv + 1) * HD)
        cols = [slice((kv * ratio + r) * HD, (kv * ratio + r + 1) * HD) for r in range(ratio)]
        keys = qkv_ref[:, key_cols]
        values = qkv_ref[:, value_cols]
        key_acc[...] = jnp.zeros_like(key_acc)
        value_acc[...] = jnp.zeros_like(value_acc)
        for start in range(0, rows, tile):
            stop = start + tile
            query = jnp.concatenate([qkv_ref[start:stop, c] for c in cols], axis=0) * BF(HD**-0.5)
            out_grad = jnp.concatenate([head_grad_ref[start:stop, c] for c in cols], axis=0)
            near = dot_nt(keys[start:stop], query)
            key_pos = lax.broadcasted_iota(jnp.int32, near.shape, 0)
            row_pos = lax.broadcasted_iota(jnp.int32, near.shape, 1) & (tile - 1)
            scores = jnp.where(key_pos <= row_pos, near, -1e30)
            if start:
                scores = jnp.concatenate([dot_nt(keys[:start], query), scores], axis=0)
            probs = jnp.exp(scores - lse_ref[pl.ds(kv * (rows // tile) + start // tile, 1), :])
            prob_grad = dot_nt(values[:stop], out_grad)
            inner = jnp.sum(probs * prob_grad, axis=0, keepdims=True)
            score_grad = (probs * (prob_grad - inner)).astype(BF)
            value_acc[:stop] += dot_nn(probs.astype(BF), out_grad)
            key_acc[:stop] += dot_nn(score_grad, query)
            query_grad = (dot_tn(score_grad, keys[:stop]) * (HD**-0.5)).astype(BF)
            for r, c in enumerate(cols):
                proj_grad_ref[start:stop, c] = query_grad[r * tile : (r + 1) * tile]
        proj_grad_ref[:, key_cols] = key_acc[...].astype(BF)
        proj_grad_ref[:, value_cols] = value_acc[...].astype(BF)
    product_rows(spots_ref, proj_grad_ref, w_ref[:, :proj_width], kept_ref, sent_ref, x_scr, gain_ref)
    proj_part = dot_tn(x_scr[...], proj_grad_ref[...])
    out_part = dot_tn(dy_scr[...], heads_ref[...])
    if first:
        grads_ref[:, :proj_width] = proj_part
        grads_ref[:, proj_width:] = out_part
    else:
        grads_ref[:, :proj_width] = earlier_ref[:, :proj_width] + proj_part
        grads_ref[:, proj_width:] = earlier_ref[:, proj_width:] + out_part
        depth, blk, _ = grads_kept_ref.shape
        for r in range(depth):
            here = pl.ds(pl.multiple_of(block_spots_ref[r] * blk, blk), blk)
            grads_kept_ref[r] = grads_ref[here, :]
            here = pl.ds(pl.multiple_of(block_spots_ref[depth + r] * blk, blk), blk)
            grads_sent_ref[r] = grads_ref[here, :].astype(BF)


def attn_forward(spots, weight_spots, pieces, weights, widths):
    rows, model_width = pieces[0].shape
    width = weights[0].shape[1]
    whole = len(weights) == 1
    tile = min(256, 4 * rows)
    stats = (widths[1] // HD * (4 * rows // tile), widths[0] // widths[1] * tile)
    outs = [
        jax.ShapeDtypeStruct((4 * rows, widths[0] + 2 * widths[1]), BF),
        jax.ShapeDtypeStruct((4 * rows, widths[0]), BF),
        jax.ShapeDtypeStruct((2, rows, model_width), FP),
        jax.ShapeDtypeStruct((2, rows, model_width), BF),
        jax.ShapeDtypeStruct(stats, FP),
    ] + ([] if whole else [jax.ShapeDtypeStruct((model_width, width), BF)])
    results = pl.pallas_call(
        functools.partial(attn_forward_kernel, widths, len(weights)),
        in_specs=[SMEM] * 2 + [VMEM] * (4 + len(weights)),
        out_specs=[VMEM] * len(outs),
        out_shape=outs,
        scratch_shapes=[pltpu.VMEM((4 * rows, model_width), BF)],
        compiler_params=pltpu.CompilerParams(vmem_limit_bytes=56 << 20),
        cost_estimate=cost(14 << 30),
    )(spots, weight_spots, *pieces, *weights)
    return results if not whole else [*results, weights[0]]


def attn_backward(spots, block_spots, dy, x, qkv, heads, lse, weights, earlier, widths):
    rows, model_width = x[0].shape
    width = weights.shape[1]
    first = earlier is None
    operands = [*dy, *x, qkv, heads, lse, weights] + ([] if first else [earlier])
    depth = block_spots.shape[0] // 2
    whole = (model_width, width)
    blocks = (depth, model_width // depth // 2, width)
    scratch = [
        pltpu.VMEM((4 * rows, model_width), BF),
        pltpu.VMEM((4 * rows, model_width), BF),
        pltpu.VMEM(heads.shape, BF),
        pltpu.VMEM(qkv.shape, BF),
        pltpu.VMEM((4 * rows, HD), FP),
        pltpu.VMEM((4 * rows, HD), FP),
    ]
    if first:
        outs = [jax.ShapeDtypeStruct(whole, FP)]
    else:
        outs = [jax.ShapeDtypeStruct(blocks, FP), jax.ShapeDtypeStruct(blocks, BF)]
        scratch = [pltpu.VMEM(whole, FP)] + scratch
    outs += [jax.ShapeDtypeStruct((2, rows, model_width), t) for t in (FP, BF)]
    outs += [jax.ShapeDtypeStruct((1, model_width), FP)]
    return pl.pallas_call(
        functools.partial(attn_backward_kernel, widths, first),
        in_specs=[SMEM] * 2 + [VMEM] * len(operands),
        out_specs=[VMEM] * len(outs),
        out_shape=outs,
        scratch_shapes=scratch,
        compiler_params=pltpu.CompilerParams(vmem_limit_bytes=58 << 20),
        cost_estimate=cost(1 << 24),
    )(spots, block_spots, *operands)


def on_device(
    block_input,
    cotangent,
    routes,
    gate_weights,
    w_query,
    w_key,
    w_value,
    w_out,
    w_gate_up,
    w_down,
    norm_attn,
    norm_moe,
):
    depth = lax.axis_size("z")
    micro_count, rows_local, model_width = block_input.shape
    q_width, kv_width = w_query.shape[1], w_key.shape[1]
    widths = (q_width, kv_width)
    proj_width = q_width + 2 * kv_width
    side, chip, core = lax.axis_index("y"), lax.axis_index("x"), lax.axis_index("c")
    side_at = side.astype(jnp.int32).reshape(1)
    spots = jnp.stack([2 * x + c for c in (core, 1 - core) for x in (chip, 1 - chip)])
    spots = spots.astype(jnp.int32)
    place = lax.axis_index("z")
    block_spots = jnp.stack(
        [2 * lax.rem(place + r, depth) + s for s in (side, 1 - side) for r in range(depth)]
    ).astype(jnp.int32)

    packed_attn = pack_attn(w_query, w_key, w_value, w_out)
    packed = pack_experts(after(side_at, packed_attn), w_gate_up, w_down)
    in_rows = after(block_input, packed[0][1]).astype(FP)
    normed_attn, scale_attn = row_norm(in_rows, norm_attn)
    normed = [normed_attn[m].astype(BF) for m in range(micro_count)]
    cots = [cotangent[m] for m in range(micro_count)]

    def shard_of(chunk, got):
        mine = packed[chunk][0]
        first = side == 0
        return jnp.stack([jnp.where(first, mine, got), jnp.where(first, got, mine)])

    def whole_of(shard):
        whole = lax.all_gather(shard, "z", axis=0)
        return whole.reshape(-1, *whole.shape[2:])

    column, places = along_z(packed_attn, depth)
    weight_spots = jnp.stack([2 * z + s for s in (side, 1 - side) for z in places])
    weight_spots = weight_spots.astype(jnp.int32)
    across = swap(normed[0], "x")
    got = swap(packed[0][1], "y")
    own_across = swap(packed_attn, "y")
    *column, across, got = together(*column, across, got)
    shards = [shard_of(0, got)]
    chunk_weights = [whole_of(shards[0])]
    *column, across, next_normed, cot, _ = together(
        *column, across, normed[1], cots[0], shards[0]
    )

    weights = column + [own_across] + [swap(piece, "y") for piece in column[1:]]
    near_rows, far_rows = swap(normed[0], "c"), swap(across, "c")
    next_across, cot_across = swap(next_normed, "x"), swap(cot, "x")
    *weights, near_rows, far_rows, cot, next_across = together(
        *weights, near_rows, far_rows, cots[0], next_across
    )
    attn_in = [[normed[0], across, near_rows, far_rows]]

    cot_diagonal = cross(cot)
    turn = after(spots, shards[0])
    qkv, heads, kept, sent, lse, whole = attn_forward(
        turn, weight_spots, attn_in[0], weights, widths
    )
    weights = [whole]
    saved = [(qkv, heads, lse)]
    sent, cot_diagonal, cot_across, across = together(
        sent, cot_diagonal, cot_across, next_across
    )

    got = swap(sent, "c")
    near_rows, far_rows = swap(normed[1], "c"), swap(across, "c")
    along = plus(kept[1], got[1]).astype(BF)
    own = plus(kept[0], got[0])
    along, near_rows, far_rows, cot, turn = together(along, near_rows, far_rows, cots[0], spots)
    attn_in.append([normed[1], across, near_rows, far_rows])

    expert_ids = jnp.arange(E, dtype=jnp.int32)[:, None, None, None]
    gates = jnp.sum(jnp.where(routes == expert_ids, gate_weights, 0.0), axis=3)
    gates = gates.reshape(2, E // 2, micro_count, 2, 2, rows_local)
    gates = jnp.where(chip == 0, gates, gates[:, :, :, ::-1])
    gates = jnp.where(core == 0, gates, gates[:, :, :, :, ::-1])
    mine = lax.dynamic_index_in_dim(gates, side, 0, False)
    other = lax.dynamic_index_in_dim(gates, 1 - side, 0, False)
    other = after(other.reshape(E // 2, -1), along)
    came, cot_near, gates_got = swap(along, "x"), swap(cot, "y"), swap(other, "y")
    qkv, heads, kept, sent, lse, _ = attn_forward(
        turn, weight_spots, attn_in[1], weights, widths
    )
    saved.append((qkv, heads, lse))
    sent, came, cot_near, gates_got = together(sent, came, cot_near, gates_got)

    def moe_rows(middle):
        normed, scale = row_norm(middle, norm_moe)
        return normed.astype(BF), scale

    got = swap(sent, "c")
    middle = [in_rows[0] + plus(own, came)]
    low, scale = moe_rows(middle[0])
    normed, scale_moe = [low], [scale]
    along = plus(kept[1], got[1]).astype(BF)
    own = plus(kept[0], got[0])
    along, low = together(along, low)

    near, across, diagonal = to_neighbours([low] * 3)
    gates = jnp.stack([mine, gates_got.reshape(mine.shape)])
    gates = gates.transpose(2, 3, 0, 4, 5, 1).reshape(micro_count, 4, 2, rows_local, E // 2)
    near, across, diagonal, gates, along, theirs = together(
        near, across, diagonal, gates, along, packed[1][1]
    )

    came, theirs = swap(along, "x"), swap(theirs, "y")
    blocks = stacked(
        [normed[0], cots[0], near, cot_near, across, cot_across, diagonal, cot_diagonal]
    )
    experts_in = [(blocks, swap(blocks, "c"))]
    came, theirs, blocks = together(came, theirs, blocks)
    middle.append(in_rows[1] + plus(own, came))
    low, scale = moe_rows(middle[1])
    normed.append(low)
    scale_moe.append(scale)
    pair = stacked([low, cots[1]])
    shards.append(shard_of(1, theirs))
    chunk_weights.append(whole_of(shards[1]))
    neighbours = to_neighbours([pair] * 3)

    sums = [None] * micro_count
    turn = after(side_at, shards[1], pair)
    all_grads = []
    first_expert = 0
    for chunk, count in enumerate(CHUNKS):
        last = chunk == len(CHUNKS) - 1
        grads = None
        for m in range(micro_count):
            sums[m], grads = moe_chunk(
                turn,
                experts_in[m],
                gates,
                chunk_weights[chunk],
                sums[m],
                grads,
                m,
                first_expert,
                last,
            )
            waited = [grads]
            if m == 0 and chunk == 0:
                *neighbours, _ = together(*neighbours, grads)
                blocks = stacked([pair, *neighbours])
                blocks = blocks.reshape(-1, *blocks.shape[2:])
                experts_in.append((blocks, swap(blocks, "c")))
            if m == 0 and last:
                mixed_own, mixed_along = half_sums(*sums[0][:2])
                own, along = half_sums(*sums[0][2:])
                along = [jnp.stack(both) for both in zip(along, mixed_along)]
                *along, turn, _ = together(*along, side_at, *waited)
                came = to_neighbours(along)
            else:
                turn = after(side_at, *waited)
        first_expert += count
        all_grads.append(grads.reshape(depth, 2, *grads.shape[1:]))

    def reduce_grads(grads):
        return lax.psum_scatter(grads, "z", scatter_dimension=0, tiled=False)

    grad_shards = [reduce_grads(all_grads[0])]

    def middle_back(m, own, came):
        moe_in_grad = sum_of(own, came)
        back = norm_back(middle[m], scale_moe[m], norm_moe, moe_in_grad)
        gain = jnp.sum(moe_in_grad * middle[m] * scale_moe[m], axis=0)
        grad = cots[m].astype(FP) + back
        return grad, grad.astype(BF), gain

    def input_back(m, middle_grad, own, came):
        return middle_grad + norm_back(in_rows[m], scale_attn[m], norm_attn, plus(own, came))

    def backward(m, turn, rows, earlier):
        return attn_backward(
            turn, block_spots, rows, attn_in[m], *saved[m], weights[0], earlier, widths
        )

    *came, grads, kept, sent, last_mixed_kept, last_mixed_sent, first_shard = together(
        *came, all_grads[1], sums[1][2], sums[1][3], *sums[1][:2], grad_shards[0]
    )
    grad_shards = [first_shard, reduce_grads(grads)]
    first_came, first_mixed_own = came, mixed_own
    middle_grad, low, gain_moe = middle_back(0, own, [c[0] for c in came])
    across, near_rows = swap(low, "x"), swap(low, "c")
    last_mixed_sent, sent, _ = together(last_mixed_sent, sent, low)
    own, along = half_sums(kept, sent)
    mixed_own, mixed_along = half_sums(last_mixed_kept, last_mixed_sent)
    came = to_neighbours(along)
    across, near_rows, came[0], *mixed_along = together(across, near_rows, came[0], *mixed_along)
    far_rows = swap(across, "c")
    results = backward(0, spots, [low, across, near_rows, far_rows], None)
    *came, earlier, kept, sent, gain_attn, first_shard = together(*came, *results, first_shard)

    middle_grads = [middle_grad]
    middle_grad, low, gain = middle_back(1, own, came)
    middle_grads.append(middle_grad)
    gain_moe = gain_moe + gain
    across, near_rows = swap(low, "x"), swap(low, "c")
    input_own, input_along = half_sums(kept, sent)
    shard_got = [swap(first_shard[1], "y")]
    across, near_rows, shard_got[0], input_along, *mixed_along = together(
        across, near_rows, shard_got[0], *input_along, *mixed_along
    )
    far_rows = swap(across, "c")
    input_came = swap(input_along, "x")
    mixed_came = [swap(mixed_along[0], "y"), cross(mixed_along[2])]
    results = backward(1, spots, [low, across, near_rows, far_rows], earlier)
    input_came, (mixed_came, results, first_came) = together(
        input_came, (mixed_came, results, first_came)
    )
    grads_kept, grads_sent, kept, sent, gain = results

    gains = jnp.concatenate([(gain_attn + gain)[0] / norm_attn, gain_moe]).reshape(16, -1)
    grads_got = swap(grads_sent, "y")
    own, along = half_sums(kept, sent)
    first_input = input_back(0, middle_grads[0], input_own, input_came)
    outputs = [(middle[0] + sum_of(first_mixed_own, [c[1] for c in first_came])).astype(BF)]
    mixed_came.append(swap(mixed_along[1], "x"))
    gains = sum_over_z(gains + swap(gains, "c"), depth)
    gains, mixed_came[2] = together(gains, mixed_came[2])
    gains = gains + swap(gains, "x")
    column = grads_kept + grads_got.astype(FP)
    along, gains, first_input, outputs[0], column, last_shard, mixed_own = together(
        along[0], gains, first_input, outputs[0], column, grad_shards[1], mixed_own
    )
    input_came = swap(along, "x")
    last_sent, column = together(last_shard[1], column)
    shard_got.append(swap(last_sent, "y"))
    pieces = along_z_sent(column, depth)
    last_input = input_back(1, middle_grads[1], own, input_came)
    outputs.append((middle[1] + sum_of(mixed_own, mixed_came)).astype(BF))
    last_input, outputs[1], shard_got[1], gains, *pieces = together(
        last_input, outputs[1], shard_got[1], gains, *pieces
    )
    gains = (gains + swap(gains, "y")).reshape(2, model_width)
    shard_pair, shard_down = unpack_experts(
        side_at, w_down.shape[1], list(zip([grad_shards[0], last_shard], shard_got))
    )
    attn_shard = sum_of(column[0], pieces)
    input_grads = [first_input, last_input]
    return (
        jnp.stack(outputs),
        jnp.stack(input_grads),
        attn_shard[:, :q_width],
        attn_shard[:, q_width : q_width + kv_width],
        attn_shard[:, q_width + kv_width : proj_width],
        attn_shard[:, proj_width:].T,
        shard_pair,
        shard_down,
        gains[0],
        gains[1],
    )


def solution(mesh):
    dp, tensor = mesh.shape["dp"], mesh.shape["tensor"]
    fine = Mesh(mesh.devices.reshape(dp // 2, 2, tensor // 2, 2), ("z", "y", "x", "c"))
    dp_axes, tensor_axes = ("z", "y"), ("x", "c")
    rows = P(None, dp_axes + tensor_axes, None)
    return jax.shard_map(
        on_device,
        mesh=fine,
        in_specs=(
            rows,
            rows,
            P(None, dp_axes, None),
            P(None, dp_axes, None),
            P(dp_axes, tensor_axes),
            P(dp_axes, tensor_axes),
            P(dp_axes, tensor_axes),
            P(tensor_axes, dp_axes),
            P(None, dp_axes, None, tensor_axes),
            P(None, tensor_axes, dp_axes),
            P(),
            P(),
        ),
        out_specs=(
            rows,
            rows,
            P(dp_axes, tensor_axes),
            P(dp_axes, tensor_axes),
            P(dp_axes, tensor_axes),
            P(tensor_axes, dp_axes),
            P(None, dp_axes, None, tensor_axes),
            P(None, tensor_axes, dp_axes),
            P(),
            P(),
        ),
        check_vma=False,
    )
```

```python
import functools

import jax
import jax.numpy as jnp
from jax import lax
from jax.experimental import pallas as pl
from jax.experimental.pallas import tpu as pltpu
from jax.sharding import Mesh
from jax.sharding import PartitionSpec as P

HD = 64
E = 32
CHUNKS = (8, 8)

EPSILON = 1e-06
BF = jnp.bfloat16
FP = jnp.float32


def dot_nn(left, right):
    return lax.dot_general(left, right, (((1,), (0,)), ((), ())), preferred_element_type=FP)


def dot_tn(left, right):
    return lax.dot_general(left, right, (((0,), (0,)), ((), ())), preferred_element_type=FP)


def dot_nt(left, right):
    return lax.dot_general(left, right, (((1,), (1,)), ((), ())), preferred_element_type=FP)


def row_norm(in_rows, gain_vec):
    row_scale = lax.rsqrt(jnp.mean(in_rows * in_rows, axis=-1, keepdims=True) + EPSILON)
    return (in_rows * row_scale * gain_vec, row_scale)


def norm_back(in_rows, row_scale, gain_vec, grad_in):
    weighted = grad_in * gain_vec
    inner = jnp.mean(weighted * in_rows, axis=-1, keepdims=True)
    return row_scale * weighted - in_rows * row_scale * row_scale * row_scale * inner


def swap(value, axis):
    return lax.ppermute(value, axis, [(0, 1), (1, 0)])


def after(value, *earlier):
    return lax.optimization_barrier((value, *earlier))[0]


def together(*values):
    return lax.optimization_barrier(values)


def cross(value):
    return lax.ppermute(value, ("y", "x"), [(i, 3 - i) for i in range(4)])


def to_neighbours(rows):
    return [swap(rows[0], "y"), swap(rows[1], "x"), cross(rows[2])]


def plus(left, right):
    return left + right.astype(FP)


def half_sums(kept, sent):
    got = swap(sent, "c")
    low = [plus(kept[i], got[i]).astype(BF) for i in range(1, kept.shape[0])]
    return plus(kept[0], got[0]), low


def sum_of(total, parts):
    for part in parts:
        total = plus(total, part)
    return total


def along_z(shard, depth):
    place = lax.axis_index("z")
    turns_taken = [k for k in range(-((depth - 1) // 2), depth // 2 + 1) if k]
    pieces = [shard]
    for k in turns_taken:
        pieces.append(lax.ppermute(shard, "z", [(i, (i + k) % depth) for i in range(depth)]))
    return pieces, [lax.rem(place + depth - k, depth) for k in [0, *turns_taken]]


def along_z_sent(column, depth):
    return [
        lax.ppermute(column[r].astype(BF), "z", [(i, (i + r) % depth) for i in range(depth)])
        for r in range(1, depth)
    ]


def sum_over_z(value, depth):
    reach = 1
    while reach < depth:
        pairs = [(i, i ^ reach) for i in range(depth)]
        value = value + lax.ppermute(value, "z", pairs)
        reach *= 2
    return value


def cost(flops):
    return pl.CostEstimate(flops=flops, bytes_accessed=1 << 20, transcendentals=0)


SMALL = cost(1 << 30)
SMEM = pl.BlockSpec(memory_space=pltpu.SMEM)
VMEM = pl.BlockSpec(memory_space=pltpu.VMEM)


def stack_kernel(*refs):
    *ins, out_ref, sems = refs
    copies = [pltpu.make_async_copy(ref, out_ref.at[i], sems.at[i]) for i, ref in enumerate(ins)]
    for copy in copies:
        copy.start()
    for copy in copies:
        copy.wait()


def stacked(arrays):
    return pl.pallas_call(
        stack_kernel,
        in_specs=[pl.BlockSpec(memory_space=pl.ANY)] * len(arrays),
        out_specs=VMEM,
        out_shape=jax.ShapeDtypeStruct((len(arrays), *arrays[0].shape), arrays[0].dtype),
        scratch_shapes=[pltpu.SemaphoreType.DMA((len(arrays),))],
        compiler_params=pltpu.CompilerParams(vmem_limit_bytes=32 << 20),
        cost_estimate=cost(1 << 30),
    )(*arrays)


def pack_kernel(side_ref, gate_up_ref, down_ref, *rest):
    *outs, rows_scr = rest
    hidden_local, blk = down_ref.shape[1:]
    offset = 0
    for mine_ref, theirs_ref in zip(outs[::2], outs[1::2]):
        count = mine_ref.shape[1] // (3 * hidden_local)
        for out_ref, half in ((theirs_ref, 1 - side_ref[0]), (mine_ref, side_ref[0])):
            for i in range(count):
                expert = half * (E // 2) + offset + i
                rows_scr[...] = gate_up_ref[expert].astype(FP)
                values = [rows_scr[pl.ds(part, blk, stride=2), :] for part in range(2)]
                values.append(down_ref[expert].astype(FP).T)
                for part, value in enumerate(values):
                    start = (part * count + i) * hidden_local
                    out_ref[:, start : start + hidden_local] = value.astype(BF)
        offset += count


def pack_experts(side, w_gate_up, w_down):
    experts, blk, _, hidden_local = w_gate_up.shape
    shapes = [jax.ShapeDtypeStruct((blk, 3 * count * hidden_local), BF) for count in CHUNKS]
    outs = pl.pallas_call(
        pack_kernel,
        in_specs=[SMEM, VMEM, VMEM],
        out_specs=[VMEM] * (2 * len(CHUNKS)),
        out_shape=[shape for shape in shapes for _ in range(2)],
        scratch_shapes=[pltpu.VMEM((2 * blk, hidden_local), FP)],
        compiler_params=pltpu.CompilerParams(vmem_limit_bytes=32 << 20),
        cost_estimate=SMALL,
    )(side, w_gate_up.reshape(experts, 2 * blk, hidden_local), w_down)
    return list(zip(outs[::2], outs[1::2]))


def unpack_kernel(side_ref, *refs):
    *ins, gate_up_ref, down_ref = refs
    hidden_local, blk = down_ref.shape[1:]
    offset = 0
    for kept_ref, got_ref in zip(ins[::2], ins[1::2]):
        count = got_ref.shape[1] // (3 * hidden_local)
        for mine, half in ((True, side_ref[0]), (False, 1 - side_ref[0])):
            for i in range(count):
                expert = half * (E // 2) + offset + i
                values = []
                for part in range(3):
                    start = (part * count + i) * hidden_local
                    cols = slice(start, start + hidden_local)
                    values.append((kept_ref[0, :, cols] if mine else got_ref[:, cols]).astype(FP))
                for part in range(2):
                    gate_up_ref[expert, pl.ds(part, blk, stride=2), :] = values[part]
                down_ref[expert] = values[2].T
        offset += count


def unpack_experts(side, hidden_local, shards):
    blk = shards[0][1].shape[0]
    operands = [array for shard in shards for array in shard]
    gate_up, down = pl.pallas_call(
        unpack_kernel,
        in_specs=[SMEM] + [VMEM] * len(operands),
        out_specs=[VMEM, VMEM],
        out_shape=[
            jax.ShapeDtypeStruct((E, 2 * blk, hidden_local), FP),
            jax.ShapeDtypeStruct((E, hidden_local, blk), FP),
        ],
        compiler_params=pltpu.CompilerParams(vmem_limit_bytes=32 << 20),
        cost_estimate=SMALL,
    )(side, *operands)
    return gate_up.reshape(E, blk, 2, hidden_local), down


def pack_attn_kernel(query_ref, key_ref, value_ref, out_ref, packed_ref):
    start = 0
    for ref in (query_ref, key_ref, value_ref):
        packed_ref[:, start : start + ref.shape[1]] = ref[...]
        start += ref.shape[1]
    packed_ref[:, start:] = out_ref[...].astype(FP).T.astype(BF)


def pack_attn(w_query, w_key, w_value, w_out):
    width = w_query.shape[1] + w_key.shape[1] + w_value.shape[1] + w_out.shape[0]
    return pl.pallas_call(
        pack_attn_kernel,
        in_specs=[VMEM] * 4,
        out_specs=VMEM,
        out_shape=jax.ShapeDtypeStruct((w_query.shape[0], width), BF),
        cost_estimate=SMALL,
    )(w_query, w_key, w_value, w_out)


def moe_kernel(first, last, start, column, side_ref, xa_ref, xb_ref, ga_ref, gb_ref, gate_ref, w_ref, *rest):
    rest = list(rest)
    sums_in = [] if first else [rest.pop(0), rest.pop(0)]
    earlier_ref = None if start else rest.pop(0)
    sums_out, (grads_ref, acc, hidden_scr, pair_scr, sem) = rest[:-5], rest[-5:]
    step = pl.program_id(0)
    blocks, blk, width = w_ref.shape
    third = width // 3
    hidden_local = third // CHUNKS[0]
    part = min(2 * hidden_local, third)

    def spot(block):
        place = (block // 2) * 2 + (side_ref[0] + block % 2) % 2
        return pl.ds(pl.multiple_of(place * blk, blk), blk)

    @pl.when(step == 0)
    def _():
        if not start:
            pltpu.make_async_copy(earlier_ref, grads_ref, sem).start()
        acc[...] = jnp.zeros_like(acc)

    x = jnp.concatenate([xa_ref[...], xb_ref[...]], axis=0)
    g = jnp.concatenate([ga_ref[...], gb_ref[...]], axis=0)
    gates = gate_ref[...].reshape(x.shape[0], gate_ref.shape[-1])
    weights = w_ref.reshape(blocks * blk, width)
    for p in range(0, third, part):
        own, up_cols = slice(p, p + part), slice(third + p, third + p + part)
        gate = dot_nn(x, weights[:, own])
        up = dot_nn(x, weights[:, up_cols])
        out_back = dot_nn(g, weights[:, 2 * third + p : 2 * third + p + part])
        sig = 0.5 + 0.5 * jnp.tanh(0.5 * gate)
        share = jnp.concatenate(
            [
                jnp.broadcast_to(gates[:, i : i + 1], (x.shape[0], hidden_local))
                for i in range(column + p // hidden_local, column + (p + part) // hidden_local)
            ],
            axis=1,
        )
        silu = gate * sig
        hidden_grad = share * out_back
        hidden_scr[:, own] = (share * (silu * up)).astype(BF)
        pair_scr[:, own] = (hidden_grad * up * (sig + silu * (1.0 - sig))).astype(BF)
        pair_scr[:, up_cols] = (hidden_grad * silu).astype(BF)
    hidden = hidden_scr[...]
    pair_grad = pair_scr[...]
    totals = [
        dot_nt(hidden, weights[:, 2 * third :]),
        dot_nt(pair_grad, weights[:, : 2 * third]),
    ]
    acc[:, : 2 * third] += dot_tn(x, pair_grad)
    acc[:, 2 * third :] += dot_tn(g, hidden)
    if not first:
        totals = [s[...].reshape(t.shape) + t for s, t in zip(sums_in, totals)]
    if last:
        rows = xa_ref.shape[0]
        for kept_ref, sent_ref, total in zip(sums_out[::2], sums_out[1::2], totals):
            kept_ref[...] = total[:rows]
            sent_ref[...] = total[rows:].astype(BF)
    else:
        for out_ref, total in zip(sums_out, totals):
            out_ref[...] = total.reshape(out_ref.shape)

    @pl.when(step == pl.num_programs(0) - 1)
    def _():
        if not start:
            pltpu.make_async_copy(earlier_ref, grads_ref, sem).wait()
        for block in range(blocks):
            value = acc[spot(block), :]
            if not start:
                value = value + grads_ref[block].astype(FP)
            grads_ref[block] = value.astype(BF)


def moe_chunk(side, rows_in, gates, weights, sums, earlier, micro, column, last):
    count, rows, model_width = rows_in[0].shape
    count //= 2
    blocks, blk, width = weights.shape
    once = pl.Buffered(1)
    tile = min(128, rows)
    parts = rows // tile
    row = pl.BlockSpec((None, 2, tile, model_width), lambda i: (i // parts, 0, i % parts, 0))
    half = pl.BlockSpec((None, tile, model_width), lambda i: (i // parts, i % parts, 0))
    x_half = pl.BlockSpec((None, tile, model_width), lambda i: (2 * (i // parts), i % parts, 0))
    g_half = pl.BlockSpec((None, tile, model_width), lambda i: (2 * (i // parts) + 1, i % parts, 0))
    gate_spec = pl.BlockSpec(
        (None, None, 2, tile, gates.shape[-1]), lambda i: (micro, i // parts, 0, i % parts, 0)
    )
    whole = pl.BlockSpec(weights.shape, lambda i: (0, 0, 0), pipeline_mode=once)
    first, start = sums is None, earlier is None
    operands = [side, *rows_in, *rows_in, gates, weights] + ([] if first else list(sums))
    operands += [] if start else [earlier]
    if last:
        out_specs = [half] * 4
        outs = [jax.ShapeDtypeStruct((count, rows, model_width), t) for t in (FP, BF, FP, BF)]
    else:
        out_specs = [row] * 2
        outs = [jax.ShapeDtypeStruct((count, 2, rows, model_width), FP)] * 2
    *sums, grads = pl.pallas_call(
        functools.partial(moe_kernel, first, last, start, column),
        grid=(count * parts,),
        in_specs=[SMEM, x_half, x_half, g_half, g_half, gate_spec, whole]
        + ([] if first else [row, row])
        + ([] if start else [pl.BlockSpec(memory_space=pl.ANY)]),
        out_specs=out_specs + [whole],
        scratch_shapes=[
            pltpu.VMEM((model_width, width), FP),
            pltpu.VMEM((2 * tile, width // 3), BF),
            pltpu.VMEM((2 * tile, 2 * width // 3), BF),
            pltpu.SemaphoreType.DMA,
        ],
        out_shape=outs + [jax.ShapeDtypeStruct(weights.shape, BF)],
        input_output_aliases={} if first or last else {7: 0, 8: 1},
        compiler_params=pltpu.CompilerParams(vmem_limit_bytes=60 << 20),
        cost_estimate=cost(6 << 30),
    )(*operands)
    return sums, grads


def place_rows(spots_ref, pieces, whole_ref):
    rows = pieces[0].shape[0]
    for i, piece in enumerate(pieces):
        whole_ref[pl.ds(pl.multiple_of(spots_ref[i] * rows, rows), rows), :] = piece[...]


def product_rows(spots_ref, left_ref, right, kept_ref, sent_ref, x_ref=None, gain_ref=None):
    rows = kept_ref.shape[1]
    gain = 0.0
    for i in range(4):
        here = pl.ds(pl.multiple_of(spots_ref[i] * rows, rows), rows)
        value = dot_nt(left_ref[here, :], right)
        if i < 2:
            kept_ref[i] = value
        else:
            sent_ref[i - 2] = value.astype(BF)
        if x_ref is not None:
            gain += jnp.sum(value * x_ref[here, :].astype(FP), axis=0, keepdims=True)
    if x_ref is not None:
        gain_ref[...] = gain


def attn_forward_kernel(widths, n_weights, spots_ref, weight_spots_ref, *rest):
    q_width, kv_width = widths
    x_pieces, rest = rest[:4], rest[4:]
    w_pieces, rest = rest[:n_weights], rest[n_weights:]
    if n_weights > 1:
        qkv_ref, heads_ref, kept_ref, sent_ref, lse_ref, w_ref, x_scr = rest
        place_rows(weight_spots_ref, w_pieces, w_ref)
    else:
        qkv_ref, heads_ref, kept_ref, sent_ref, lse_ref, x_scr = rest
        w_ref = w_pieces[0]
    place_rows(spots_ref, x_pieces, x_scr)
    rows = x_scr.shape[0]
    proj_width = q_width + 2 * kv_width
    ratio = q_width // kv_width
    tile = min(256, rows)
    qkv_ref[...] = dot_nn(x_scr[...], w_ref[:, :proj_width]).astype(BF)
    for kv in range(kv_width // HD):
        keys = qkv_ref[:, q_width + kv * HD : q_width + (kv + 1) * HD]
        values = qkv_ref[:, q_width + kv_width + kv * HD : q_width + kv_width + (kv + 1) * HD]
        cols = [slice((kv * ratio + r) * HD, (kv * ratio + r + 1) * HD) for r in range(ratio)]
        for start in range(0, rows, tile):
            stop = start + tile
            query = jnp.concatenate([qkv_ref[start:stop, c] for c in cols], axis=0) * BF(HD**-0.5)
            near = dot_nt(query, keys[start:stop])
            row_pos = lax.broadcasted_iota(jnp.int32, near.shape, 0) & (tile - 1)
            col_pos = lax.broadcasted_iota(jnp.int32, near.shape, 1)
            scores = jnp.where(col_pos <= row_pos, near, -1e30)
            if start:
                scores = jnp.concatenate([dot_nt(query, keys[:start]), scores], axis=1)
            highest = jnp.max(scores, axis=-1, keepdims=True)
            exponent = jnp.exp(scores - highest)
            total = jnp.sum(exponent, axis=-1, keepdims=True)
            logs = jnp.broadcast_to(highest + jnp.log(total), (ratio * tile, 128))
            lse_ref[pl.ds(kv * (rows // tile) + start // tile, 1), :] = logs.T[:1]
            probs = (exponent * (1.0 / total)).astype(BF)
            out = dot_nn(probs, values[:stop]).astype(BF)
            for r, c in enumerate(cols):
                heads_ref[start:stop, c] = out[r * tile : (r + 1) * tile]
    product_rows(spots_ref, heads_ref, w_ref[:, proj_width:], kept_ref, sent_ref)


def attn_backward_kernel(widths, first, spots_ref, block_spots_ref, *rest):
    q_width, kv_width = widths
    proj_width = q_width + 2 * kv_width
    dy_pieces, rest = rest[:4], list(rest[4:])
    x_pieces = [] if first else [rest.pop(0) for _ in range(4)]
    qkv_ref, heads_ref, lse_ref, w_ref = rest[:4]
    rest = rest[4:]
    x_scr = gain_ref = None
    if first:
        proj_grad_ref, kept_ref, sent_ref, dy_scr, head_grad_ref, key_acc, value_acc = rest
    else:
        earlier_ref, grads_kept_ref, grads_sent_ref, kept_ref, sent_ref, gain_ref = rest[:6]
        grads_ref, dy_scr, x_scr, head_grad_ref, proj_grad_ref, key_acc, value_acc = rest[6:]
        place_rows(spots_ref, x_pieces, x_scr)
    place_rows(spots_ref, dy_pieces, dy_scr)
    rows = dy_scr.shape[0]
    ratio = q_width // kv_width
    tile = min(256, rows)
    head_grad_ref[...] = dot_nn(dy_scr[...], w_ref[:, proj_width:]).astype(BF)
    for kv in range(kv_width // HD):
        key_cols = slice(q_width + kv * HD, q_width + (kv + 1) * HD)
        value_cols = slice(q_width + kv_width + kv * HD, q_width + kv_width + (kv + 1) * HD)
        cols = [slice((kv * ratio + r) * HD, (kv * ratio + r + 1) * HD) for r in range(ratio)]
        keys = qkv_ref[:, key_cols]
        values = qkv_ref[:, value_cols]
        key_acc[...] = jnp.zeros_like(key_acc)
        value_acc[...] = jnp.zeros_like(value_acc)
        for start in range(0, rows, tile):
            stop = start + tile
            query = jnp.concatenate([qkv_ref[start:stop, c] for c in cols], axis=0) * BF(HD**-0.5)
            out_grad = jnp.concatenate([head_grad_ref[start:stop, c] for c in cols], axis=0)
            near = dot_nt(keys[start:stop], query)
            key_pos = lax.broadcasted_iota(jnp.int32, near.shape, 0)
            row_pos = lax.broadcasted_iota(jnp.int32, near.shape, 1) & (tile - 1)
            scores = jnp.where(key_pos <= row_pos, near, -1e30)
            if start:
                scores = jnp.concatenate([dot_nt(keys[:start], query), scores], axis=0)
            probs = jnp.exp(scores - lse_ref[pl.ds(kv * (rows // tile) + start // tile, 1), :])
            prob_grad = dot_nt(values[:stop], out_grad)
            inner = jnp.sum(probs * prob_grad, axis=0, keepdims=True)
            score_grad = (probs * (prob_grad - inner)).astype(BF)
            value_acc[:stop] += dot_nn(probs.astype(BF), out_grad)
            key_acc[:stop] += dot_nn(score_grad, query)
            query_grad = (dot_tn(score_grad, keys[:stop]) * (HD**-0.5)).astype(BF)
            for r, c in enumerate(cols):
                proj_grad_ref[start:stop, c] = query_grad[r * tile : (r + 1) * tile]
        proj_grad_ref[:, key_cols] = key_acc[...].astype(BF)
        proj_grad_ref[:, value_cols] = value_acc[...].astype(BF)
    product_rows(spots_ref, proj_grad_ref, w_ref[:, :proj_width], kept_ref, sent_ref, x_scr, gain_ref)
    if first:
        return
    grads_ref[:, :proj_width] = earlier_ref[:, :proj_width] + dot_tn(x_scr[...], proj_grad_ref[...])
    grads_ref[:, proj_width:] = earlier_ref[:, proj_width:] + dot_tn(dy_scr[...], heads_ref[...])
    depth, blk, _ = grads_kept_ref.shape
    for r in range(depth):
        here = pl.ds(pl.multiple_of(block_spots_ref[r] * blk, blk), blk)
        grads_kept_ref[r] = grads_ref[here, :]
        here = pl.ds(pl.multiple_of(block_spots_ref[depth + r] * blk, blk), blk)
        grads_sent_ref[r] = grads_ref[here, :].astype(BF)


def attn_weights_kernel(proj_width, spots_ref, *rest):
    dy_pieces, x_pieces, rest = rest[:4], rest[4:8], rest[8:]
    heads_ref, proj_grad_ref, w_ref, grads_ref, gain_ref, dy_scr, x_scr = rest
    place_rows(spots_ref, dy_pieces, dy_scr)
    place_rows(spots_ref, x_pieces, x_scr)
    proj_part = dot_tn(x_scr[...], proj_grad_ref[...])
    grads_ref[:, :proj_width] = proj_part
    grads_ref[:, proj_width:] = dot_tn(dy_scr[...], heads_ref[...])
    products = proj_part * w_ref[:, :proj_width].astype(FP)
    gain_ref[...] = jnp.sum(products, axis=1, keepdims=True)


def attn_weights(spots, dy, x, heads, proj_grad, weights):
    rows, model_width = x[0].shape
    return pl.pallas_call(
        functools.partial(attn_weights_kernel, proj_grad.shape[1]),
        in_specs=[SMEM] + [VMEM] * 11,
        out_specs=[VMEM] * 2,
        out_shape=[
            jax.ShapeDtypeStruct((model_width, weights.shape[1]), FP),
            jax.ShapeDtypeStruct((model_width, 1), FP),
        ],
        scratch_shapes=[pltpu.VMEM((4 * rows, model_width), BF)] * 2,
        compiler_params=pltpu.CompilerParams(vmem_limit_bytes=56 << 20),
        cost_estimate=cost(4 << 30),
    )(spots, *dy, *x, heads, proj_grad, weights)


def attn_forward(spots, weight_spots, pieces, weights, widths):
    rows, model_width = pieces[0].shape
    width = weights[0].shape[1]
    whole = len(weights) == 1
    tile = min(256, 4 * rows)
    stats = (widths[1] // HD * (4 * rows // tile), widths[0] // widths[1] * tile)
    outs = [
        jax.ShapeDtypeStruct((4 * rows, widths[0] + 2 * widths[1]), BF),
        jax.ShapeDtypeStruct((4 * rows, widths[0]), BF),
        jax.ShapeDtypeStruct((2, rows, model_width), FP),
        jax.ShapeDtypeStruct((2, rows, model_width), BF),
        jax.ShapeDtypeStruct(stats, FP),
    ] + ([] if whole else [jax.ShapeDtypeStruct((model_width, width), BF)])
    results = pl.pallas_call(
        functools.partial(attn_forward_kernel, widths, len(weights)),
        in_specs=[SMEM] * 2 + [VMEM] * (4 + len(weights)),
        out_specs=[VMEM] * len(outs),
        out_shape=outs,
        scratch_shapes=[pltpu.VMEM((4 * rows, model_width), BF)],
        compiler_params=pltpu.CompilerParams(vmem_limit_bytes=56 << 20),
        cost_estimate=cost(14 << 30),
    )(spots, weight_spots, *pieces, *weights)
    return results if not whole else [*results, weights[0]]


def attn_backward(spots, block_spots, dy, x, qkv, heads, lse, weights, earlier, widths):
    rows, model_width = x[0].shape
    width = weights.shape[1]
    first = earlier is None
    operands = [*dy] + ([] if first else [*x]) + [qkv, heads, lse, weights]
    operands += [] if first else [earlier]
    depth = block_spots.shape[0] // 2
    whole = (model_width, width)
    blocks = (depth, model_width // depth // 2, width)
    placed = pltpu.VMEM((4 * rows, model_width), BF)
    proj_shape = (4 * rows, widths[0] + 2 * widths[1])
    sums = [pltpu.VMEM((4 * rows, HD), FP)] * 2
    outs = [jax.ShapeDtypeStruct((2, rows, model_width), t) for t in (FP, BF)]
    if first:
        outs = [jax.ShapeDtypeStruct(proj_shape, BF)] + outs
        scratch = [placed, pltpu.VMEM(heads.shape, BF), *sums]
    else:
        outs = [jax.ShapeDtypeStruct(blocks, FP), jax.ShapeDtypeStruct(blocks, BF)] + outs
        outs += [jax.ShapeDtypeStruct((1, model_width), FP)]
        scratch = [pltpu.VMEM(whole, FP), placed, placed, pltpu.VMEM(heads.shape, BF)]
        scratch += [pltpu.VMEM(proj_shape, BF), *sums]
    return pl.pallas_call(
        functools.partial(attn_backward_kernel, widths, first),
        in_specs=[SMEM] * 2 + [VMEM] * len(operands),
        out_specs=[VMEM] * len(outs),
        out_shape=outs,
        scratch_shapes=scratch,
        compiler_params=pltpu.CompilerParams(vmem_limit_bytes=58 << 20),
        cost_estimate=cost(1 << 24),
    )(spots, block_spots, *operands)


def on_device(
    block_input,
    cotangent,
    routes,
    gate_weights,
    w_query,
    w_key,
    w_value,
    w_out,
    w_gate_up,
    w_down,
    norm_attn,
    norm_moe,
):
    depth = lax.axis_size("z")
    micro_count, rows_local, model_width = block_input.shape
    q_width, kv_width = w_query.shape[1], w_key.shape[1]
    widths = (q_width, kv_width)
    proj_width = q_width + 2 * kv_width
    side, chip, core = lax.axis_index("y"), lax.axis_index("x"), lax.axis_index("c")
    side_at = side.astype(jnp.int32).reshape(1)
    spots = jnp.stack([2 * x + c for c in (core, 1 - core) for x in (chip, 1 - chip)])
    spots = spots.astype(jnp.int32)
    place = lax.axis_index("z")
    block_spots = jnp.stack(
        [2 * lax.rem(place + r, depth) + s for s in (side, 1 - side) for r in range(depth)]
    ).astype(jnp.int32)

    packed_attn = pack_attn(w_query, w_key, w_value, w_out)
    packed = pack_experts(after(side_at, packed_attn), w_gate_up, w_down)
    in_rows = after(block_input, packed[0][1]).astype(FP)
    normed_attn, scale_attn = row_norm(in_rows, norm_attn)
    normed = [normed_attn[m].astype(BF) for m in range(micro_count)]
    cots = [cotangent[m] for m in range(micro_count)]

    def shard_of(chunk, got):
        mine = packed[chunk][0]
        first = side == 0
        return jnp.stack([jnp.where(first, mine, got), jnp.where(first, got, mine)])

    def whole_of(shard):
        whole = lax.all_gather(shard, "z", axis=0)
        return whole.reshape(-1, *whole.shape[2:])

    column, places = along_z(packed_attn, depth)
    weight_spots = jnp.stack([2 * z + s for s in (side, 1 - side) for z in places])
    weight_spots = weight_spots.astype(jnp.int32)
    across = swap(normed[0], "x")
    got = swap(packed[0][1], "y")
    own_across = swap(packed_attn, "y")
    *column, across, got = together(*column, across, got)
    shards = [shard_of(0, got)]
    chunk_weights = [whole_of(shards[0])]
    *column, across, next_normed, cot, _ = together(
        *column, across, normed[1], cots[0], shards[0]
    )

    weights = column + [own_across] + [swap(piece, "y") for piece in column[1:]]
    near_rows, far_rows = swap(normed[0], "c"), swap(across, "c")
    next_across, cot_across = swap(next_normed, "x"), swap(cot, "x")
    *weights, near_rows, far_rows, cot, next_across = together(
        *weights, near_rows, far_rows, cots[0], next_across
    )
    attn_in = [[normed[0], across, near_rows, far_rows]]

    cot_diagonal = cross(cot)
    turn = after(spots, shards[0])
    qkv, heads, kept, sent, lse, whole = attn_forward(
        turn, weight_spots, attn_in[0], weights, widths
    )
    weights = [whole]
    saved = [(qkv, heads, lse)]
    sent, cot_diagonal, cot_across, across = together(
        sent, cot_diagonal, cot_across, next_across
    )

    got = swap(sent, "c")
    near_rows, far_rows = swap(normed[1], "c"), swap(across, "c")
    along = plus(kept[1], got[1]).astype(BF)
    own = plus(kept[0], got[0])
    along, near_rows, far_rows, cot, turn = together(along, near_rows, far_rows, cots[0], spots)
    attn_in.append([normed[1], across, near_rows, far_rows])

    expert_ids = jnp.arange(E, dtype=jnp.int32)[:, None, None, None]
    gates = jnp.sum(jnp.where(routes == expert_ids, gate_weights, 0.0), axis=3)
    gates = gates.reshape(2, E // 2, micro_count, 2, 2, rows_local)
    gates = jnp.where(chip == 0, gates, gates[:, :, :, ::-1])
    gates = jnp.where(core == 0, gates, gates[:, :, :, :, ::-1])
    mine = lax.dynamic_index_in_dim(gates, side, 0, False)
    other = lax.dynamic_index_in_dim(gates, 1 - side, 0, False)
    other = after(other.reshape(E // 2, -1), along)
    came, cot_near, gates_got = swap(along, "x"), swap(cot, "y"), swap(other, "y")
    qkv, heads, kept, sent, lse, _ = attn_forward(
        turn, weight_spots, attn_in[1], weights, widths
    )
    saved.append((qkv, heads, lse))
    sent, came, cot_near, gates_got = together(sent, came, cot_near, gates_got)

    def moe_rows(middle):
        normed, scale = row_norm(middle, norm_moe)
        return normed.astype(BF), scale

    got = swap(sent, "c")
    middle = [in_rows[0] + plus(own, came)]
    low, scale = moe_rows(middle[0])
    normed, scale_moe = [low], [scale]
    along = plus(kept[1], got[1]).astype(BF)
    own = plus(kept[0], got[0])
    along, low = together(along, low)

    near, across, diagonal = to_neighbours([low] * 3)
    gates = jnp.stack([mine, gates_got.reshape(mine.shape)])
    gates = gates.transpose(2, 3, 0, 4, 5, 1).reshape(micro_count, 4, 2, rows_local, E // 2)
    near, across, diagonal, gates, along, theirs = together(
        near, across, diagonal, gates, along, packed[1][1]
    )

    came, theirs = swap(along, "x"), swap(theirs, "y")
    blocks = stacked(
        [normed[0], cots[0], near, cot_near, across, cot_across, diagonal, cot_diagonal]
    )
    experts_in = [(blocks, swap(blocks, "c"))]
    came, theirs, blocks = together(came, theirs, blocks)
    middle.append(in_rows[1] + plus(own, came))
    low, scale = moe_rows(middle[1])
    normed.append(low)
    scale_moe.append(scale)
    pair = stacked([low, cots[1]])
    shards.append(shard_of(1, theirs))
    chunk_weights.append(whole_of(shards[1]))
    neighbours = to_neighbours([pair] * 3)

    sums = [None] * micro_count
    turn = after(side_at, shards[1], pair)
    all_grads = []
    first_expert = 0
    for chunk, count in enumerate(CHUNKS):
        last = chunk == len(CHUNKS) - 1
        grads = None
        for m in range(micro_count):
            sums[m], grads = moe_chunk(
                turn,
                experts_in[m],
                gates,
                chunk_weights[chunk],
                sums[m],
                grads,
                m,
                first_expert,
                last,
            )
            waited = [grads]
            if m == 0 and chunk == 0:
                *neighbours, _ = together(*neighbours, grads)
                blocks = stacked([pair, *neighbours])
                blocks = blocks.reshape(-1, *blocks.shape[2:])
                experts_in.append((blocks, swap(blocks, "c")))
            if m == 0 and last:
                mixed_own, mixed_along = half_sums(*sums[0][:2])
                own, along = half_sums(*sums[0][2:])
                along = [jnp.stack(both) for both in zip(along, mixed_along)]
                *along, turn, _ = together(*along, side_at, *waited)
                came = to_neighbours(along)
            else:
                turn = after(side_at, *waited)
        first_expert += count
        all_grads.append(grads.reshape(depth, 2, *grads.shape[1:]))

    def reduce_grads(grads):
        return lax.psum_scatter(grads, "z", scatter_dimension=0, tiled=False)

    grad_shards = [reduce_grads(all_grads[0])]

    def middle_back(m, own, came):
        moe_in_grad = sum_of(own, came)
        back = norm_back(middle[m], scale_moe[m], norm_moe, moe_in_grad)
        gain = jnp.sum(moe_in_grad * middle[m] * scale_moe[m], axis=0)
        grad = cots[m].astype(FP) + back
        return grad, grad.astype(BF), gain

    def input_back(m, middle_grad, own, came):
        return middle_grad + norm_back(in_rows[m], scale_attn[m], norm_attn, plus(own, came))

    def backward(m, turn, rows, earlier):
        return attn_backward(
            turn, block_spots, rows, attn_in[m], *saved[m], weights[0], earlier, widths
        )

    *came, grads, kept, sent, last_mixed_kept, last_mixed_sent, first_shard = together(
        *came, all_grads[1], sums[1][2], sums[1][3], *sums[1][:2], grad_shards[0]
    )
    grad_shards = [first_shard, reduce_grads(grads)]
    first_came, first_mixed_own = came, mixed_own
    middle_grad, low, gain_moe = middle_back(0, own, [c[0] for c in came])
    across, near_rows = swap(low, "x"), swap(low, "c")
    last_mixed_sent, sent, _ = together(last_mixed_sent, sent, low)
    own, along = half_sums(kept, sent)
    mixed_own, mixed_along = half_sums(last_mixed_kept, last_mixed_sent)
    came = to_neighbours(along)
    across, near_rows, came[:2], mixed_along = together(across, near_rows, came[:2], mixed_along)
    far_rows = swap(across, "c")
    rows = [low, across, near_rows, far_rows]
    results = backward(0, spots, rows, None)
    *came, proj_grad, kept, sent, first_shard = together(*came, *results, first_shard)
    earlier, gain_attn = attn_weights(
        spots, rows, attn_in[0], saved[0][1], proj_grad, weights[0]
    )

    middle_grads = [middle_grad]
    middle_grad, low, gain = middle_back(1, own, came)
    middle_grads.append(middle_grad)
    gain_moe = gain_moe + gain
    across, near_rows = swap(low, "x"), swap(low, "c")
    input_own, input_along = half_sums(kept, sent)
    shard_got = [swap(first_shard[1], "y")]
    across, near_rows, shard_got[0], input_along, earlier, *mixed_along = together(
        across, near_rows, shard_got[0], *input_along, earlier, *mixed_along
    )
    far_rows = swap(across, "c")
    input_came = swap(input_along, "x")
    mixed_came = [swap(mixed_along[0], "y"), cross(mixed_along[2])]
    results = backward(1, spots, [low, across, near_rows, far_rows], earlier)
    input_came, gain_attn, (mixed_came, results, first_came) = together(
        input_came, gain_attn, (mixed_came, results, first_came)
    )
    grads_kept, grads_sent, kept, sent, gain = results

    gains = jnp.concatenate([(gain_attn[:, 0] + gain[0]) / norm_attn, gain_moe]).reshape(16, -1)
    grads_got = swap(grads_sent, "y")
    own, along = half_sums(kept, sent)
    first_input = input_back(0, middle_grads[0], input_own, input_came)
    outputs = [(middle[0] + sum_of(first_mixed_own, [c[1] for c in first_came])).astype(BF)]
    mixed_came.append(swap(mixed_along[1], "x"))
    gains = sum_over_z(gains + swap(gains, "c"), depth)
    gains, mixed_came[2] = together(gains, mixed_came[2])
    gains = gains + swap(gains, "x")
    column = grads_kept + grads_got.astype(FP)
    along, gains, first_input, outputs[0], column, last_shard, mixed_own = together(
        along[0], gains, first_input, outputs[0], column, grad_shards[1], mixed_own
    )
    input_came = swap(along, "x")
    last_sent, column = together(last_shard[1], column)
    shard_got.append(swap(last_sent, "y"))
    pieces = along_z_sent(column, depth)
    last_input = input_back(1, middle_grads[1], own, input_came)
    outputs.append((middle[1] + sum_of(mixed_own, mixed_came)).astype(BF))
    last_input, outputs[1], shard_got[1], gains, *pieces = together(
        last_input, outputs[1], shard_got[1], gains, *pieces
    )
    gains = (gains + swap(gains, "y")).reshape(2, model_width)
    shard_pair, shard_down = unpack_experts(
        side_at, w_down.shape[1], list(zip([grad_shards[0], last_shard], shard_got))
    )
    attn_shard = sum_of(column[0], pieces)
    input_grads = [first_input, last_input]
    return (
        jnp.stack(outputs),
        jnp.stack(input_grads),
        attn_shard[:, :q_width],
        attn_shard[:, q_width : q_width + kv_width],
        attn_shard[:, q_width + kv_width : proj_width],
        attn_shard[:, proj_width:].T,
        shard_pair,
        shard_down,
        gains[0],
        gains[1],
    )


def solution(mesh):
    dp, tensor = mesh.shape["dp"], mesh.shape["tensor"]
    fine = Mesh(mesh.devices.reshape(dp // 2, 2, tensor // 2, 2), ("z", "y", "x", "c"))
    dp_axes, tensor_axes = ("z", "y"), ("x", "c")
    rows = P(None, dp_axes + tensor_axes, None)
    return jax.shard_map(
        on_device,
        mesh=fine,
        in_specs=(
            rows,
            rows,
            P(None, dp_axes, None),
            P(None, dp_axes, None),
            P(dp_axes, tensor_axes),
            P(dp_axes, tensor_axes),
            P(dp_axes, tensor_axes),
            P(tensor_axes, dp_axes),
            P(None, dp_axes, None, tensor_axes),
            P(None, tensor_axes, dp_axes),
            P(),
            P(),
        ),
        out_specs=(
            rows,
            rows,
            P(dp_axes, tensor_axes),
            P(dp_axes, tensor_axes),
            P(dp_axes, tensor_axes),
            P(tensor_axes, dp_axes),
            P(None, dp_axes, None, tensor_axes),
            P(None, tensor_axes, dp_axes),
            P(),
            P(),
        ),
        check_vma=False,
    )
```

```python
import functools

import jax
import jax.numpy as jnp
from jax import lax
from jax.experimental import pallas as pl
from jax.experimental.pallas import tpu as pltpu
from jax.sharding import Mesh
from jax.sharding import PartitionSpec as P

HD = 64
E = 32
CHUNKS = (8, 8)

EPSILON = 1e-06
BF = jnp.bfloat16
FP = jnp.float32


def dot_nn(left, right):
    return lax.dot_general(left, right, (((1,), (0,)), ((), ())), preferred_element_type=FP)


def dot_tn(left, right):
    return lax.dot_general(left, right, (((0,), (0,)), ((), ())), preferred_element_type=FP)


def dot_nt(left, right):
    return lax.dot_general(left, right, (((1,), (1,)), ((), ())), preferred_element_type=FP)


def row_norm(in_rows, gain_vec):
    row_scale = lax.rsqrt(jnp.mean(in_rows * in_rows, axis=-1, keepdims=True) + EPSILON)
    return (in_rows * row_scale * gain_vec, row_scale)


def norm_back(in_rows, row_scale, gain_vec, grad_in):
    weighted = grad_in * gain_vec
    inner = jnp.mean(weighted * in_rows, axis=-1, keepdims=True)
    return row_scale * weighted - in_rows * row_scale * row_scale * row_scale * inner


def swap(value, axis):
    return lax.ppermute(value, axis, [(0, 1), (1, 0)])


def after(value, *earlier):
    return lax.optimization_barrier((value, *earlier))[0]


def together(*values):
    return lax.optimization_barrier(values)


def cross(value):
    return lax.ppermute(value, ("y", "x"), [(i, 3 - i) for i in range(4)])


def to_neighbours(rows):
    return [swap(rows[0], "y"), swap(rows[1], "x"), cross(rows[2])]


def plus(left, right):
    return left + right.astype(FP)


def half_sums(kept, sent):
    got = swap(sent, "c")
    low = [plus(kept[i], got[i]).astype(BF) for i in range(1, kept.shape[0])]
    return plus(kept[0], got[0]), low


def sum_of(total, parts):
    for part in parts:
        total = plus(total, part)
    return total


def along_z(shard, depth):
    place = lax.axis_index("z")
    turns_taken = [k for k in range(-((depth - 1) // 2), depth // 2 + 1) if k]
    pieces = [shard]
    for k in turns_taken:
        pieces.append(lax.ppermute(shard, "z", [(i, (i + k) % depth) for i in range(depth)]))
    return pieces, [lax.rem(place + depth - k, depth) for k in [0, *turns_taken]]


def along_z_sent(column, depth):
    return [
        lax.ppermute(column[r].astype(BF), "z", [(i, (i + r) % depth) for i in range(depth)])
        for r in range(1, depth)
    ]


def sum_over_z(value, depth):
    reach = 1
    while reach < depth:
        pairs = [(i, i ^ reach) for i in range(depth)]
        value = value + lax.ppermute(value, "z", pairs)
        reach *= 2
    return value


def cost(flops):
    return pl.CostEstimate(flops=flops, bytes_accessed=1 << 20, transcendentals=0)


SMALL = cost(1 << 30)
SMEM = pl.BlockSpec(memory_space=pltpu.SMEM)
VMEM = pl.BlockSpec(memory_space=pltpu.VMEM)


def stack_kernel(*refs):
    *ins, out_ref, sems = refs
    copies = [pltpu.make_async_copy(ref, out_ref.at[i], sems.at[i]) for i, ref in enumerate(ins)]
    for copy in copies:
        copy.start()
    for copy in copies:
        copy.wait()


def stacked(arrays):
    return pl.pallas_call(
        stack_kernel,
        in_specs=[pl.BlockSpec(memory_space=pl.ANY)] * len(arrays),
        out_specs=VMEM,
        out_shape=jax.ShapeDtypeStruct((len(arrays), *arrays[0].shape), arrays[0].dtype),
        scratch_shapes=[pltpu.SemaphoreType.DMA((len(arrays),))],
        compiler_params=pltpu.CompilerParams(vmem_limit_bytes=32 << 20),
        cost_estimate=cost(1 << 30),
    )(*arrays)


def pack_kernel(side_ref, gate_up_ref, down_ref, *rest):
    *outs, rows_scr = rest
    hidden_local, blk = down_ref.shape[1:]
    offset = 0
    for mine_ref, theirs_ref in zip(outs[::2], outs[1::2]):
        count = mine_ref.shape[1] // (3 * hidden_local)
        for out_ref, half in ((theirs_ref, 1 - side_ref[0]), (mine_ref, side_ref[0])):
            for i in range(count):
                expert = half * (E // 2) + offset + i
                rows_scr[...] = gate_up_ref[expert].astype(FP)
                values = [rows_scr[pl.ds(part, blk, stride=2), :] for part in range(2)]
                values.append(down_ref[expert].astype(FP).T)
                for part, value in enumerate(values):
                    start = (part * count + i) * hidden_local
                    out_ref[:, start : start + hidden_local] = value.astype(BF)
        offset += count


def pack_experts(side, w_gate_up, w_down):
    experts, blk, _, hidden_local = w_gate_up.shape
    shapes = [jax.ShapeDtypeStruct((blk, 3 * count * hidden_local), BF) for count in CHUNKS]
    outs = pl.pallas_call(
        pack_kernel,
        in_specs=[SMEM, VMEM, VMEM],
        out_specs=[VMEM] * (2 * len(CHUNKS)),
        out_shape=[shape for shape in shapes for _ in range(2)],
        scratch_shapes=[pltpu.VMEM((2 * blk, hidden_local), FP)],
        compiler_params=pltpu.CompilerParams(vmem_limit_bytes=32 << 20),
        cost_estimate=SMALL,
    )(side, w_gate_up.reshape(experts, 2 * blk, hidden_local), w_down)
    return list(zip(outs[::2], outs[1::2]))


def unpack_kernel(side_ref, *refs):
    *ins, gate_up_ref, down_ref = refs
    hidden_local, blk = down_ref.shape[1:]
    offset = 0
    for kept_ref, got_ref in zip(ins[::2], ins[1::2]):
        count = got_ref.shape[1] // (3 * hidden_local)
        for mine, half in ((True, side_ref[0]), (False, 1 - side_ref[0])):
            for i in range(count):
                expert = half * (E // 2) + offset + i
                values = []
                for part in range(3):
                    start = (part * count + i) * hidden_local
                    cols = slice(start, start + hidden_local)
                    values.append((kept_ref[0, :, cols] if mine else got_ref[:, cols]).astype(FP))
                for part in range(2):
                    gate_up_ref[expert, pl.ds(part, blk, stride=2), :] = values[part]
                down_ref[expert] = values[2].T
        offset += count


def unpack_experts(side, hidden_local, shards):
    blk = shards[0][1].shape[0]
    operands = [array for shard in shards for array in shard]
    gate_up, down = pl.pallas_call(
        unpack_kernel,
        in_specs=[SMEM] + [VMEM] * len(operands),
        out_specs=[VMEM, VMEM],
        out_shape=[
            jax.ShapeDtypeStruct((E, 2 * blk, hidden_local), FP),
            jax.ShapeDtypeStruct((E, hidden_local, blk), FP),
        ],
        compiler_params=pltpu.CompilerParams(vmem_limit_bytes=32 << 20),
        cost_estimate=SMALL,
    )(side, *operands)
    return gate_up.reshape(E, blk, 2, hidden_local), down


def pack_attn_kernel(query_ref, key_ref, value_ref, out_ref, packed_ref):
    start = 0
    for ref in (query_ref, key_ref, value_ref):
        packed_ref[:, start : start + ref.shape[1]] = ref[...]
        start += ref.shape[1]
    packed_ref[:, start:] = out_ref[...].astype(FP).T.astype(BF)


def pack_attn(w_query, w_key, w_value, w_out):
    width = w_query.shape[1] + w_key.shape[1] + w_value.shape[1] + w_out.shape[0]
    return pl.pallas_call(
        pack_attn_kernel,
        in_specs=[VMEM] * 4,
        out_specs=VMEM,
        out_shape=jax.ShapeDtypeStruct((w_query.shape[0], width), BF),
        cost_estimate=SMALL,
    )(w_query, w_key, w_value, w_out)


def moe_kernel(first, last, start, column, side_ref, xa_ref, xb_ref, ga_ref, gb_ref, gate_ref, w_ref, *rest):
    rest = list(rest)
    sums_in = [] if first else [rest.pop(0), rest.pop(0)]
    earlier_ref = None if start else rest.pop(0)
    sums_out, (grads_ref, acc, hidden_scr, pair_scr, sem) = rest[:-5], rest[-5:]
    step = pl.program_id(0)
    blocks, blk, width = w_ref.shape
    third = width // 3
    hidden_local = third // CHUNKS[0]
    part = min(2 * hidden_local, third)

    def spot(block):
        place = (block // 2) * 2 + (side_ref[0] + block % 2) % 2
        return pl.ds(pl.multiple_of(place * blk, blk), blk)

    @pl.when(step == 0)
    def _():
        if not start:
            pltpu.make_async_copy(earlier_ref, grads_ref, sem).start()
        acc[...] = jnp.zeros_like(acc)

    x = jnp.concatenate([xa_ref[...], xb_ref[...]], axis=0)
    g = jnp.concatenate([ga_ref[...], gb_ref[...]], axis=0)
    gates = gate_ref[...].reshape(x.shape[0], gate_ref.shape[-1])
    weights = w_ref.reshape(blocks * blk, width)
    for p in range(0, third, part):
        own, up_cols = slice(p, p + part), slice(third + p, third + p + part)
        gate = dot_nn(x, weights[:, own])
        up = dot_nn(x, weights[:, up_cols])
        out_back = dot_nn(g, weights[:, 2 * third + p : 2 * third + p + part])
        sig = 0.5 + 0.5 * jnp.tanh(0.5 * gate)
        share = jnp.concatenate(
            [
                jnp.broadcast_to(gates[:, i : i + 1], (x.shape[0], hidden_local))
                for i in range(column + p // hidden_local, column + (p + part) // hidden_local)
            ],
            axis=1,
        )
        silu = gate * sig
        hidden_grad = share * out_back
        hidden_scr[:, own] = (share * (silu * up)).astype(BF)
        pair_scr[:, own] = (hidden_grad * up * (sig + silu * (1.0 - sig))).astype(BF)
        pair_scr[:, up_cols] = (hidden_grad * silu).astype(BF)
    hidden = hidden_scr[...]
    pair_grad = pair_scr[...]
    totals = [
        dot_nt(hidden, weights[:, 2 * third :]),
        dot_nt(pair_grad, weights[:, : 2 * third]),
    ]
    acc[:, : 2 * third] += dot_tn(x, pair_grad)
    acc[:, 2 * third :] += dot_tn(g, hidden)
    if not first:
        totals = [s[...].reshape(t.shape) + t for s, t in zip(sums_in, totals)]
    if last:
        rows = xa_ref.shape[0]
        for kept_ref, sent_ref, total in zip(sums_out[::2], sums_out[1::2], totals):
            kept_ref[...] = total[:rows]
            sent_ref[...] = total[rows:].astype(BF)
    else:
        for out_ref, total in zip(sums_out, totals):
            out_ref[...] = total.reshape(out_ref.shape)

    @pl.when(step == pl.num_programs(0) - 1)
    def _():
        if not start:
            pltpu.make_async_copy(earlier_ref, grads_ref, sem).wait()
        for block in range(blocks):
            value = acc[spot(block), :]
            if not start:
                value = value + grads_ref[block].astype(FP)
            grads_ref[block] = value.astype(BF)


def moe_chunk(side, rows_in, gates, weights, sums, earlier, micro, column, last):
    count, rows, model_width = rows_in[0].shape
    count //= 2
    blocks, blk, width = weights.shape
    once = pl.Buffered(1)
    tile = min(128, rows)
    parts = rows // tile
    row = pl.BlockSpec((None, 2, tile, model_width), lambda i: (i // parts, 0, i % parts, 0))
    half = pl.BlockSpec((None, tile, model_width), lambda i: (i // parts, i % parts, 0))
    x_half = pl.BlockSpec((None, tile, model_width), lambda i: (2 * (i // parts), i % parts, 0))
    g_half = pl.BlockSpec((None, tile, model_width), lambda i: (2 * (i // parts) + 1, i % parts, 0))
    gate_spec = pl.BlockSpec(
        (None, None, 2, tile, gates.shape[-1]), lambda i: (micro, i // parts, 0, i % parts, 0)
    )
    whole = pl.BlockSpec(weights.shape, lambda i: (0, 0, 0), pipeline_mode=once)
    first, start = sums is None, earlier is None
    operands = [side, *rows_in, *rows_in, gates, weights] + ([] if first else list(sums))
    operands += [] if start else [earlier]
    if last:
        out_specs = [half] * 4
        outs = [jax.ShapeDtypeStruct((count, rows, model_width), t) for t in (FP, BF, FP, BF)]
    else:
        out_specs = [row] * 2
        outs = [jax.ShapeDtypeStruct((count, 2, rows, model_width), FP)] * 2
    *sums, grads = pl.pallas_call(
        functools.partial(moe_kernel, first, last, start, column),
        grid=(count * parts,),
        in_specs=[SMEM, x_half, x_half, g_half, g_half, gate_spec, whole]
        + ([] if first else [row, row])
        + ([] if start else [pl.BlockSpec(memory_space=pl.ANY)]),
        out_specs=out_specs + [whole],
        scratch_shapes=[
            pltpu.VMEM((model_width, width), FP),
            pltpu.VMEM((2 * tile, width // 3), BF),
            pltpu.VMEM((2 * tile, 2 * width // 3), BF),
            pltpu.SemaphoreType.DMA,
        ],
        out_shape=outs + [jax.ShapeDtypeStruct(weights.shape, BF)],
        input_output_aliases={} if first or last else {7: 0, 8: 1},
        compiler_params=pltpu.CompilerParams(vmem_limit_bytes=60 << 20),
        cost_estimate=cost(6 << 30),
    )(*operands)
    return sums, grads


def place_rows(spots_ref, pieces, whole_ref):
    rows = pieces[0].shape[0]
    for i, piece in enumerate(pieces):
        whole_ref[pl.ds(pl.multiple_of(spots_ref[i] * rows, rows), rows), :] = piece[...]


def product_rows(spots_ref, left_ref, right, kept_ref, sent_ref, x_ref=None, gain_ref=None):
    rows = kept_ref.shape[1]
    gain = 0.0
    for i in range(4):
        here = pl.ds(pl.multiple_of(spots_ref[i] * rows, rows), rows)
        value = dot_nt(left_ref[here, :], right)
        if i < 2:
            kept_ref[i] = value
        else:
            sent_ref[i - 2] = value.astype(BF)
        if x_ref is not None:
            gain += jnp.sum(value * x_ref[here, :].astype(FP), axis=0, keepdims=True)
    if x_ref is not None:
        gain_ref[...] = gain


def attn_forward_kernel(widths, n_weights, spots_ref, weight_spots_ref, *rest):
    q_width, kv_width = widths
    x_pieces, rest = rest[:4], rest[4:]
    w_pieces, rest = rest[:n_weights], rest[n_weights:]
    if n_weights > 1:
        qkv_ref, heads_ref, kept_ref, sent_ref, lse_ref, w_ref, x_scr = rest
        place_rows(weight_spots_ref, w_pieces, w_ref)
    else:
        qkv_ref, heads_ref, kept_ref, sent_ref, lse_ref, x_scr = rest
        w_ref = w_pieces[0]
    place_rows(spots_ref, x_pieces, x_scr)
    rows = x_scr.shape[0]
    proj_width = q_width + 2 * kv_width
    ratio = q_width // kv_width
    tile = min(512, rows)
    qkv_ref[...] = dot_nn(x_scr[...], w_ref[:, :proj_width]).astype(BF)
    for kv in range(kv_width // HD):
        keys = qkv_ref[:, q_width + kv * HD : q_width + (kv + 1) * HD]
        values = qkv_ref[:, q_width + kv_width + kv * HD : q_width + kv_width + (kv + 1) * HD]
        cols = [slice((kv * ratio + r) * HD, (kv * ratio + r + 1) * HD) for r in range(ratio)]
        for start in range(0, rows, tile):
            stop = start + tile
            query = jnp.concatenate([qkv_ref[start:stop, c] for c in cols], axis=0) * BF(HD**-0.5)
            near = dot_nt(query, keys[start:stop])
            row_pos = lax.broadcasted_iota(jnp.int32, near.shape, 0) & (tile - 1)
            col_pos = lax.broadcasted_iota(jnp.int32, near.shape, 1)
            scores = jnp.where(col_pos <= row_pos, near, -1e30)
            if start:
                scores = jnp.concatenate([dot_nt(query, keys[:start]), scores], axis=1)
            highest = jnp.max(scores, axis=-1, keepdims=True)
            exponent = jnp.exp(scores - highest)
            total = jnp.sum(exponent, axis=-1, keepdims=True)
            logs = jnp.broadcast_to(highest + jnp.log(total), (ratio * tile, 128))
            lse_ref[pl.ds(kv * (rows // tile) + start // tile, 1), :] = logs.T[:1]
            probs = (exponent * (1.0 / total)).astype(BF)
            out = dot_nn(probs, values[:stop]).astype(BF)
            for r, c in enumerate(cols):
                heads_ref[start:stop, c] = out[r * tile : (r + 1) * tile]
    product_rows(spots_ref, heads_ref, w_ref[:, proj_width:], kept_ref, sent_ref)


def attn_backward_kernel(widths, first, spots_ref, block_spots_ref, *rest):
    q_width, kv_width = widths
    proj_width = q_width + 2 * kv_width
    dy_pieces, rest = rest[:4], list(rest[4:])
    x_pieces = [] if first else [rest.pop(0) for _ in range(4)]
    qkv_ref, heads_ref, lse_ref, w_ref = rest[:4]
    rest = rest[4:]
    x_scr = gain_ref = None
    if first:
        proj_grad_ref, kept_ref, sent_ref, dy_scr, head_grad_ref, key_acc, value_acc = rest
    else:
        earlier_ref, grads_kept_ref, grads_sent_ref, kept_ref, sent_ref, gain_ref = rest[:6]
        grads_ref, dy_scr, x_scr, head_grad_ref, proj_grad_ref, key_acc, value_acc = rest[6:]
        place_rows(spots_ref, x_pieces, x_scr)
    place_rows(spots_ref, dy_pieces, dy_scr)
    rows = dy_scr.shape[0]
    ratio = q_width // kv_width
    tile = min(512, rows)
    head_grad_ref[...] = dot_nn(dy_scr[...], w_ref[:, proj_width:]).astype(BF)
    for kv in range(kv_width // HD):
        key_cols = slice(q_width + kv * HD, q_width + (kv + 1) * HD)
        value_cols = slice(q_width + kv_width + kv * HD, q_width + kv_width + (kv + 1) * HD)
        cols = [slice((kv * ratio + r) * HD, (kv * ratio + r + 1) * HD) for r in range(ratio)]
        keys = qkv_ref[:, key_cols]
        values = qkv_ref[:, value_cols]
        key_acc[...] = jnp.zeros_like(key_acc)
        value_acc[...] = jnp.zeros_like(value_acc)
        for start in range(0, rows, tile):
            stop = start + tile
            query = jnp.concatenate([qkv_ref[start:stop, c] for c in cols], axis=0) * BF(HD**-0.5)
            out_grad = jnp.concatenate([head_grad_ref[start:stop, c] for c in cols], axis=0)
            near = dot_nt(keys[start:stop], query)
            key_pos = lax.broadcasted_iota(jnp.int32, near.shape, 0)
            row_pos = lax.broadcasted_iota(jnp.int32, near.shape, 1) & (tile - 1)
            scores = jnp.where(key_pos <= row_pos, near, -1e30)
            if start:
                scores = jnp.concatenate([dot_nt(keys[:start], query), scores], axis=0)
            probs = jnp.exp(scores - lse_ref[pl.ds(kv * (rows // tile) + start // tile, 1), :])
            prob_grad = dot_nt(values[:stop], out_grad)
            inner = jnp.sum(probs * prob_grad, axis=0, keepdims=True)
            score_grad = (probs * (prob_grad - inner)).astype(BF)
            value_acc[:stop] += dot_nn(probs.astype(BF), out_grad)
            key_acc[:stop] += dot_nn(score_grad, query)
            query_grad = (dot_tn(score_grad, keys[:stop]) * (HD**-0.5)).astype(BF)
            for r, c in enumerate(cols):
                proj_grad_ref[start:stop, c] = query_grad[r * tile : (r + 1) * tile]
        proj_grad_ref[:, key_cols] = key_acc[...].astype(BF)
        proj_grad_ref[:, value_cols] = value_acc[...].astype(BF)
    product_rows(spots_ref, proj_grad_ref, w_ref[:, :proj_width], kept_ref, sent_ref, x_scr, gain_ref)
    if first:
        return
    grads_ref[:, :proj_width] = earlier_ref[:, :proj_width] + dot_tn(x_scr[...], proj_grad_ref[...])
    grads_ref[:, proj_width:] = earlier_ref[:, proj_width:] + dot_tn(dy_scr[...], heads_ref[...])
    depth, blk, _ = grads_kept_ref.shape
    for r in range(depth):
        here = pl.ds(pl.multiple_of(block_spots_ref[r] * blk, blk), blk)
        grads_kept_ref[r] = grads_ref[here, :]
        here = pl.ds(pl.multiple_of(block_spots_ref[depth + r] * blk, blk), blk)
        grads_sent_ref[r] = grads_ref[here, :].astype(BF)


def attn_weights_kernel(proj_width, spots_ref, *rest):
    dy_pieces, x_pieces, rest = rest[:4], rest[4:8], rest[8:]
    heads_ref, proj_grad_ref, w_ref, grads_ref, gain_ref, dy_scr, x_scr = rest
    place_rows(spots_ref, dy_pieces, dy_scr)
    place_rows(spots_ref, x_pieces, x_scr)
    proj_part = dot_tn(x_scr[...], proj_grad_ref[...])
    grads_ref[:, :proj_width] = proj_part
    grads_ref[:, proj_width:] = dot_tn(dy_scr[...], heads_ref[...])
    products = proj_part * w_ref[:, :proj_width].astype(FP)
    gain_ref[...] = jnp.sum(products, axis=1, keepdims=True)


def attn_weights(spots, dy, x, heads, proj_grad, weights):
    rows, model_width = x[0].shape
    return pl.pallas_call(
        functools.partial(attn_weights_kernel, proj_grad.shape[1]),
        in_specs=[SMEM] + [VMEM] * 11,
        out_specs=[VMEM] * 2,
        out_shape=[
            jax.ShapeDtypeStruct((model_width, weights.shape[1]), FP),
            jax.ShapeDtypeStruct((model_width, 1), FP),
        ],
        scratch_shapes=[pltpu.VMEM((4 * rows, model_width), BF)] * 2,
        compiler_params=pltpu.CompilerParams(vmem_limit_bytes=56 << 20),
        cost_estimate=cost(4 << 30),
    )(spots, *dy, *x, heads, proj_grad, weights)


def attn_forward(spots, weight_spots, pieces, weights, widths):
    rows, model_width = pieces[0].shape
    width = weights[0].shape[1]
    whole = len(weights) == 1
    tile = min(512, 4 * rows)
    stats = (widths[1] // HD * (4 * rows // tile), widths[0] // widths[1] * tile)
    outs = [
        jax.ShapeDtypeStruct((4 * rows, widths[0] + 2 * widths[1]), BF),
        jax.ShapeDtypeStruct((4 * rows, widths[0]), BF),
        jax.ShapeDtypeStruct((2, rows, model_width), FP),
        jax.ShapeDtypeStruct((2, rows, model_width), BF),
        jax.ShapeDtypeStruct(stats, FP),
    ] + ([] if whole else [jax.ShapeDtypeStruct((model_width, width), BF)])
    results = pl.pallas_call(
        functools.partial(attn_forward_kernel, widths, len(weights)),
        in_specs=[SMEM] * 2 + [VMEM] * (4 + len(weights)),
        out_specs=[VMEM] * len(outs),
        out_shape=outs,
        scratch_shapes=[pltpu.VMEM((4 * rows, model_width), BF)],
        compiler_params=pltpu.CompilerParams(vmem_limit_bytes=56 << 20),
        cost_estimate=cost(14 << 30),
    )(spots, weight_spots, *pieces, *weights)
    return results if not whole else [*results, weights[0]]


def attn_backward(spots, block_spots, dy, x, qkv, heads, lse, weights, earlier, widths):
    rows, model_width = x[0].shape
    width = weights.shape[1]
    first = earlier is None
    operands = [*dy] + ([] if first else [*x]) + [qkv, heads, lse, weights]
    operands += [] if first else [earlier]
    depth = block_spots.shape[0] // 2
    whole = (model_width, width)
    blocks = (depth, model_width // depth // 2, width)
    placed = pltpu.VMEM((4 * rows, model_width), BF)
    proj_shape = (4 * rows, widths[0] + 2 * widths[1])
    sums = [pltpu.VMEM((4 * rows, HD), FP)] * 2
    outs = [jax.ShapeDtypeStruct((2, rows, model_width), t) for t in (FP, BF)]
    if first:
        outs = [jax.ShapeDtypeStruct(proj_shape, BF)] + outs
        scratch = [placed, pltpu.VMEM(heads.shape, BF), *sums]
    else:
        outs = [jax.ShapeDtypeStruct(blocks, FP), jax.ShapeDtypeStruct(blocks, BF)] + outs
        outs += [jax.ShapeDtypeStruct((1, model_width), FP)]
        scratch = [pltpu.VMEM(whole, FP), placed, placed, pltpu.VMEM(heads.shape, BF)]
        scratch += [pltpu.VMEM(proj_shape, BF), *sums]
    return pl.pallas_call(
        functools.partial(attn_backward_kernel, widths, first),
        in_specs=[SMEM] * 2 + [VMEM] * len(operands),
        out_specs=[VMEM] * len(outs),
        out_shape=outs,
        scratch_shapes=scratch,
        compiler_params=pltpu.CompilerParams(vmem_limit_bytes=58 << 20),
        cost_estimate=cost(1 << 24),
    )(spots, block_spots, *operands)


def on_device(
    block_input,
    cotangent,
    routes,
    gate_weights,
    w_query,
    w_key,
    w_value,
    w_out,
    w_gate_up,
    w_down,
    norm_attn,
    norm_moe,
):
    depth = lax.axis_size("z")
    micro_count, rows_local, model_width = block_input.shape
    q_width, kv_width = w_query.shape[1], w_key.shape[1]
    widths = (q_width, kv_width)
    proj_width = q_width + 2 * kv_width
    side, chip, core = lax.axis_index("y"), lax.axis_index("x"), lax.axis_index("c")
    side_at = side.astype(jnp.int32).reshape(1)
    spots = jnp.stack([2 * x + c for c in (core, 1 - core) for x in (chip, 1 - chip)])
    spots = spots.astype(jnp.int32)
    place = lax.axis_index("z")
    block_spots = jnp.stack(
        [2 * lax.rem(place + r, depth) + s for s in (side, 1 - side) for r in range(depth)]
    ).astype(jnp.int32)

    packed_attn = pack_attn(w_query, w_key, w_value, w_out)
    packed = pack_experts(after(side_at, packed_attn), w_gate_up, w_down)
    in_rows = after(block_input, packed[0][1]).astype(FP)
    normed_attn, scale_attn = row_norm(in_rows, norm_attn)
    normed = [normed_attn[m].astype(BF) for m in range(micro_count)]
    cots = [cotangent[m] for m in range(micro_count)]

    def shard_of(chunk, got):
        mine = packed[chunk][0]
        first = side == 0
        return jnp.stack([jnp.where(first, mine, got), jnp.where(first, got, mine)])

    def whole_of(shard):
        whole = lax.all_gather(shard, "z", axis=0)
        return whole.reshape(-1, *whole.shape[2:])

    column, places = along_z(packed_attn, depth)
    weight_spots = jnp.stack([2 * z + s for s in (side, 1 - side) for z in places])
    weight_spots = weight_spots.astype(jnp.int32)
    across = swap(normed[0], "x")
    got = swap(packed[0][1], "y")
    own_across = swap(packed_attn, "y")
    *column, across, got = together(*column, across, got)
    shards = [shard_of(0, got)]
    chunk_weights = [whole_of(shards[0])]
    *column, across, next_normed, cot, _ = together(
        *column, across, normed[1], cots[0], shards[0]
    )

    weights = column + [own_across] + [swap(piece, "y") for piece in column[1:]]
    near_rows, far_rows = swap(normed[0], "c"), swap(across, "c")
    next_across, cot_across = swap(next_normed, "x"), swap(cot, "x")
    *weights, near_rows, far_rows, cot, next_across = together(
        *weights, near_rows, far_rows, cots[0], next_across
    )
    attn_in = [[normed[0], across, near_rows, far_rows]]

    cot_diagonal = cross(cot)
    turn = after(spots, shards[0])
    qkv, heads, kept, sent, lse, whole = attn_forward(
        turn, weight_spots, attn_in[0], weights, widths
    )
    weights = [whole]
    saved = [(qkv, heads, lse)]
    sent, cot_diagonal, cot_across, across = together(
        sent, cot_diagonal, cot_across, next_across
    )

    got = swap(sent, "c")
    near_rows, far_rows = swap(normed[1], "c"), swap(across, "c")
    along = plus(kept[1], got[1]).astype(BF)
    own = plus(kept[0], got[0])
    along, near_rows, far_rows, cot, turn = together(along, near_rows, far_rows, cots[0], spots)
    attn_in.append([normed[1], across, near_rows, far_rows])

    expert_ids = jnp.arange(E, dtype=jnp.int32)[:, None, None, None]
    gates = jnp.sum(jnp.where(routes == expert_ids, gate_weights, 0.0), axis=3)
    gates = gates.reshape(2, E // 2, micro_count, 2, 2, rows_local)
    gates = jnp.where(chip == 0, gates, gates[:, :, :, ::-1])
    gates = jnp.where(core == 0, gates, gates[:, :, :, :, ::-1])
    mine = lax.dynamic_index_in_dim(gates, side, 0, False)
    other = lax.dynamic_index_in_dim(gates, 1 - side, 0, False)
    other = after(other.reshape(E // 2, -1), along)
    came, cot_near, gates_got = swap(along, "x"), swap(cot, "y"), swap(other, "y")
    qkv, heads, kept, sent, lse, _ = attn_forward(
        turn, weight_spots, attn_in[1], weights, widths
    )
    saved.append((qkv, heads, lse))
    sent, came, cot_near, gates_got = together(sent, came, cot_near, gates_got)

    def moe_rows(middle):
        normed, scale = row_norm(middle, norm_moe)
        return normed.astype(BF), scale

    got = swap(sent, "c")
    middle = [in_rows[0] + plus(own, came)]
    low, scale = moe_rows(middle[0])
    normed, scale_moe = [low], [scale]
    along = plus(kept[1], got[1]).astype(BF)
    own = plus(kept[0], got[0])
    along, low = together(along, low)

    near, across, diagonal = to_neighbours([low] * 3)
    gates = jnp.stack([mine, gates_got.reshape(mine.shape)])
    gates = gates.transpose(2, 3, 0, 4, 5, 1).reshape(micro_count, 4, 2, rows_local, E // 2)
    near, across, diagonal, gates, along, theirs = together(
        near, across, diagonal, gates, along, packed[1][1]
    )

    came, theirs = swap(along, "x"), swap(theirs, "y")
    blocks = stacked(
        [normed[0], cots[0], near, cot_near, across, cot_across, diagonal, cot_diagonal]
    )
    experts_in = [(blocks, swap(blocks, "c"))]
    came, theirs, blocks = together(came, theirs, blocks)
    middle.append(in_rows[1] + plus(own, came))
    low, scale = moe_rows(middle[1])
    normed.append(low)
    scale_moe.append(scale)
    pair = stacked([low, cots[1]])
    shards.append(shard_of(1, theirs))
    chunk_weights.append(whole_of(shards[1]))
    neighbours = to_neighbours([pair] * 3)

    sums = [None] * micro_count
    turn = after(side_at, shards[1], pair)
    all_grads = []
    first_expert = 0
    for chunk, count in enumerate(CHUNKS):
        last = chunk == len(CHUNKS) - 1
        grads = None
        for m in range(micro_count):
            sums[m], grads = moe_chunk(
                turn,
                experts_in[m],
                gates,
                chunk_weights[chunk],
                sums[m],
                grads,
                m,
                first_expert,
                last,
            )
            waited = [grads]
            if m == 0 and chunk == 0:
                *neighbours, _ = together(*neighbours, grads)
                blocks = stacked([pair, *neighbours])
                blocks = blocks.reshape(-1, *blocks.shape[2:])
                experts_in.append((blocks, swap(blocks, "c")))
            if m == 0 and last:
                mixed_own, mixed_along = half_sums(*sums[0][:2])
                own, along = half_sums(*sums[0][2:])
                along = [jnp.stack(both) for both in zip(along, mixed_along)]
                *along, turn, _ = together(*along, side_at, *waited)
                came = to_neighbours(along)
            else:
                turn = after(side_at, *waited)
        first_expert += count
        all_grads.append(grads.reshape(depth, 2, *grads.shape[1:]))

    def reduce_grads(grads):
        return lax.psum_scatter(grads, "z", scatter_dimension=0, tiled=False)

    grad_shards = [reduce_grads(all_grads[0])]

    def middle_back(m, own, came):
        moe_in_grad = sum_of(own, came)
        back = norm_back(middle[m], scale_moe[m], norm_moe, moe_in_grad)
        gain = jnp.sum(moe_in_grad * middle[m] * scale_moe[m], axis=0)
        grad = cots[m].astype(FP) + back
        return grad, grad.astype(BF), gain

    def input_back(m, middle_grad, own, came):
        return middle_grad + norm_back(in_rows[m], scale_attn[m], norm_attn, plus(own, came))

    def backward(m, turn, rows, earlier):
        return attn_backward(
            turn, block_spots, rows, attn_in[m], *saved[m], weights[0], earlier, widths
        )

    *came, grads, kept, sent, last_mixed_kept, last_mixed_sent, first_shard = together(
        *came, all_grads[1], sums[1][2], sums[1][3], *sums[1][:2], grad_shards[0]
    )
    grad_shards = [first_shard, reduce_grads(grads)]
    first_came, first_mixed_own = came, mixed_own
    middle_grad, low, gain_moe = middle_back(0, own, [c[0] for c in came])
    across, near_rows = swap(low, "x"), swap(low, "c")
    last_mixed_sent, sent, _ = together(last_mixed_sent, sent, low)
    own, along = half_sums(kept, sent)
    mixed_own, mixed_along = half_sums(last_mixed_kept, last_mixed_sent)
    came = to_neighbours(along)
    across, near_rows, came[:2], mixed_along = together(across, near_rows, came[:2], mixed_along)
    far_rows = swap(across, "c")
    rows = [low, across, near_rows, far_rows]
    results = backward(0, spots, rows, None)
    *came, proj_grad, kept, sent, first_shard = together(*came, *results, first_shard)
    earlier, gain_attn = attn_weights(
        spots, rows, attn_in[0], saved[0][1], proj_grad, weights[0]
    )

    middle_grads = [middle_grad]
    middle_grad, low, gain = middle_back(1, own, came)
    middle_grads.append(middle_grad)
    gain_moe = gain_moe + gain
    across, near_rows = swap(low, "x"), swap(low, "c")
    input_own, input_along = half_sums(kept, sent)
    shard_got = [swap(first_shard[1], "y")]
    across, near_rows, shard_got[0], input_along, earlier, *mixed_along = together(
        across, near_rows, shard_got[0], *input_along, earlier, *mixed_along
    )
    far_rows = swap(across, "c")
    input_came = swap(input_along, "x")
    mixed_came = [swap(mixed_along[0], "y"), cross(mixed_along[2])]
    results = backward(1, spots, [low, across, near_rows, far_rows], earlier)
    input_came, gain_attn, (mixed_came, results, first_came) = together(
        input_came, gain_attn, (mixed_came, results, first_came)
    )
    grads_kept, grads_sent, kept, sent, gain = results

    gains = jnp.concatenate([(gain_attn[:, 0] + gain[0]) / norm_attn, gain_moe]).reshape(16, -1)
    grads_got = swap(grads_sent, "y")
    own, along = half_sums(kept, sent)
    first_input = input_back(0, middle_grads[0], input_own, input_came)
    outputs = [(middle[0] + sum_of(first_mixed_own, [c[1] for c in first_came])).astype(BF)]
    mixed_came.append(swap(mixed_along[1], "x"))
    gains = sum_over_z(gains + swap(gains, "c"), depth)
    gains, mixed_came[2] = together(gains, mixed_came[2])
    gains = gains + swap(gains, "x")
    column = grads_kept + grads_got.astype(FP)
    along, gains, first_input, outputs[0], column, last_shard, mixed_own = together(
        along[0], gains, first_input, outputs[0], column, grad_shards[1], mixed_own
    )
    input_came = swap(along, "x")
    last_sent, column = together(last_shard[1], column)
    shard_got.append(swap(last_sent, "y"))
    pieces = along_z_sent(column, depth)
    last_input = input_back(1, middle_grads[1], own, input_came)
    outputs.append((middle[1] + sum_of(mixed_own, mixed_came)).astype(BF))
    last_input, outputs[1], shard_got[1], gains, *pieces = together(
        last_input, outputs[1], shard_got[1], gains, *pieces
    )
    gains = (gains + swap(gains, "y")).reshape(2, model_width)
    shard_pair, shard_down = unpack_experts(
        side_at, w_down.shape[1], list(zip([grad_shards[0], last_shard], shard_got))
    )
    attn_shard = sum_of(column[0], pieces)
    input_grads = [first_input, last_input]
    return (
        jnp.stack(outputs),
        jnp.stack(input_grads),
        attn_shard[:, :q_width],
        attn_shard[:, q_width : q_width + kv_width],
        attn_shard[:, q_width + kv_width : proj_width],
        attn_shard[:, proj_width:].T,
        shard_pair,
        shard_down,
        gains[0],
        gains[1],
    )


def solution(mesh):
    dp, tensor = mesh.shape["dp"], mesh.shape["tensor"]
    fine = Mesh(mesh.devices.reshape(dp // 2, 2, tensor // 2, 2), ("z", "y", "x", "c"))
    dp_axes, tensor_axes = ("z", "y"), ("x", "c")
    rows = P(None, dp_axes + tensor_axes, None)
    return jax.shard_map(
        on_device,
        mesh=fine,
        in_specs=(
            rows,
            rows,
            P(None, dp_axes, None),
            P(None, dp_axes, None),
            P(dp_axes, tensor_axes),
            P(dp_axes, tensor_axes),
            P(dp_axes, tensor_axes),
            P(tensor_axes, dp_axes),
            P(None, dp_axes, None, tensor_axes),
            P(None, tensor_axes, dp_axes),
            P(),
            P(),
        ),
        out_specs=(
            rows,
            rows,
            P(dp_axes, tensor_axes),
            P(dp_axes, tensor_axes),
            P(dp_axes, tensor_axes),
            P(tensor_axes, dp_axes),
            P(None, dp_axes, None, tensor_axes),
            P(None, tensor_axes, dp_axes),
            P(),
            P(),
        ),
        check_vma=False,
    )
```
